32 devices in a mesh: wide: 8 (over y, x, core), narrow: 4 (over z).
Axes of the slice: x: 2, y: 2, z: 4, core: 2. Of those that a mesh axis runs over, the one named last changes fastest.
Arguments:
- tokens: bfloat16 [8192, 768], P('wide'), may hold values from -6 to 6
- segments: int32 [8, 1024], P('wide'), may hold values from 0 to 21, never falling along the last dimension, each value on 1 to 256 neighbouring positions
- first_gain: float32 [768], replicated, may hold values from 0.1 to 1.9
- qkv_weight: bfloat16 [3, 768, 768], P(None, None, 'narrow'), may hold values from -0.21875 to 0.21875
- output_weight: bfloat16 [768, 768], P('narrow'), may hold values from -0.875 to 0.875
- second_gain: float32 [768], replicated, may hold values from 0.1 to 1.9
- geglu_weight: bfloat16 [2, 768, 1152], P(None, None, 'narrow'), may hold values from -0.21875 to 0.21875
- down_weight: bfloat16 [1152, 768], P('narrow'), may hold values from -0.25 to 0.25
- cotangent: bfloat16 [8192, 768], P('wide'), may hold values from -6 to 6
Outputs:
- layer_out: bfloat16 [8192, 768], P(('wide', 'narrow'))
- tokens_grad: float32 [8192, 768], P(('wide', 'narrow'))
- first_gain_grad: float32 [768], replicated
- qkv_grad: float32 [3, 768, 768], P(None, 'wide', 'narrow')
- output_grad: float32 [768, 768], P('narrow', 'wide')
- second_gain_grad: float32 [768], replicated
- geglu_grad: float32 [2, 768, 1152], P(None, 'wide', 'narrow')
- down_grad: float32 [1152, 768], P('narrow', 'wide')
The draws below stay inside these ranges and needn't reach their ends.
Inputs may be any that keep to these rules, and one draw needn't show every extreme that they name: `segments`: segment numbers never fall along a row; each number names one document of 1 to 256 consecutive tokens, and every number from 0 up to the largest is used in each row.
All inputs are finite; a program needn't handle non-finite values.
Results may differ from the reference program's by a relative error of at most 0.014.
The reference program's roundings to bfloat16 on the way count: a program that leaves them out, or rounds other values in their place, can miss the bound.
Values may be sent and summed in bfloat16 or wider, within the bound.
No kernel may reach another device: no remote copies, remote signals or barrier semaphores. Data moves between devices by JAX's collectives and lax.ppermute only.
A program may use at most 128 MiB of HBM per device.

```python
import math
import jax
import jax.numpy as jnp
import numpy as np
from jax import lax

D = 768
HEADS = 12
HEAD = 64
FF = 1152
LEN = 1024
ROWS = 8
TOKENS = 8192


def raised(result, own_key, source, target, blocks, factor):
    owner, partner = [(jnp.arange(result.shape[axis_at]) // (result.shape[axis_at] // blocks)).reshape([-1 if axis == axis_at else 1 for axis in range(result.ndim)]) for axis_at in (source, target)]
    chosen = jax.random.permutation(own_key, blocks)[partner]
    strong = (owner == chosen) | (owner == (partner + blocks // 2) % blocks)
    return jnp.where(strong, factor * result, result)


def levels(own_key, dims, cuts, least, high):
    def one(dim, blocks):
        draws = jax.random.uniform(jax.random.fold_in(jax.random.fold_in(own_key, 6), dim), (blocks,), jnp.float32, least / len(cuts), high / len(cuts))
        return jnp.repeat(jnp.exp(draws), dims[dim] // blocks).reshape((-1,) + (1,) * (len(dims) - dim - 1))

    level = one(*cuts[0])
    for cut in cuts[1:]:
        level = level * one(*cut)
    return level


def profile(amount, total, limit, skew):
    portions = [(1 << 20) // math.isqrt(standing ** skew) + 1 for standing in range(2, amount + 1)]
    spare, given = total - limit - (amount - 1), [1] * (amount - 1)
    while spare > 0:
        candidates = [i for i in range(amount - 1) if given[i] < limit]
        whole, remaining = sum([portions[i] for i in candidates]), spare
        for i in candidates:
            addition = min(limit - given[i], max(1, remaining * portions[i] // whole), spare)
            given[i] = given[i] + addition
            spare = spare - addition
    return np.array([limit] + given)


def ragged(rng, number_of, total, bound, skew):
    if number_of == 2:
        one = jax.random.randint(rng, (), max(1, total - bound), min(bound, total - 1) + 1)
        return jnp.stack([one, total - one])
    tallies = jnp.asarray(profile(number_of, total, bound, skew), jnp.int32)
    couples = (number_of - 1) // 2
    giver, sink = tallies[1:1 + 2 * couples:2], tallies[2:2 + 2 * couples:2]
    margin = jnp.minimum(giver - 1, bound - sink)
    passed = jax.random.randint(jax.random.fold_in(rng, 1), (couples,), 0, 1 << 20) % (margin + 1)
    tallies = tallies.at[1:1 + 2 * couples:2].set(giver - passed).at[2:2 + 2 * couples:2].set(sink + passed)
    return tallies[jax.random.permutation(jax.random.fold_in(rng, 2), number_of)]


def noise(key, shape, width, most, cuts=(), kind=jnp.bfloat16):
    values = width * jax.random.normal(key, shape, jnp.float32)
    if cuts:
        values = values * levels(key, shape, cuts, -0.22, 0.18)
    return jnp.clip(values, -most, most).astype(kind)


def heavy_noise(rng, extent, width, bound, split, heavy, kind=jnp.bfloat16):
    drawn = width * jax.random.normal(rng, extent, jnp.float32)
    if split:
        drawn = drawn * levels(rng, extent, split, -0.22, 0.18)
    return jnp.clip(raised(drawn, jax.random.fold_in(rng, 3), *heavy), -bound, bound).astype(kind)


def setup_inputs(seed: int = 0) -> dict:
    key_list = jax.random.split(jax.random.key(seed), 10)
    return {
        "tokens": noise(key_list[0], (TOKENS, D), 1.0, 6.0, ((0, 8),)),
        "segments": jax.vmap(lambda own: jnp.searchsorted(jnp.cumsum(ragged(own, LEN // 64 + 6, LEN, LEN // 4, 1)), jnp.arange(LEN), side="right"))(jax.random.split(key_list[1], ROWS)).reshape((ROWS, LEN)).astype(jnp.int32),
        "first_gain": jnp.clip(1.0 + 0.18 * jax.random.normal(key_list[2], (D,), jnp.float32), 0.1, 1.9),
        "qkv_weight": noise(key_list[3], (3, D, D), D ** -0.5, 0.21875, ((2, 4),)),
        "output_weight": noise(key_list[4], (D, D), (D // 16) ** -0.5, 0.875, ((0, 4),)),
        "second_gain": jnp.clip(1.0 + 0.18 * jax.random.normal(key_list[5], (D,), jnp.float32), 0.1, 1.9),
        "geglu_weight": noise(key_list[6], (2, D, FF), D ** -0.5, 0.21875, ((2, 4),)),
        "down_weight": noise(key_list[7], (FF, D), (FF // 2) ** -0.5, 0.25, ((0, 4),)),
        "cotangent": heavy_noise(key_list[8], (TOKENS, D), 1.0, 6.0, ((0, 8),), (0, 1, 8, 2.0)),
    }


EPSILON = 1e-05
ROPE_BASE = 160000.0
HIGHEST = lax.Precision.HIGHEST

@jax.custom_vjp
def low(v):
    return lax.optimization_barrier(v.astype(jnp.bfloat16)).astype(jnp.float32)

@jax.custom_vjp
def low_back(v):
    return v

def low_keep(v):
    return (low(v), None)

def low_pass(kept, grad):
    return (grad,)

def back_keep(v):
    return (v, None)

def back_low(kept, grad):
    return (low(grad),)
low.defvjp(low_keep, low_pass)
low_back.defvjp(back_keep, back_low)

def normalize(values):
    centre = values - lax.optimization_barrier(jnp.mean(values, axis=-1, keepdims=True))
    spread = lax.optimization_barrier(jnp.mean(centre * centre, axis=-1, keepdims=True))
    return centre * lax.rsqrt(spread + EPSILON)

def rotary_tables(segments):
    earlier = lax.optimization_barrier(jnp.sum((segments[:, None, :] < segments[:, :, None]).astype(jnp.int32), axis=2))
    places = (jnp.arange(segments.shape[1], dtype=jnp.int32)[None, :] - earlier).reshape(-1).astype(jnp.float32)
    frequency = jnp.power(ROPE_BASE, -2.0 * jnp.arange(HEAD // 2, dtype=jnp.float32) / HEAD)
    angles = places[:, None] * frequency[None, :]
    return (jnp.cos(angles)[:, None, :], jnp.sin(angles)[:, None, :])

def rotate(values, cosine, sine_table):
    half_size = values.shape[-1] // 2
    first_half = values[..., :half_size]
    second = values[..., half_size:]
    return jnp.concatenate([first_half * cosine - second * sine_table, second * cosine + first_half * sine_table], axis=-1)

def attend_row(pieces):
    queries, key_rows, values, segment_row = pieces
    scores = low_back(jnp.einsum('qhd,khd->hqk', queries, key_rows, precision=HIGHEST) / math.sqrt(HEAD))
    same_doc = segment_row[:, None] == segment_row[None, :]
    scores = jnp.where(same_doc[None], scores, -1e+30)
    probability = jax.nn.softmax(scores, axis=-1)
    return jnp.einsum('hqk,khd->qhd', low(probability), values, precision=HIGHEST)

def reference(tokens, segments, first_gain, qkv_weight, output_weight, second_gain, geglu_weight, down_weight, cotangent):
    cosine, sine_table = rotary_tables(segments)
    rows_count = segments.shape[0]

    def forward(inputs, gain_one, weight_qkv, weight_out, gain_two, weight_geglu, weight_down):
        tokens_count = inputs.shape[0]
        normed_one = low(normalize(inputs) * gain_one)
        projected = low_back(jnp.einsum('td,sde->ste', normed_one, weight_qkv, precision=HIGHEST))

        def heads_of(block_in):
            return block_in.reshape(tokens_count, HEADS, HEAD)

        def by_rows(block_in):
            return block_in.reshape(rows_count, LEN, HEADS, HEAD)
        queries = low(rotate(heads_of(projected[0]), cosine, sine_table))
        key_rows = low(rotate(heads_of(projected[1]), cosine, sine_table))
        values = low(heads_of(projected[2]))
        context = lax.map(jax.checkpoint(attend_row), (by_rows(queries), by_rows(key_rows), by_rows(values), segments))
        context = low(low_back(context.reshape(tokens_count, D)))
        residual = inputs + low_back(jnp.dot(context, weight_out, precision=HIGHEST))
        normed_two = low(normalize(residual) * gain_two)
        geglu_out = low_back(jnp.einsum('td,sdf->stf', normed_two, weight_geglu, precision=HIGHEST))
        activated = low(jax.nn.gelu(geglu_out[0], approximate=False) * geglu_out[1])
        return residual + low_back(jnp.dot(activated, weight_down, precision=HIGHEST))
    primals = (tokens.astype(jnp.float32), first_gain, qkv_weight.astype(jnp.float32), output_weight.astype(jnp.float32), second_gain, geglu_weight.astype(jnp.float32), down_weight.astype(jnp.float32))
    layer_out, pullback = jax.vjp(forward, *primals)
    gradients = pullback(cotangent.astype(jnp.float32))
    return (layer_out.astype(jnp.bfloat16), gradients[0], gradients[1], gradients[2], gradients[3], gradients[4], gradients[5], gradients[6])
```

```python
import functools
import math

import jax
import jax.numpy as jnp
import numpy as np
from jax import lax
from jax.experimental import pallas as pl
from jax.experimental.pallas import tpu as pltpu
from jax.sharding import PartitionSpec as P

HEAD = 64
LEN = 1024
D = 768
HEADS_HERE = 3
COLS = HEADS_HERE * HEAD
LANES = 256
DOC = 256
QB = 128
EPSILON = 1e-05
ROPE_BASE = 160000.0
NARROW = 4
BLOCK = LEN // NARROW
F32 = jnp.float32
BF16 = jnp.bfloat16
NEGATIVE = -1e30
VMEM_LIMIT = 48 * 1024 * 1024

NN = (((1,), (0,)), ((), ()))
NT = (((1,), (1,)), ((), ()))
TN = (((0,), (0,)), ((), ()))


def dot(a, b, dims=NN):
    return lax.dot_general(a, b, dims, preferred_element_type=F32)


def call(body, ins, outs, scratch=(), flops=0, scalars=1):
    specs = [pl.BlockSpec(memory_space=pltpu.SMEM)] * scalars
    specs += [pl.BlockSpec(memory_space=pltpu.VMEM)] * (len(ins) - scalars)
    size = sum(math.prod(x.shape) * x.dtype.itemsize for x in (*ins, *outs))
    return pl.pallas_call(
        body,
        out_shape=tuple(jax.ShapeDtypeStruct(o.shape, o.dtype) for o in outs),
        in_specs=specs,
        out_specs=tuple(pl.BlockSpec(memory_space=pltpu.VMEM) for _ in outs),
        scratch_shapes=list(scratch),
        compiler_params=pltpu.CompilerParams(vmem_limit_bytes=VMEM_LIMIT),
        cost_estimate=pl.CostEstimate(flops=flops, bytes_accessed=size, transcendentals=0),
    )(*ins)


def sds(shape, dtype):
    return jax.ShapeDtypeStruct(shape, dtype)


def rotary_table():
    position = np.arange(DOC, dtype=np.float64)
    frequency = ROPE_BASE ** (-2.0 * np.arange(HEAD // 2, dtype=np.float64) / HEAD)
    angle = position[:, None] * frequency[None, :]
    cosine, sine = np.cos(angle), np.sin(angle)
    table = np.zeros((DOC, 2 * LANES), np.float32)
    for h in range(HEADS_HERE):
        base = h * HEAD
        table[:, base : base + 32] = cosine
        table[:, base + 32 : base + 64] = cosine
        table[:, LANES + base : LANES + base + 32] = -sine
        table[:, LANES + base + 32 : LANES + base + 64] = sine
    high = table.astype(jnp.bfloat16)
    low = (table - high.astype(np.float32)).astype(jnp.bfloat16)
    return np.stack([high, low])


def normalize(values):
    centre = values - jnp.mean(values, axis=-1, keepdims=True)
    spread = jnp.mean(centre * centre, axis=-1, keepdims=True)
    inverse = lax.rsqrt(spread + EPSILON)
    return centre * inverse, inverse


def norm_back(upstream, unit_rows, inverse, gain):
    scaled = upstream * gain
    first_mean = jnp.mean(scaled, axis=-1, keepdims=True)
    second_mean = jnp.mean(scaled * unit_rows, axis=-1, keepdims=True)
    return inverse * (scaled - first_mean - unit_rows * second_mean)


def lane_head(rows):
    return lax.broadcasted_iota(jnp.int32, (rows, LANES), 1) // HEAD


def swap_halves(x):
    lane = lax.broadcasted_iota(jnp.int32, x.shape, 1)
    return jnp.where(
        lane % HEAD < HEAD // 2,
        pltpu.roll(x, LANES - HEAD // 2, 1),
        pltpu.roll(x, HEAD // 2, 1),
    )


def by_head(block, head):
    return jnp.concatenate(
        [jnp.where(head == h, block, jnp.zeros_like(block)) for h in range(HEADS_HERE)], axis=0
    )


def merge_heads(stacked, head):
    parts = jnp.split(stacked, HEADS_HERE, axis=0)
    return jnp.where(head == 0, parts[0], jnp.where(head == 1, parts[1], parts[2]))


def window(i):
    reach = DOC // QB
    return max(0, i - reach) * QB, min(LEN // QB, i + reach + 1) * QB


def forward_kernel(
    z_ref, tok_ref, seg_ref, gain_ref, w_ref, table_ref,
    c0_ref, c1_ref, c2_ref, c3_ref, q_ref, k_ref, v_ref, normed_ref, lse_ref, trig_ref, segc_ref,
    proj_ref, ctx_ref,
):
    z = z_ref[0]
    seg = jnp.broadcast_to(seg_ref[...].astype(F32), (8, LEN))
    index = lax.broadcasted_iota(jnp.int32, (8, LEN), 1)
    first = jnp.where(seg != pltpu.roll(seg, 1, 1), index, 0)
    first = jnp.where(index == 0, 0, first).astype(F32)
    shift = 1
    while shift < DOC:
        first = jnp.maximum(first, jnp.where(index >= shift, pltpu.roll(first, shift, 1), 0.0))
        shift *= 2
    place = index.astype(F32) - first
    segc_ref[...] = jnp.transpose(jnp.broadcast_to(seg[:1], (128, LEN)))
    placec = jnp.transpose(jnp.broadcast_to(place[:1], (128, LEN)))
    lane = lax.broadcasted_iota(jnp.int32, (LEN, 128), 1).astype(F32)
    hot = jnp.concatenate(
        [jnp.where(placec == lane + 128.0 * j, 1.0, 0.0) for j in range(DOC // 128)], axis=1
    ).astype(BF16)
    trig_ref[...] = dot(hot, table_ref[0]) + dot(hot, table_ref[1])

    def norm_rows(i, carry):
        rows = pl.ds(pl.multiple_of(i * 128, 128), 128)
        unit, _ = normalize(tok_ref[rows, :].astype(F32))
        normed_ref[rows, :] = (unit * gain_ref[...]).astype(BF16)
        return carry

    lax.fori_loop(0, LEN // 128, norm_rows, 0)
    proj_ref[:, COLS:] = jnp.zeros((LEN, LANES - COLS), F32)
    for s, out in enumerate((q_ref, k_ref)):
        proj_ref[:, :COLS] = dot(normed_ref[...], w_ref[s])
        x = proj_ref[...]
        out[...] = (x * trig_ref[:, :LANES] + swap_halves(x) * trig_ref[:, LANES:]).astype(BF16)
    proj_ref[:, :COLS] = dot(normed_ref[...], w_ref[2])
    v_ref[...] = proj_ref[...].astype(BF16)

    head = lane_head(QB)
    column = lax.broadcasted_iota(jnp.int32, (QB, 128), 1)
    for i in range(LEN // QB):
        low, high = window(i)
        rows = slice(i * QB, (i + 1) * QB)
        stacked = by_head(q_ref[rows, :] * jnp.asarray(1.0 / math.sqrt(HEAD), BF16), head)
        scores = dot(stacked, k_ref[low:high, :], NT)
        same = segc_ref[rows, 0:1] == seg_ref[0:1, low:high].astype(F32)
        parts, logs = [], []
        for h in range(HEADS_HERE):
            mine = jnp.where(same, scores[h * QB : (h + 1) * QB], NEGATIVE)
            top = jnp.max(mine, axis=-1, keepdims=True)
            weights = jnp.exp(mine - top)
            total = jnp.sum(weights, axis=-1, keepdims=True)
            parts.append((weights * (1.0 / total)).astype(BF16))
            logs.append(top + jnp.log(total))
        lse_ref[rows, :] = jnp.where(column == 0, logs[0], jnp.where(column == 1, logs[1], logs[2]))
        mixed = dot(jnp.concatenate(parts, axis=0), v_ref[low:high, :])
        context = merge_heads(mixed, head)[:, :COLS].astype(BF16)
        block, r = i * QB // BLOCK, i * QB % BLOCK
        ctx_ref[block, r : r + QB, :COLS] = context
        ctx_ref[block ^ 1, r : r + QB, COLS:] = context
    for k, out in enumerate((c0_ref, c1_ref, c2_ref, c3_ref)):
        out[...] = ctx_ref[z ^ k]


def middle_kernel(
    tok_own, tok_par, cot_own, cot_par, c0, c1, c2, c3, wo_ref, gain_ref, gw_ref, dw_ref, other_ref,
    res_ref, normed_ref, act_ref, gb_ref, keep_ref, send_ref, out_keep_ref, out_send_ref,
    cot_ref,
):
    for half, tok in enumerate((tok_own, tok_par)):
        rows = slice(half * BLOCK, (half + 1) * BLOCK)
        attended = jnp.zeros((BLOCK, D), F32)
        for k, c in enumerate((c0, c1, c2, c3)):
            attended += dot(c[:, half * COLS : (half + 1) * COLS], wo_ref[k])
        residual = tok[...].astype(F32) + attended
        res_ref[rows, :] = residual
        unit, _ = normalize(residual)
        normed_ref[rows, :] = (unit * gain_ref[...]).astype(BF16)
    cot_ref[:BLOCK, :] = cot_own[...]
    cot_ref[BLOCK:, :] = cot_par[...]
    branch, back = None, None
    for j in range(2):
        w0 = gw_ref[0] if j == 0 else other_ref[0]
        w1 = gw_ref[1] if j == 0 else other_ref[1]
        gate = dot(normed_ref[...], w0)
        linear = dot(normed_ref[...], w1)
        act_back = dot(cot_ref[...], dw_ref[...], NT) if j == 0 else dot(cot_ref[...], other_ref[2])
        cdf = 0.5 * (1.0 + lax.erf(gate * math.sqrt(0.5)))
        slope = cdf + gate * (jnp.exp(-0.5 * gate * gate) * (1.0 / math.sqrt(2.0 * math.pi)))
        gelu = gate * cdf
        act = (gelu * linear).astype(BF16)
        gb0 = (act_back * linear * slope).astype(BF16)
        gb1 = (act_back * gelu).astype(BF16)
        act_ref[j] = act
        gb_ref[j, 0] = gb0
        gb_ref[j, 1] = gb1
        branch_part = dot(act, dw_ref[...]) if j == 0 else dot(act, other_ref[2], NT)
        back_part = dot(gb0, w0, NT) + dot(gb1, w1, NT)
        branch = branch_part if branch is None else branch + branch_part
        back = back_part if back is None else back + back_part
    keep_ref[...] = back[:BLOCK]
    send_ref[...] = back[BLOCK:].astype(BF16)
    out_keep_ref[...] = branch[:BLOCK] + res_ref[:BLOCK, :]
    out_send_ref[...] = branch[BLOCK:].astype(BF16)


def ff_grad_kernel(normed_ref, act_ref, gb_ref, cot_own, cot_par, out_ref):
    width = act_ref.shape[2]
    for j in range(2):
        base = j * 3 * width
        for s in range(2):
            at = base + s * width
            out_ref[:, at : at + width] = dot(normed_ref[...], gb_ref[j, s], TN).astype(BF16)
        at = base + 2 * width
        part = dot(cot_own[...], act_ref[j, :BLOCK], TN) + dot(cot_par[...], act_ref[j, BLOCK:], TN)
        out_ref[:, at : at + width] = part.astype(BF16)


def residual_kernel(
    keep_ref, recv_ref, res_ref, gain_ref, cot_ref, wo_ref,
    back_ref, low_ref, gain_out, b0, b1, b2, b3,
):
    unit, inverse = normalize(res_ref[:BLOCK, :])
    upstream = keep_ref[...] + recv_ref[...].astype(F32)
    back = cot_ref[...].astype(F32) + norm_back(upstream, unit, inverse, gain_ref[...])
    back_ref[...] = back
    gain_out[...] = jnp.sum(upstream * unit, axis=0, keepdims=True)
    low = back.astype(BF16)
    low_ref[...] = low
    for k, out in enumerate((b0, b1, b2, b3)):
        part = dot(low, wo_ref[k], NT).astype(BF16)
        out[:, :COLS] = part[: BLOCK // 2]
        out[:, COLS:] = part[BLOCK // 2 :]


def output_grad_kernel(low_ref, c0, c1, c2, c3, out_ref):
    for k, c in enumerate((c0, c1, c2, c3)):
        out_ref[:, k * COLS : (k + 1) * COLS] = dot(low_ref[...], c[:, :COLS], TN).astype(BF16)


def backward_kernel(
    z_ref, seg_ref, segc_ref, q_ref, k_ref, v_ref, lse_ref, trig_ref, b0, b1, b2, b3, w_ref,
    qkv_ref, n0, n1, n2, n3,
    back_ref, dq_ref, dk_ref, dv_ref,
):
    z = z_ref[0]
    half = BLOCK // 2
    back_ref[:, COLS:] = jnp.zeros((LEN, LANES - COLS), BF16)
    for k, b in enumerate((b0, b1, b2, b3)):
        base = pl.multiple_of((z ^ k) * BLOCK, BLOCK)
        back_ref[pl.ds(base, half), :COLS] = b[:, :COLS]
        back_ref[pl.ds(pl.multiple_of(base + half, half), half), :COLS] = b[:, COLS:]
    dk_ref[...] = jnp.zeros_like(dk_ref)
    dv_ref[...] = jnp.zeros_like(dv_ref)
    head = lane_head(QB)
    scale = jnp.asarray(1.0 / math.sqrt(HEAD), BF16)
    for i in range(LEN // QB):
        low, high = window(i)
        rows = slice(i * QB, (i + 1) * QB)
        stacked = by_head(q_ref[rows, :] * scale, head)
        upstream = by_head(back_ref[rows, :], head)
        scores = dot(stacked, k_ref[low:high, :], NT)
        prob_back = dot(upstream, v_ref[low:high, :], NT)
        same = segc_ref[rows, 0:1] == seg_ref[0:1, low:high].astype(F32)
        probs, grads = [], []
        for h in range(HEADS_HERE):
            at = slice(h * QB, (h + 1) * QB)
            prob = jnp.exp(jnp.where(same, scores[at], NEGATIVE) - lse_ref[rows, h : h + 1])
            inner = jnp.sum(prob * prob_back[at], axis=-1, keepdims=True)
            probs.append(prob.astype(BF16))
            grads.append((prob * (prob_back[at] - inner)).astype(BF16))
        prob = jnp.concatenate(probs, axis=0)
        grad = jnp.concatenate(grads, axis=0)
        dv_ref[low:high, :] += dot(prob, upstream, TN)
        dk_ref[low:high, :] += dot(grad, stacked, TN)
        dq_ref[rows, :] = merge_heads(dot(grad, k_ref[low:high, :]), head) * (1.0 / math.sqrt(HEAD))
    cosine, signed = trig_ref[:, :LANES], trig_ref[:, LANES:]
    for s, grad_ref in enumerate((dq_ref, dk_ref)):
        g = grad_ref[...]
        turned = g * cosine - swap_halves(g) * signed
        qkv_ref[:, s * COLS : (s + 1) * COLS] = turned[:, :COLS].astype(BF16)
    qkv_ref[:, 2 * COLS :] = dv_ref[:, :COLS].astype(BF16)
    for k, out in enumerate((n0, n1, n2, n3)):
        base = pl.multiple_of((z ^ k) * BLOCK, BLOCK)
        part = None
        for s in range(3):
            piece = dot(qkv_ref[pl.ds(base, BLOCK), s * COLS : (s + 1) * COLS], w_ref[s], NT)
            part = piece if part is None else part + piece
        out[...] = part.astype(out.dtype)


def qkv_grad_kernel(normed_ref, qkv_ref, w_ref, out_ref, gain_out):
    total = None
    for s in range(3):
        part = dot(normed_ref[...], qkv_ref[:, s * COLS : (s + 1) * COLS], TN)
        out_ref[:, s * COLS : (s + 1) * COLS] = part.astype(BF16)
        weighted = jnp.sum(part * w_ref[s].astype(F32), axis=1, keepdims=True)
        total = weighted if total is None else total + weighted
    gain_out[...] = jnp.broadcast_to(total, gain_out.shape)


def final_kernel(tok_ref, gain_ref, back_ref, n0, n1, n2, n3, out_ref):
    upstream = n0[...] + n1[...].astype(F32) + n2[...].astype(F32) + n3[...].astype(F32)
    unit, inverse = normalize(tok_ref[...].astype(F32))
    out_ref[...] = back_ref[...] + norm_back(upstream, unit, inverse, gain_ref[...])


def along_narrow(x, k):
    return lax.ppermute(x, "narrow", [(i, i ^ k) for i in range(NARROW)])


def in_plane(x):
    size = lax.axis_size("wide")
    copies = jnp.broadcast_to(x[None], (size, *x.shape))
    return lax.all_to_all(copies, "wide", 0, 0)


def per_device(
    tokens, segments, first_gain, qkv_weight, output_weight, second_gain, geglu_weight, down_weight,
    cotangent,
):
    size = lax.axis_size("wide")
    mine = lax.axis_index("wide")
    z = lax.axis_index("narrow")
    z_array = z.astype(jnp.int32).reshape(1)
    hidden = geglu_weight.shape[2]
    rows_d = D // size
    gain_one = first_gain.reshape(1, D)
    gain_two = second_gain.reshape(1, D)

    geglu_slice = lax.dynamic_slice_in_dim(geglu_weight, mine * rows_d, rows_d, 1)
    down_slice = lax.dynamic_slice_in_dim(down_weight, mine * rows_d, rows_d, 1).T
    ff_slice = jnp.concatenate([geglu_slice, down_slice[None]], axis=0)
    out_rows = COLS // size
    out_slice = lax.dynamic_slice_in_dim(output_weight, mine * out_rows, out_rows, 0)
    ff_there = in_plane(along_narrow(ff_slice, 2))
    out_there = in_plane(jnp.stack([along_narrow(out_slice, k) for k in (1, 2, 3)]))
    other = ff_there.transpose(1, 0, 2, 3).reshape(3, D, hidden)
    whole_out = jnp.concatenate(
        [output_weight[None], out_there.transpose(1, 0, 2, 3).reshape(3, COLS, D)], axis=0
    )

    def block_of(x, k):
        return lax.dynamic_slice_in_dim(x, (z ^ k) * BLOCK, BLOCK, 0)

    tok_own, tok_par = block_of(tokens, 0), block_of(tokens, 1)
    cot_own, cot_par = block_of(cotangent, 0), block_of(cotangent, 1)

    piece = sds((BLOCK, 2 * COLS), BF16)
    wide_rows = sds((LEN, LANES), BF16)
    c0, c1, c2, c3, q, k, v, normed_one, lse, trig, segc = call(
        forward_kernel,
        (z_array, tokens, segments, gain_one, qkv_weight, jnp.asarray(rotary_table())),
        (piece, piece, piece, piece, wide_rows, wide_rows, wide_rows, sds((LEN, D), BF16),
         sds((LEN, 128), F32), sds((LEN, 2 * LANES), F32), sds((LEN, 128), F32)),
        [pltpu.VMEM((LEN, LANES), F32), pltpu.VMEM((NARROW, BLOCK, 2 * COLS), BF16)],
        flops=5_000_000_000,
    )
    context = (c0, *(along_narrow(c, k) for k, c in ((1, c1), (2, c2), (3, c3))))

    own = sds((BLOCK, D), F32)
    own_low = sds((BLOCK, D), BF16)
    res, normed_two, act, gb, keep, send, out_keep, out_send = call(
        middle_kernel,
        (tok_own, tok_par, cot_own, cot_par, *context, whole_out, gain_two, geglu_weight,
         down_weight, other),
        (sds((2 * BLOCK, D), F32), sds((2 * BLOCK, D), BF16), sds((2, 2 * BLOCK, hidden), BF16),
         sds((2, 2, 2 * BLOCK, hidden), BF16), own, own_low, own, own_low),
        [pltpu.VMEM((2 * BLOCK, D), BF16)],
        flops=8_000_000_000,
        scalars=0,
    )
    recv = along_narrow(send, 1)
    layer_out = (out_keep + along_narrow(out_send, 1).astype(F32)).astype(BF16)
    (ff_part,) = call(
        ff_grad_kernel,
        (normed_two, act, gb, cot_own, cot_par),
        (sds((D, 6 * hidden), BF16),),
        flops=4_000_000_000,
        scalars=0,
    )
    ff_blocks = lax.all_to_all(ff_part.reshape(size, rows_d, 6 * hidden), "wide", 0, 0)

    low_piece = sds((BLOCK // 2, 2 * COLS), BF16)
    back, low, gain_two_part, b0, b1, b2, b3 = call(
        residual_kernel,
        (keep, recv, res, gain_two, cot_own, whole_out),
        (own, own_low, sds((1, D), F32), low_piece, low_piece, low_piece, low_piece),
        flops=1_000_000_000,
        scalars=0,
    )
    upstream = (b0, *(along_narrow(b, k) for k, b in ((1, b1), (2, b2), (3, b3))))
    (out_part,) = call(
        output_grad_kernel,
        (low, *context),
        (sds((D, NARROW * COLS), BF16),),
        flops=500_000_000,
        scalars=0,
    )
    out_blocks = lax.all_to_all(out_part.reshape(size, rows_d, NARROW * COLS), "wide", 0, 0)

    qkv_back, n0, n1, n2, n3 = call(
        backward_kernel,
        (z_array, segments, segc, q, k, v, lse, trig, *upstream, qkv_weight),
        (sds((LEN, 3 * COLS), BF16), own, own_low, own_low, own_low),
        [pltpu.VMEM((LEN, LANES), BF16)] + [pltpu.VMEM((LEN, LANES), F32)] * 3,
        flops=6_000_000_000,
    )
    others = [along_narrow(n, k) for k, n in ((1, n1), (2, n2), (3, n3))]
    qkv_part, gain_one_part = call(
        qkv_grad_kernel,
        (normed_one, qkv_back, qkv_weight),
        (sds((D, 3 * COLS), BF16), sds((D, 128), F32)),
        flops=1_000_000_000,
        scalars=0,
    )
    qkv_blocks = lax.all_to_all(qkv_part.reshape(size, rows_d, 3 * COLS), "wide", 0, 0)
    gains = jnp.stack([gain_one_part[:, 0] / first_gain, gain_two_part[0]])
    bit = 1
    while bit < size:
        gains = gains + lax.ppermute(gains, "wide", [(i, i ^ bit) for i in range(size)])
        bit *= 2
    for bit in (1, 2):
        gains = gains + along_narrow(gains, bit)

    (tokens_grad,) = call(
        final_kernel, (tok_own, gain_one, back, n0, *others), (own,), scalars=0
    )

    ff_sum = jnp.sum(ff_blocks.astype(F32), axis=0)
    half = 3 * hidden
    ff_own = ff_sum[:, :half] + along_narrow(ff_sum[:, half:].astype(BF16), 2).astype(F32)
    geglu_grad = ff_own[:, : 2 * hidden].reshape(rows_d, 2, hidden).transpose(1, 0, 2)
    down_grad = ff_own[:, 2 * hidden :].T
    out_sum = jnp.sum(out_blocks.astype(F32), axis=0)
    out_own = out_sum[:, :COLS]
    for k in (1, 2, 3):
        there = out_sum[:, k * COLS : (k + 1) * COLS].astype(BF16)
        out_own = out_own + along_narrow(there, k).astype(F32)
    qkv_sum = jnp.sum(qkv_blocks.astype(F32), axis=0)
    qkv_grad = qkv_sum.reshape(rows_d, 3, COLS).transpose(1, 0, 2)
    return (
        layer_out, tokens_grad, gains[0], qkv_grad, out_own.T, gains[1], geglu_grad, down_grad,
    )


def solution(mesh):
    return jax.shard_map(
        per_device,
        mesh=mesh,
        in_specs=(
            P("wide", None),
            P("wide", None),
            P(),
            P(None, None, "narrow"),
            P("narrow", None),
            P(),
            P(None, None, "narrow"),
            P("narrow", None),
            P("wide", None),
        ),
        out_specs=(
            P(("wide", "narrow"), None),
            P(("wide", "narrow"), None),
            P(),
            P(None, "wide", "narrow"),
            P("narrow", "wide"),
            P(),
            P(None, "wide", "narrow"),
            P("narrow", "wide"),
        ),
        check_vma=False,
    )
```

```python
import functools
import math

import jax
import jax.numpy as jnp
import numpy as np
from jax import lax
from jax.experimental import pallas as pl
from jax.experimental.pallas import tpu as pltpu
from jax.sharding import PartitionSpec as P

HEAD = 64
LEN = 1024
D = 768
HEADS_HERE = 3
COLS = HEADS_HERE * HEAD
LANES = 256
DOC = 256
QB = 128
WINDOW = QB + 2 * DOC
EPSILON = 1e-05
ROPE_BASE = 160000.0
NARROW = 4
BLOCK = LEN // NARROW
F32 = jnp.float32
GAIN_ROWS = 16
BF16 = jnp.bfloat16
NEGATIVE = -1e30
MIB = 1024 * 1024
COST = {
    "finish_kernel": 1,
    "qkv_sum_kernel": 1,
    "pack_kernel": 1,
    "arrived_kernel": 1,
    "pairs_kernel": 1,
    "quads_kernel": 1,
    "project_kernel": 6,
    "attend_kernel": 10000,
    "middle_kernel": 10000,
    "partner_kernel": 3,
    "own_kernel": 10,
    "residual_kernel": 10000,
    "output_grad_kernel": 2,
    "fold_kernel": 2,
    "backward_far_kernel": 10000,
    "backward_near_kernel": 10000,
    "add_kernel": 10000,
    "qkv_grad_kernel": 1,
    "collect_kernel": 1,
    "final_kernel": 10000,
}

NN = (((1,), (0,)), ((), ()))
NT = (((1,), (1,)), ((), ()))
TN = (((0,), (0,)), ((), ()))


def dot(a, b, dims=NN):
    return lax.dot_general(a, b, dims, preferred_element_type=F32)


def call(body, ins, outs, scratch=(), scalars=1):
    name = getattr(body, "func", body).__name__
    specs = [pl.BlockSpec(memory_space=pltpu.SMEM)] * scalars
    specs += [pl.BlockSpec(memory_space=pltpu.VMEM)] * (len(ins) - scalars)
    size = sum(math.prod(x.shape) * x.dtype.itemsize for x in (*ins, *outs))
    held = sum(math.prod(x.shape) * x.dtype.itemsize for x in scratch)
    return pl.pallas_call(
        body,
        name=name,
        out_shape=tuple(jax.ShapeDtypeStruct(o.shape, o.dtype) for o in outs),
        in_specs=specs,
        out_specs=tuple(pl.BlockSpec(memory_space=pltpu.VMEM) for _ in outs),
        scratch_shapes=list(scratch),
        compiler_params=pltpu.CompilerParams(vmem_limit_bytes=size + size // 4 + held + 8 * MIB),
        cost_estimate=pl.CostEstimate(flops=COST[name] * 10**9, bytes_accessed=size, transcendentals=0),
    )(*ins)


def sds(shape, dtype):
    return jax.ShapeDtypeStruct(shape, dtype)


def rotary_table():
    position = np.arange(DOC, dtype=np.float64)
    frequency = ROPE_BASE ** (-2.0 * np.arange(HEAD // 2, dtype=np.float64) / HEAD)
    angle = position[:, None] * frequency[None, :]
    cosine, sine = np.cos(angle), np.sin(angle)
    table = np.zeros((DOC, 2 * LANES), np.float32)
    for h in range(HEADS_HERE):
        base = h * HEAD
        table[:, base : base + 32] = cosine
        table[:, base + 32 : base + 64] = cosine
        table[:, LANES + base : LANES + base + 32] = -sine
        table[:, LANES + base + 32 : LANES + base + 64] = sine
    high = table.astype(jnp.bfloat16)
    low = (table - high.astype(np.float32)).astype(jnp.bfloat16)
    return np.stack([high, low])


def normalize(values):
    centre = values - jnp.mean(values, axis=-1, keepdims=True)
    spread = jnp.mean(centre * centre, axis=-1, keepdims=True)
    inverse = lax.rsqrt(spread + EPSILON)
    return centre * inverse, inverse


def norm_back(upstream, unit_rows, inverse, gain):
    scaled = upstream * gain
    first_mean = jnp.mean(scaled, axis=-1, keepdims=True)
    second_mean = jnp.mean(scaled * unit_rows, axis=-1, keepdims=True)
    return inverse * (scaled - first_mean - unit_rows * second_mean)


def lane_head(rows):
    return lax.broadcasted_iota(jnp.int32, (rows, LANES), 1) // HEAD


def swap_halves(x):
    lane = lax.broadcasted_iota(jnp.int32, x.shape, 1)
    return jnp.where(
        lane % HEAD < HEAD // 2,
        pltpu.roll(x, LANES - HEAD // 2, 1),
        pltpu.roll(x, HEAD // 2, 1),
    )


def by_head(block, head):
    return jnp.concatenate(
        [jnp.where(head == h, block, jnp.zeros_like(block)) for h in range(HEADS_HERE)], axis=0
    )


def merge_heads(stacked, head):
    parts = jnp.split(stacked, HEADS_HERE, axis=0)
    return jnp.where(head == 0, parts[0], jnp.where(head == 1, parts[1], parts[2]))


def own_window(i):
    return jnp.clip(i - DOC // QB, 0, (LEN - WINDOW) // QB) * QB


def static_window(i):
    reach = DOC // QB
    return max(0, i - reach) * QB, min(LEN // QB, i + reach + 1) * QB


def project_kernel(
    tok_ref, seg_ref, gain_ref, w_ref, table_ref,
    q_ref, k_ref, v_ref, normed_ref, trig_ref, segc_ref,
    proj_ref,
):
    seg = jnp.broadcast_to(seg_ref[...].astype(F32), (8, LEN))
    index = lax.broadcasted_iota(jnp.int32, (8, LEN), 1)
    first = jnp.where(seg != pltpu.roll(seg, 1, 1), index, 0)
    first = jnp.where(index == 0, 0, first).astype(F32)
    shift = 1
    while shift < DOC:
        first = jnp.maximum(first, jnp.where(index >= shift, pltpu.roll(first, shift, 1), 0.0))
        shift *= 2
    place = index.astype(F32) - first
    segc_ref[...] = jnp.transpose(jnp.broadcast_to(seg[:1], (128, LEN)))
    placec = jnp.transpose(jnp.broadcast_to(place[:1], (128, LEN)))
    lane = lax.broadcasted_iota(jnp.int32, (LEN, 128), 1).astype(F32)
    hot = jnp.concatenate(
        [jnp.where(placec == lane + 128.0 * j, 1.0, 0.0) for j in range(DOC // 128)], axis=1
    ).astype(BF16)
    trig_ref[...] = dot(hot, table_ref[0]) + dot(hot, table_ref[1])

    def norm_rows(i, carry):
        rows = pl.ds(pl.multiple_of(i * 128, 128), 128)
        unit, _ = normalize(tok_ref[rows, :].astype(F32))
        normed_ref[rows, :] = (unit * gain_ref[...]).astype(BF16)
        return carry

    lax.fori_loop(0, LEN // 128, norm_rows, 0)
    proj_ref[:, COLS:] = jnp.zeros((LEN, LANES - COLS), F32)
    for s, out in enumerate((q_ref, k_ref)):
        proj_ref[:, :COLS] = dot(normed_ref[...], w_ref[s], NT)
        x = proj_ref[...]
        out[...] = (x * trig_ref[:, :LANES] + swap_halves(x) * trig_ref[:, LANES:]).astype(BF16)
    proj_ref[:, :COLS] = dot(normed_ref[...], w_ref[2], NT)
    v_ref[...] = proj_ref[...].astype(BF16)


def attend_kernel(
    s_ref, seg_ref, segc_ref, q_ref, k_ref, v_ref, c0_ref, c1_ref, c2_ref, c3_ref, lse_ref, ctx_ref
):
    z = s_ref[0]
    head = lane_head(QB)
    column = lax.broadcasted_iota(jnp.int32, (QB, 128), 1)
    for i in range(LEN // QB):
        low, high = static_window(i)
        rows = slice(i * QB, (i + 1) * QB)
        stacked = by_head(q_ref[rows, :] * jnp.asarray(1.0 / math.sqrt(HEAD), BF16), head)
        scores = dot(stacked, k_ref[low:high, :], NT)
        same = segc_ref[rows, 0:1] == seg_ref[0:1, low:high].astype(F32)
        parts, logs = [], []
        for h in range(HEADS_HERE):
            mine = jnp.where(same, scores[h * QB : (h + 1) * QB], NEGATIVE)
            top = jnp.max(mine, axis=-1, keepdims=True)
            weights = jnp.exp(mine - top)
            total = jnp.sum(weights, axis=-1, keepdims=True)
            parts.append((weights * (1.0 / total)).astype(BF16))
            logs.append(top + jnp.log(total))
        lse_ref[rows, :] = jnp.where(column == 0, logs[0], jnp.where(column == 1, logs[1], logs[2]))
        mixed = dot(jnp.concatenate(parts, axis=0), v_ref[low:high, :])
        context = merge_heads(mixed, head)[:, :COLS].astype(BF16)
        block, r = i * QB // BLOCK, i * QB % BLOCK
        ctx_ref[block, r : r + QB, :COLS] = context
        ctx_ref[block ^ 1, r : r + QB, COLS:] = context
    for k, out in enumerate((c0_ref, c1_ref, c2_ref, c3_ref)):
        out[...] = ctx_ref[z ^ k]


def place_slots(s_ref, even_ref, odd_ref, out_ref, first, rows):
    cols = D // 2
    for i in range(8):
        slot = s_ref[2 + i]
        piece = even_ref[i, first : first + rows, :] if i < 4 else odd_ref[i - 4, first : first + rows, :]
        there = pl.ds(pl.multiple_of((slot // 2) * rows, 16), rows)
        out_ref[there, pl.ds(pl.multiple_of((slot % 2) * cols, 128), cols)] = piece


def gated(normed, cot, w_in, w_down, act_ref, gb_ref, width):
    both = dot(normed, w_in, NT)
    gate, linear = both[:, :width], both[:, width:]
    act_back = dot(cot, w_down, NT)
    cdf = 0.5 * (1.0 + lax.erf(gate * math.sqrt(0.5)))
    slope = cdf + gate * (jnp.exp(-0.5 * gate * gate) * (1.0 / math.sqrt(2.0 * math.pi)))
    gelu = gate * cdf
    act_ref[...] = (gelu * linear).astype(BF16)
    gb_ref[:, :width] = (act_back * linear * slope).astype(BF16)
    gb_ref[:, width:] = (act_back * gelu).astype(BF16)
    return dot(act_ref[...], w_down), dot(gb_ref[...], w_in)


def middle_kernel(
    s_ref, tok_ref, cot_ref, c0, c1, c2, c3, w_ref, here_ref, there_ref, gain_ref, gw_ref, dw_ref,
    res_ref, normed_ref, act_ref, gb_ref, branch_ref, back_ref, wo_ref, cot_out,
):
    z = s_ref[0]
    wo_ref[0] = w_ref[...]
    few = COLS // 4
    pieces = ((0, here_ref, 0), (2, here_ref, 1), (1, there_ref, 0), (3, there_ref, 1))
    for chip, ref, i in pieces:
        there = pl.ds(pl.multiple_of(s_ref[10 + chip] * few, 16), few)
        for k in range(3):
            for side in range(2):
                first = (2 * k + side) * few
                lanes = slice(side * (D // 2), (side + 1) * (D // 2))
                wo_ref[k + 1, there, lanes] = ref[i, first : first + few, :]
    for half in range(2):
        base = (z if half == 0 else z ^ 1) * BLOCK
        there = pl.ds(pl.multiple_of(base, BLOCK), BLOCK)
        rows = slice(half * BLOCK, (half + 1) * BLOCK)
        attended = jnp.zeros((BLOCK, D), F32)
        for k, c in enumerate((c0, c1, c2, c3)):
            attended += dot(c[:, half * COLS : (half + 1) * COLS], wo_ref[k])
        residual = tok_ref[there, :].astype(F32) + attended
        if half == 0:
            res_ref[...] = residual
            branch_ref[rows, :] = residual
        else:
            branch_ref[rows, :] = jnp.zeros_like(residual)
        unit, _ = normalize(residual)
        normed_ref[rows, :] = (unit * gain_ref[...]).astype(BF16)
        cot_out[rows, :] = cot_ref[there, :]
    branch, back = gated(
        normed_ref[...], cot_out[...], gw_ref[...], dw_ref[...], act_ref, gb_ref, dw_ref.shape[0]
    )
    branch_ref[...] += branch
    back_ref[...] = back


def partner_kernel(
    s_ref, normed_ref, cot_ref, branch_in, back_in, fe_ref, fo_ref,
    act_ref, gb_ref, branch_ref, back_ref, other_ref,
):
    width = act_ref.shape[1]
    place_slots(s_ref, fe_ref, fo_ref, other_ref, 0, other_ref.shape[0] // 4)
    branch, back = gated(
        normed_ref[BLOCK:, :], cot_ref[BLOCK:, :], other_ref[: 2 * width, :],
        other_ref[2 * width : 3 * width, :], act_ref, gb_ref, width,
    )
    branch_ref[...] = (branch_in[BLOCK:, :] + branch).astype(BF16)
    back_ref[...] = (back_in[BLOCK:, :] + back).astype(BF16)


def own_kernel(
    s_ref, normed_ref, cot_ref, branch_in, back_in, other_ref, act_ref, gb_ref, act_par, gb_par,
    branch_ref, back_ref, whole_ref,
    act_own, gb_own,
):
    width = act_ref.shape[1]
    branch, back = gated(
        normed_ref[:BLOCK, :], cot_ref[:BLOCK, :], other_ref[: 2 * width, :],
        other_ref[2 * width : 3 * width, :], act_own, gb_own, width,
    )
    branch_ref[...] = branch_in[:BLOCK, :] + branch
    back_ref[...] = back_in[:BLOCK, :] + back
    half = whole_ref.shape[1] // 2
    whole_ref[:, : 2 * width] = dot(normed_ref[...], gb_ref[...], TN).astype(BF16)
    whole_ref[:, 2 * width : 3 * width] = dot(cot_ref[...], act_ref[...], TN).astype(BF16)
    part = dot(normed_ref[:BLOCK, :], gb_own[...], TN) + dot(normed_ref[BLOCK:, :], gb_par[...], TN)
    whole_ref[:, half : half + 2 * width] = part.astype(BF16)
    part = dot(cot_ref[:BLOCK, :], act_own[...], TN) + dot(cot_ref[BLOCK:, :], act_par[...], TN)
    whole_ref[:, half + 2 * width : half + 3 * width] = part.astype(BF16)
    pad = jnp.zeros((D, half - 3 * width), BF16)
    whole_ref[:, 3 * width : half] = pad
    whole_ref[:, half + 3 * width :] = pad


def finish_kernel(keep_ref, r1, r2, r3, geglu_ref, down_ref, out_ref, pad_ref):
    half = r2.shape[1] - COLS
    rows, width = geglu_ref.shape[1:]
    ff = keep_ref[:, :half] + r2[:, :half].astype(F32)
    geglu_ref[0] = ff[:, :width]
    geglu_ref[1] = ff[:, width : 2 * width]
    out = keep_ref[:, half:] + r1[...].astype(F32) + r2[:, half:].astype(F32) + r3[...].astype(F32)
    pad_ref[...] = jnp.zeros_like(pad_ref)
    pad_ref[:rows, :width] = ff[:, 2 * width : 3 * width]
    down_ref[...] = jnp.transpose(pad_ref[...])[:width, :rows]
    pad_ref[:rows, :COLS] = out
    out_ref[...] = jnp.transpose(pad_ref[...])[:COLS, :rows]


def qkv_sum_kernel(parts_ref, grad_ref, gains_ref):
    rows = grad_ref.shape[1]
    total = jnp.sum(parts_ref[...].astype(F32), axis=0)
    for s in range(3):
        grad_ref[s] = total[:rows, s * COLS : (s + 1) * COLS]
    for gain in range(2):
        for side in range(2):
            first = rows + 6 * gain + side
            part = total[first : first + 1] + total[first + 2 : first + 3] + total[first + 4 : first + 5]
            gains_ref[gain : gain + 1, side * (D // 2) : (side + 1) * (D // 2)] = part[:, : D // 2]


def residual_kernel(
    keep_ref, recv_ref, res_ref, gain_ref, cot_ref, wo_ref,
    back_ref, low_ref, gain_out, b0, b1, b2, b3,
):
    unit, inverse = normalize(res_ref[...])
    upstream = keep_ref[...] + recv_ref[...].astype(F32)
    back = cot_ref[:BLOCK, :].astype(F32) + norm_back(upstream, unit, inverse, gain_ref[...])
    back_ref[...] = back
    gain_out[...] = jnp.sum(upstream * unit, axis=0, keepdims=True)
    low = back.astype(BF16)
    low_ref[...] = low
    for k, out in enumerate((b0, b1, b2, b3)):
        part = dot(low, wo_ref[k], NT).astype(BF16)
        out[:, :COLS] = part[: BLOCK // 2]
        out[:, COLS:] = part[BLOCK // 2 :]


def output_grad_kernel(s_ref, low_ref, c0, c1, c2, c3, ff_ref, even_ref, odd_ref, whole_ref):
    for k, c in enumerate((c0, c1, c2, c3)):
        whole_ref[:, k * COLS : (k + 1) * COLS] = dot(low_ref[...], c[:, :COLS], TN).astype(BF16)
    rows, ff = even_ref.shape[1], ff_ref.shape[1]
    for i in range(8):
        there = pl.ds(pl.multiple_of(s_ref[2 + i] * rows, 16), rows)
        out = even_ref.at[i] if i < 4 else odd_ref.at[i - 4]
        out[:, :ff] = ff_ref[there, :]
        out[:, ff:] = whole_ref[there, :]


def collect_kernel(own_ref, r1, r2, r3, keep_ref, s1, s2, s3):
    total = own_ref[...] + r1[...].astype(F32) + r2[...].astype(F32) + r3[...].astype(F32)
    half = keep_ref.shape[1] - COLS
    keep_ref[:, :half] = total[:, :half]
    keep_ref[:, half:] = total[:, 2 * half : 2 * half + COLS]
    s2[:, :half] = total[:, half : 2 * half].astype(BF16)
    for k, out in ((1, s1), (2, s2), (3, s3)):
        first = 2 * half + k * COLS
        out[:, out.shape[1] - COLS :] = total[:, first : first + COLS].astype(BF16)


def pack_kernel(s_ref, w_in_ref, w_down_ref, w_out_ref, out_ref, both_ref, whole_ref):
    slot = s_ref[1]
    there, cols = slot // 2, pl.ds(pl.multiple_of((slot % 2) * (D // 2), 128), D // 2)
    n_in, n_down = w_in_ref.shape[0], w_down_ref.shape[0]
    whole_ref[:n_in, :] = w_in_ref[...]
    whole_ref[n_in : n_in + n_down, :] = w_down_ref[...]
    whole_ref[n_in + n_down :, :] = jnp.zeros((whole_ref.shape[0] - n_in - n_down, D), BF16)
    rows = whole_ref.shape[0] // 4
    few = w_out_ref.shape[0] // 4
    here = pl.ds(pl.multiple_of(there * few, 16), few)
    both_ref[:rows, :] = whole_ref[pl.ds(pl.multiple_of(there * rows, 16), rows), cols]
    for side in range(2):
        mine = w_out_ref[here, side * (D // 2) : (side + 1) * (D // 2)]
        out_ref[side * few : (side + 1) * few, :] = mine
        both_ref[rows + side * few : rows + (side + 1) * few, :] = mine


def arrived_kernel(s_ref, f1, f2, f3, ff_ref, out_ref):
    ff, few = ff_ref.shape[0], f1.shape[0]
    ff_ref[...] = f2[:ff, :]
    for i, piece in enumerate((f1[...], f2[ff:, :], f3[...])):
        out_ref[i * few : (i + 1) * few, :] = piece


def pairs_kernel(s_ref, a0, a1, b0, b1, a_ref, b_ref):
    for i, (a, b) in enumerate(((a0, b0), (a1, b1))):
        a_ref[i] = a[...]
        b_ref[i] = b[...]


def quads_kernel(a0, a1, out_ref):
    out_ref[:2] = a0[...]
    out_ref[2:] = a1[...]


def backward_steps(
    first, count, seg_ref, segc_ref, q_ref, k_ref, v_ref, lse_ref, back_ref, dq_ref, dk_ref, dv_ref
):
    head = lane_head(QB)
    scale = jnp.asarray(1.0 / math.sqrt(HEAD), BF16)
    for j in range(count):
        i = first + j
        rows = pl.ds(pl.multiple_of(i * QB, QB), QB)
        keys = pl.ds(pl.multiple_of(own_window(i), QB), WINDOW)
        stacked = by_head(q_ref[rows, :] * scale, head)
        upstream = by_head(back_ref[rows, :], head)
        scores = dot(stacked, k_ref[keys, :], NT)
        prob_back = dot(upstream, v_ref[keys, :], NT)
        same = segc_ref[rows, 0:1] == seg_ref[0:1, keys].astype(F32)
        probs, grads = [], []
        for h in range(HEADS_HERE):
            at = slice(h * QB, (h + 1) * QB)
            prob = jnp.exp(jnp.where(same, scores[at], NEGATIVE) - lse_ref[rows, h : h + 1])
            inner = jnp.sum(prob * prob_back[at], axis=-1, keepdims=True)
            probs.append(prob.astype(BF16))
            grads.append((prob * (prob_back[at] - inner)).astype(BF16))
        prob = jnp.concatenate(probs, axis=0)
        grad = jnp.concatenate(grads, axis=0)
        dv_ref[keys, :] += dot(prob, upstream, TN)
        dk_ref[keys, :] += dot(grad, stacked, TN)
        dq_ref[rows, :] = merge_heads(dot(grad, k_ref[keys, :]), head) * (1.0 / math.sqrt(HEAD))


def rows_back(base, dq_ref, dk_ref, dv_ref, trig_ref, w_ref, qkv_ref):
    rows = pl.ds(pl.multiple_of(base, BLOCK), BLOCK)
    cosine, signed = trig_ref[rows, :LANES], trig_ref[rows, LANES:]
    total = None
    for part, grad_ref in enumerate((dq_ref, dk_ref, dv_ref)):
        g = grad_ref[rows, :]
        if part < 2:
            g = g * cosine - swap_halves(g) * signed
        low = g[:, :COLS].astype(BF16)
        qkv_ref[:, part * COLS : (part + 1) * COLS] = low
        product = dot(low, w_ref[part])
        total = product if total is None else total + product
    return total


def backward_far_kernel(
    s_ref, seg_ref, segc_ref, q_ref, k_ref, v_ref, lse_ref, trig_ref, b0, b1, b2, b3, w_ref,
    n2, n3, qkv_ref, back_ref, dq_ref, dk_ref, dv_ref,
):
    z = s_ref[0]
    pair = z // 2
    half = BLOCK // 2
    back_ref[:, COLS:] = jnp.zeros((LEN, LANES - COLS), BF16)
    for k, b in enumerate((b0, b1, b2, b3)):
        base = pl.multiple_of((z ^ k) * BLOCK, BLOCK)
        back_ref[pl.ds(base, half), :COLS] = b[:, :COLS]
        back_ref[pl.ds(pl.multiple_of(base + half, half), half), :COLS] = b[:, COLS:]
    dk_ref[...] = jnp.zeros_like(dk_ref)
    dv_ref[...] = jnp.zeros_like(dv_ref)
    refs = (seg_ref, segc_ref, q_ref, k_ref, v_ref, lse_ref, back_ref, dq_ref, dk_ref, dv_ref)
    steps = LEN // QB
    reach = DOC // QB
    backward_steps((1 - pair) * (steps // 2 - reach), steps // 2 + reach, *refs)
    for k, out in ((2, n2), (3, n3)):
        at = qkv_ref.at[(k - 2) * BLOCK : (k - 1) * BLOCK]
        part = rows_back((z ^ k) * BLOCK, dq_ref, dk_ref, dv_ref, trig_ref, w_ref, at)
        out[...] = part.astype(out.dtype)


def add_kernel(mine_ref, recv_ref, out_ref):
    out_ref[...] = (mine_ref[...] + recv_ref[...].astype(F32)).astype(out_ref.dtype)


def backward_near_kernel(
    s_ref, seg_ref, segc_ref, q_ref, k_ref, v_ref, lse_ref, trig_ref, back_ref, dq_in, dk_in, dv_in,
    w_ref, n0, n1, qkv_ref, dq_ref, dk_ref, dv_ref,
):
    z = s_ref[0]
    pair = z // 2
    dq_ref[...] = dq_in[...]
    dk_ref[...] = dk_in[...]
    dv_ref[...] = dv_in[...]
    refs = (seg_ref, segc_ref, q_ref, k_ref, v_ref, lse_ref, back_ref, dq_ref, dk_ref, dv_ref)
    steps = LEN // QB
    reach = DOC // QB
    backward_steps(pair * (steps // 2 + reach), steps // 2 - reach, *refs)
    for k, out in ((0, n0), (1, n1)):
        at = qkv_ref.at[k * BLOCK : (k + 1) * BLOCK]
        part = rows_back((z ^ k) * BLOCK, dq_ref, dk_ref, dv_ref, trig_ref, w_ref, at)
        out[...] = part.astype(out.dtype)


def qkv_grad_kernel(
    s_ref, normed_ref, near_ref, far_ref, w_ref, gain_ref, gain_two_ref, out_ref, whole_ref, rows_ref
):
    for k in range(NARROW):
        base = pl.multiple_of((s_ref[0] ^ k) * BLOCK, BLOCK)
        rows_ref[k * BLOCK : (k + 1) * BLOCK, :] = normed_ref[pl.ds(base, BLOCK), :]
    pair = 2 * BLOCK
    total = None
    for s in range(3):
        cols = slice(s * COLS, (s + 1) * COLS)
        part = dot(rows_ref[:pair, :], near_ref[:, cols], TN)
        part += dot(rows_ref[pair:, :], far_ref[:, cols], TN)
        whole_ref[:, cols] = part.astype(BF16)
        weighted = part * jnp.transpose(w_ref[s].astype(F32))
        total = weighted if total is None else total + weighted
    column = jnp.broadcast_to(jnp.sum(total, axis=1, keepdims=True), (D, 128))
    gains = (jnp.transpose(column)[:1, :] / gain_ref[...], gain_two_ref[...])
    extra = jnp.zeros((GAIN_ROWS, D // 2), F32)
    row = lax.broadcasted_iota(jnp.int32, extra.shape, 0)
    at = 0
    for gain in gains:
        rest = gain
        for _ in range(3):
            term = rest.astype(BF16).astype(F32)
            rest = rest - term
            for side in range(2):
                extra = jnp.where(row == at, term[:, side * (D // 2) : (side + 1) * (D // 2)], extra)
                at += 1
    blocks, rows, cols = out_ref.shape
    rows -= GAIN_ROWS
    for i in range(blocks):
        if rows % 16 == 0:
            out_ref[i, :rows, :] = whole_ref[i * rows : (i + 1) * rows, :]
            out_ref[i, rows:, :] = jnp.zeros((GAIN_ROWS, cols), BF16)
            out_ref[i, rows:, : D // 2] = extra.astype(BF16)
        else:
            lines = [whole_ref[i * rows : (i + 1) * rows, :].astype(F32)]
            pad = jnp.zeros((GAIN_ROWS, cols - D // 2), F32)
            lines.append(jnp.concatenate([extra, pad], axis=1))
            out_ref[i] = jnp.concatenate(lines, axis=0).astype(BF16)


def final_kernel(s_ref, tok_ref, gain_ref, back_ref, n0, n1, n2, out_ref):
    upstream = n0[...] + n1[:BLOCK, :].astype(F32) + n2[...].astype(F32)
    rows = pl.ds(pl.multiple_of(s_ref[0] * BLOCK, BLOCK), BLOCK)
    unit, inverse = normalize(tok_ref[rows, :].astype(F32))
    out_ref[...] = back_ref[...] + norm_back(upstream, unit, inverse, gain_ref[...])


def fold_kernel(even_ref, recv_ref, own_ref, s1_ref, s2_ref, s3_ref):
    for i, out in enumerate((own_ref, s1_ref, s2_ref, s3_ref)):
        out[...] = (even_ref[i].astype(F32) + recv_ref[i].astype(F32)).astype(out.dtype)


def along_narrow(x, k):
    return lax.ppermute(x, "narrow", [(i, i ^ k) for i in range(NARROW)])


def along_wide(x, k):
    return lax.ppermute(x, "wide", [(i, i ^ k) for i in range(lax.axis_size("wide"))])


def tie(x, *others):
    return lax.optimization_barrier((x, *others))[0]


def quarter_slice(x, slot):
    rows, cols = x.shape[-2] // 4, x.shape[-1] // 2
    x = lax.dynamic_slice_in_dim(x, (slot // 2) * rows, rows, x.ndim - 2)
    return lax.dynamic_slice_in_dim(x, (slot % 2) * cols, cols, x.ndim - 1)


def all_slots(x, hops):
    whole = jnp.stack([along_narrow(x, k) for k in hops])
    slots = jnp.stack([quarter_slice(whole, i) for i in range(8)])
    return slots[:4], slots[4:]


def sum_wide(x):
    return jnp.sum(lax.all_to_all(x, "wide", 0, 0).astype(F32), axis=0)


def per_device(
    tokens, segments, first_gain, qkv_weight, output_weight, second_gain, geglu_weight, down_weight,
    cotangent,
):
    size = lax.axis_size("wide")
    plane = size == 8
    mine = lax.axis_index("wide").astype(jnp.int32)
    z = lax.axis_index("narrow").astype(jnp.int32)
    order = jnp.asarray([0, 2, 4, 6, 1, 3, 5, 7], jnp.int32)
    slots = (mine ^ order) if plane else jnp.arange(8, dtype=jnp.int32)
    chips = ((mine // 2) ^ jnp.arange(4, dtype=jnp.int32)) if plane else jnp.arange(4, dtype=jnp.int32)
    scalars = jnp.concatenate([z[None], mine[None], slots, chips])
    hidden = geglu_weight.shape[2]
    padded = -(-3 * hidden // 64) * 64
    rows_d = D // size
    gain_one = first_gain.reshape(1, D)
    gain_two = second_gain.reshape(1, D)
    w_qkv = qkv_weight.transpose(0, 2, 1)
    w_in = geglu_weight.transpose(0, 2, 1).reshape(2 * hidden, D)

    few, many = COLS // 4, padded // 4
    if plane:
        slot_out, slot_both = call(
            pack_kernel,
            (scalars, w_in, down_weight, output_weight),
            (sds((2 * few, D // 2), BF16), sds((many + 2 * few, D // 2), BF16)),
            [pltpu.VMEM((padded, D), BF16)],
        )
        fetched = [along_narrow(x, k) for k, x in ((1, slot_out), (2, slot_both), (3, slot_out))]
    else:
        whole = jnp.concatenate(
            [w_in, down_weight, jnp.zeros((padded - 3 * hidden, D), BF16)], axis=0
        )
        even, odd = (x[:, 0] for x in all_slots(whole, (2,)))
        quarters = jnp.stack([along_narrow(output_weight, k) for k in (1, 2, 3)])
        quarters = quarters.reshape(3, 4, few, 2, D // 2).transpose(1, 0, 3, 2, 4)
        quarters = quarters.reshape(4, 6 * few, D // 2)
        b_pair, b_there = quarters[::2], quarters[1::2]

    wide_rows = sds((LEN, LANES), BF16)
    q, k, v, normed_one, trig, segc = call(
        project_kernel,
        (tokens, segments, gain_one, w_qkv, jnp.asarray(rotary_table())),
        (wide_rows, wide_rows, wide_rows, sds((LEN, D), BF16), sds((LEN, 2 * LANES), F32),
         sds((LEN, 128), F32)),
        [pltpu.VMEM((LEN, LANES), F32)],
        scalars=0,
    )
    now = scalars
    if plane:
        a0, b0 = call(
            arrived_kernel,
            (tie(scalars, q), *fetched),
            (sds((many, D // 2), BF16), sds((6 * few, D // 2), BF16)),
        )
        a1, b1 = along_wide(a0, 2), along_wide(b0, 4)
        now = tie(scalars, a0)
    piece = sds((BLOCK, 2 * COLS), BF16)
    c0, c1, c2, c3, lse = call(
        attend_kernel,
        (now, segments, segc, q, k, v),
        (piece, piece, piece, piece, sds((LEN, 128), F32)),
        [pltpu.VMEM((NARROW, BLOCK, 2 * COLS), BF16)],
    )
    context = (c0, *(along_narrow(c, k) for k, c in ((1, c1), (2, c2), (3, c3))))
    if plane:
        a_pair, b_pair = call(
            pairs_kernel,
            (tie(scalars, lse), a0, a1, b0, b1),
            (sds((2, many, D // 2), BF16), sds((2, 6 * few, D // 2), BF16)),
        )
        b_there = along_wide(b_pair, 2)
        (even,) = call(
            quads_kernel, (a_pair, along_wide(a_pair, 4)), (sds((4, many, D // 2), BF16),), scalars=0
        )
        odd = along_wide(even, 1)

    whole = sds((2 * BLOCK, D), F32)
    own = sds((BLOCK, D), F32)
    own_low = sds((BLOCK, D), BF16)
    res, normed_two, act, gb, branch, back, wo, cot = call(
        middle_kernel,
        (scalars, tokens, cotangent, *context, output_weight, b_pair, b_there, gain_two,
         w_in, down_weight),
        (own, sds((2 * BLOCK, D), BF16), sds((2 * BLOCK, hidden), BF16),
         sds((2 * BLOCK, 2 * hidden), BF16), whole, whole, sds((NARROW, COLS, D), BF16),
         sds((2 * BLOCK, D), BF16)),
    )
    part_act, part_gb = sds((BLOCK, hidden), BF16), sds((BLOCK, 2 * hidden), BF16)
    act_par, gb_par, out_send, send, other = call(
        partner_kernel,
        (scalars, normed_two, cot, branch, back, even, odd),
        (part_act, part_gb, own_low, own_low, sds((padded, D), BF16)),
    )
    recv = along_narrow(send, 1)
    half = -(-3 * hidden // 128) * 128
    out_keep, keep, ff_part = call(
        own_kernel,
        (scalars, normed_two, cot, branch, back, other, act, gb, act_par, gb_par),
        (own, own, sds((D, 2 * half), BF16)),
        [pltpu.VMEM((BLOCK, hidden), BF16), pltpu.VMEM((BLOCK, 2 * hidden), BF16)],
    )
    low_piece = sds((BLOCK // 2, 2 * COLS), BF16)
    back, low, gain_two_part, b0, b1, b2, b3 = call(
        residual_kernel,
        (keep, recv, res, gain_two, cot, wo),
        (own, own_low, sds((1, D), F32), low_piece, low_piece, low_piece, low_piece),
        scalars=0,
    )
    upstream = (b0, *(along_narrow(b, k) for k, b in ((1, b1), (2, b2), (3, b3))))
    grad_cols = 2 * half + NARROW * COLS
    even_part, odd_part = call(
        output_grad_kernel,
        (scalars, low, *context, ff_part),
        (sds((4, D // 8, grad_cols), BF16),) * 2,
        [pltpu.VMEM((D, NARROW * COLS), BF16)],
    )
    block = sds((rows_d, grad_cols), F32)
    if plane:
        block_low = sds((rows_d, grad_cols), BF16)
        grad_sum, *grad_sends = call(
            fold_kernel,
            (even_part, along_wide(odd_part, 1)),
            (block, block_low, block_low, block_low),
            scalars=0,
        )
        grad_recv = [along_wide(x, 2 * (i + 1)) for i, x in enumerate(grad_sends)]
        now = tie(scalars, *grad_sends)
    else:
        blocks = jnp.concatenate([even_part, odd_part], axis=0)
        grad_sum = sum_wide(blocks.reshape(size, rows_d, grad_cols))
        grad_recv = [jnp.zeros((rows_d, grad_cols), BF16)] * 3
        now = tie(scalars, even_part)

    rows_f32 = sds((LEN, LANES), F32)
    pair_qkv = sds((2 * BLOCK, 3 * COLS), BF16)
    n2, n3, qkv_far, back_rows, *grads = call(
        backward_far_kernel,
        (now, segments, segc, q, k, v, lse, trig, *upstream, w_qkv),
        (own, own_low, pair_qkv, wide_rows, rows_f32, rows_f32, rows_f32),
    )
    exchanged = along_narrow(n3, 1)
    n0, n1, qkv_near = call(
        backward_near_kernel,
        (scalars, segments, segc, q, k, v, lse, trig, back_rows, *grads, w_qkv),
        (own, own_low, pair_qkv),
        [pltpu.VMEM((LEN, LANES), F32)] * 3,
    )
    (qkv_part,) = call(
        qkv_grad_kernel,
        (tie(scalars, n1), normed_one, qkv_near, qkv_far, w_qkv, gain_one, gain_two_part),
        (sds((size, rows_d + GAIN_ROWS, 3 * COLS), BF16),),
        [pltpu.VMEM((D, 3 * COLS), BF16), pltpu.VMEM((LEN, D), BF16)],
    )
    near_recv = along_narrow(jnp.concatenate([n1, out_send], axis=0), 1)
    (pair_sum,) = call(add_kernel, (tie(n2, qkv_part), exchanged), (own_low,), scalars=0)
    far_recv = along_narrow(pair_sum, 2)
    qkv_grad, gains = call(
        qkv_sum_kernel,
        (lax.all_to_all(tie(qkv_part, pair_sum), "wide", 0, 0),),
        (sds((3, rows_d, COLS), F32), sds((2, D), F32)),
        scalars=0,
    )
    few_cols = sds((rows_d, COLS), BF16)
    grad_keep, *there = call(
        collect_kernel,
        (tie(grad_sum, near_recv, pair_sum), *grad_recv),
        (sds((rows_d, half + COLS), F32), few_cols, sds((rows_d, half + COLS), BF16), few_cols),
        scalars=0,
    )
    there = [along_narrow(x, k) for k, x in zip((1, 2, 3), there)]
    geglu_grad, down_grad, out_grad = call(
        finish_kernel,
        (grad_keep, *there),
        (sds((2, rows_d, hidden), F32), sds((hidden, rows_d), F32), sds((COLS, rows_d), F32)),
        [pltpu.VMEM((128, -(-hidden // 128) * 128), F32)],
        scalars=0,
    )
    (tokens_grad,) = call(
        final_kernel,
        (scalars, tokens, gain_one, back, n0, near_recv, far_recv),
        (own,),
    )
    gains = gains + along_narrow(gains, 1) + along_narrow(gains, 2) + along_narrow(gains, 3)
    layer_out = (out_keep + near_recv[BLOCK:].astype(F32)).astype(BF16)
    return (
        layer_out, tokens_grad, gains[0], qkv_grad, out_grad, gains[1], geglu_grad, down_grad,
    )


def solution(mesh):
    return jax.shard_map(
        per_device,
        mesh=mesh,
        in_specs=(
            P("wide", None),
            P("wide", None),
            P(),
            P(None, None, "narrow"),
            P("narrow", None),
            P(),
            P(None, None, "narrow"),
            P("narrow", None),
            P("wide", None),
        ),
        out_specs=(
            P(("wide", "narrow"), None),
            P(("wide", "narrow"), None),
            P(),
            P(None, "wide", "narrow"),
            P("narrow", "wide"),
            P(),
            P(None, "wide", "narrow"),
            P("narrow", "wide"),
        ),
        check_vma=False,
    )
```

```python
import functools
import math

import jax
import jax.numpy as jnp
import numpy as np
from jax import lax
from jax.experimental import pallas as pl
from jax.experimental.pallas import tpu as pltpu
from jax.sharding import PartitionSpec as P

HEAD = 64
LEN = 1024
D = 768
HEADS_HERE = 3
COLS = HEADS_HERE * HEAD
LANES = 256
DOC = 256
QB = 128
WINDOW = QB + 2 * DOC
EPSILON = 1e-05
ROPE_BASE = 160000.0
NARROW = 4
BLOCK = LEN // NARROW
F32 = jnp.float32
GAIN_ROWS = 16
BF16 = jnp.bfloat16
NEGATIVE = -1e30
MIB = 1024 * 1024
COST = {
    "finish_kernel": 1,
    "qkv_sum_kernel": 1,
    "pack_kernel": 1,
    "arrived_kernel": 1,
    "pair_kernel": 1,
    "begin_kernel": 10000,
    "project_kernel": 6,
    "attend_kernel": 10000,
    "middle_kernel": 10000,
    "partner_kernel": 3,
    "own_kernel": 10,
    "residual_kernel": 10000,
    "output_grad_kernel": 2,
    "fold_kernel": 2,
    "backward_far_kernel": 10000,
    "backward_near_kernel": 10000,
    "add_kernel": 10000,
    "qkv_grad_kernel": 1,
    "collect_kernel": 1,
    "final_kernel": 10000,
}

NN = (((1,), (0,)), ((), ()))
NT = (((1,), (1,)), ((), ()))
TN = (((0,), (0,)), ((), ()))


def dot(a, b, dims=NN):
    return lax.dot_general(a, b, dims, preferred_element_type=F32)


def call(body, ins, outs, scratch=(), scalars=1):
    name = getattr(body, "func", body).__name__
    specs = [pl.BlockSpec(memory_space=pltpu.SMEM)] * scalars
    specs += [pl.BlockSpec(memory_space=pltpu.VMEM)] * (len(ins) - scalars)
    size = sum(math.prod(x.shape) * x.dtype.itemsize for x in (*ins, *outs))
    held = sum(math.prod(x.shape) * x.dtype.itemsize for x in scratch)
    return pl.pallas_call(
        body,
        name=name,
        out_shape=tuple(jax.ShapeDtypeStruct(o.shape, o.dtype) for o in outs),
        in_specs=specs,
        out_specs=tuple(pl.BlockSpec(memory_space=pltpu.VMEM) for _ in outs),
        scratch_shapes=list(scratch),
        compiler_params=pltpu.CompilerParams(vmem_limit_bytes=size + size // 4 + held + 8 * MIB),
        cost_estimate=pl.CostEstimate(flops=COST[name] * 10**9, bytes_accessed=size, transcendentals=0),
    )(*ins)


def sds(shape, dtype):
    return jax.ShapeDtypeStruct(shape, dtype)


def rotary_table():
    position = np.arange(DOC, dtype=np.float64)
    frequency = ROPE_BASE ** (-2.0 * np.arange(HEAD // 2, dtype=np.float64) / HEAD)
    angle = position[:, None] * frequency[None, :]
    cosine, sine = np.cos(angle), np.sin(angle)
    table = np.zeros((DOC, 2 * LANES), np.float32)
    for h in range(HEADS_HERE):
        base = h * HEAD
        table[:, base : base + 32] = cosine
        table[:, base + 32 : base + 64] = cosine
        table[:, LANES + base : LANES + base + 32] = -sine
        table[:, LANES + base + 32 : LANES + base + 64] = sine
    high = table.astype(jnp.bfloat16)
    low = (table - high.astype(np.float32)).astype(jnp.bfloat16)
    return np.stack([high, low])


def normalize(values):
    centre = values - jnp.mean(values, axis=-1, keepdims=True)
    spread = jnp.mean(centre * centre, axis=-1, keepdims=True)
    inverse = lax.rsqrt(spread + EPSILON)
    return centre * inverse, inverse


def norm_back(upstream, unit_rows, inverse, gain):
    scaled = upstream * gain
    first_mean = jnp.mean(scaled, axis=-1, keepdims=True)
    second_mean = jnp.mean(scaled * unit_rows, axis=-1, keepdims=True)
    return inverse * (scaled - first_mean - unit_rows * second_mean)


def lane_head(rows):
    return lax.broadcasted_iota(jnp.int32, (rows, LANES), 1) // HEAD


def swap_halves(x):
    lane = lax.broadcasted_iota(jnp.int32, x.shape, 1)
    return jnp.where(
        lane % HEAD < HEAD // 2,
        pltpu.roll(x, LANES - HEAD // 2, 1),
        pltpu.roll(x, HEAD // 2, 1),
    )


def by_head(block, head):
    return jnp.concatenate(
        [jnp.where(head == h, block, jnp.zeros_like(block)) for h in range(HEADS_HERE)], axis=0
    )


def merge_heads(stacked, head):
    parts = jnp.split(stacked, HEADS_HERE, axis=0)
    return jnp.where(head == 0, parts[0], jnp.where(head == 1, parts[1], parts[2]))


def own_window(i):
    return jnp.clip(i - DOC // QB, 0, (LEN - WINDOW) // QB) * QB


def static_window(i):
    reach = DOC // QB
    return max(0, i - reach) * QB, min(LEN // QB, i + reach + 1) * QB


def project_kernel(
    tok_ref, seg_ref, gain_ref, w_ref, table_ref,
    q_ref, k_ref, v_ref, normed_ref, trig_ref, segc_ref,
    proj_ref,
):
    seg = jnp.broadcast_to(seg_ref[...].astype(F32), (8, LEN))
    index = lax.broadcasted_iota(jnp.int32, (8, LEN), 1)
    first = jnp.where(seg != pltpu.roll(seg, 1, 1), index, 0)
    first = jnp.where(index == 0, 0, first).astype(F32)
    shift = 1
    while shift < DOC:
        first = jnp.maximum(first, jnp.where(index >= shift, pltpu.roll(first, shift, 1), 0.0))
        shift *= 2
    place = index.astype(F32) - first
    segc_ref[...] = jnp.transpose(jnp.broadcast_to(seg[:1], (128, LEN)))
    placec = jnp.transpose(jnp.broadcast_to(place[:1], (128, LEN)))
    lane = lax.broadcasted_iota(jnp.int32, (LEN, 128), 1).astype(F32)
    hot = jnp.concatenate(
        [jnp.where(placec == lane + 128.0 * j, 1.0, 0.0) for j in range(DOC // 128)], axis=1
    ).astype(BF16)
    trig_ref[...] = dot(hot, table_ref[0]) + dot(hot, table_ref[1])

    def norm_rows(i, carry):
        rows = pl.ds(pl.multiple_of(i * 128, 128), 128)
        unit, _ = normalize(tok_ref[rows, :].astype(F32))
        normed_ref[rows, :] = (unit * gain_ref[...]).astype(BF16)
        return carry

    lax.fori_loop(0, LEN // 128, norm_rows, 0)
    proj_ref[:, COLS:] = jnp.zeros((LEN, LANES - COLS), F32)
    for s, out in enumerate((q_ref, k_ref)):
        proj_ref[:, :COLS] = dot(normed_ref[...], w_ref[s], NT)
        x = proj_ref[...]
        out[...] = (x * trig_ref[:, :LANES] + swap_halves(x) * trig_ref[:, LANES:]).astype(BF16)
    proj_ref[:, :COLS] = dot(normed_ref[...], w_ref[2], NT)
    v_ref[...] = proj_ref[...].astype(BF16)


def attend_kernel(
    s_ref, seg_ref, segc_ref, q_ref, k_ref, v_ref, c0_ref, c1_ref, c2_ref, c3_ref, lse_ref, ctx_ref
):
    z = s_ref[0]
    head = lane_head(QB)
    column = lax.broadcasted_iota(jnp.int32, (QB, 128), 1)
    for i in range(LEN // QB):
        low, high = static_window(i)
        rows = slice(i * QB, (i + 1) * QB)
        stacked = by_head(q_ref[rows, :] * jnp.asarray(1.0 / math.sqrt(HEAD), BF16), head)
        scores = dot(stacked, k_ref[low:high, :], NT)
        same = segc_ref[rows, 0:1] == seg_ref[0:1, low:high].astype(F32)
        parts, logs = [], []
        for h in range(HEADS_HERE):
            mine = jnp.where(same, scores[h * QB : (h + 1) * QB], NEGATIVE)
            top = jnp.max(mine, axis=-1, keepdims=True)
            weights = jnp.exp(mine - top)
            total = jnp.sum(weights, axis=-1, keepdims=True)
            parts.append((weights * (1.0 / total)).astype(BF16))
            logs.append(top + jnp.log(total))
        lse_ref[rows, :] = jnp.where(column == 0, logs[0], jnp.where(column == 1, logs[1], logs[2]))
        mixed = dot(jnp.concatenate(parts, axis=0), v_ref[low:high, :])
        context = merge_heads(mixed, head)[:, :COLS].astype(BF16)
        block, r = i * QB // BLOCK, i * QB % BLOCK
        ctx_ref[block, r : r + QB, :COLS] = context
        ctx_ref[block ^ 1, r : r + QB, COLS:] = context
    for k, out in enumerate((c0_ref, c1_ref, c2_ref, c3_ref)):
        out[...] = ctx_ref[z ^ k]


def place_slots(s_ref, refs, out_ref):
    rows, cols = refs[0].shape[1:]
    for group, ref in enumerate(refs):
        for i in range(2):
            slot = s_ref[2 + 4 * (group // 2) + 2 * i + group % 2]
            there = pl.ds(pl.multiple_of((slot // 2) * rows, 16), rows)
            out_ref[there, pl.ds(pl.multiple_of((slot % 2) * cols, 128), cols)] = ref[i]


def gated(normed, act_back, w_in, w_down, act_ref, gb_ref, width):
    both = dot(normed, w_in, NT)
    gate, linear = both[:, :width], both[:, width:]
    cdf = 0.5 * (1.0 + lax.erf(gate * math.sqrt(0.5)))
    slope = cdf + gate * (jnp.exp(-0.5 * gate * gate) * (1.0 / math.sqrt(2.0 * math.pi)))
    gelu = gate * cdf
    act_ref[...] = (gelu * linear).astype(BF16)
    gb_ref[:, :width] = (act_back * linear * slope).astype(BF16)
    gb_ref[:, width:] = (act_back * gelu).astype(BF16)
    return dot(act_ref[...], w_down), dot(gb_ref[...], w_in)


def begin_kernel(
    s_ref, tok_ref, cot_ref, c0, c1, c2, c3, w_ref, dw_ref, res_ref, context_ref, cot_out, back_ref
):
    z = s_ref[0]
    for half in range(2):
        base = (z if half == 0 else z ^ 1) * BLOCK
        there = pl.ds(pl.multiple_of(base, BLOCK), BLOCK)
        rows = slice(half * BLOCK, (half + 1) * BLOCK)
        mine = slice(half * COLS, (half + 1) * COLS)
        res_ref[rows, :] = tok_ref[there, :].astype(F32) + dot(c0[:, mine], w_ref[...])
        for k, c in enumerate((c1, c2, c3)):
            context_ref[k, rows, :] = c[:, mine]
        cot_out[rows, :] = cot_ref[there, :]
    back_ref[...] = dot(cot_out[...], dw_ref[...], NT)


def middle_kernel(
    s_ref, part_ref, context_ref, cot_ref, act_back_ref, w_ref, here_ref, there_ref, gain_ref, gw_ref, dw_ref,
    res_ref, normed_ref, act_ref, gb_ref, branch_ref, back_ref, wo_ref,
):
    wo_ref[0] = w_ref[...]
    few = COLS // 4
    pieces = ((0, here_ref, 0), (1, here_ref, 1), (2, there_ref, 0), (3, there_ref, 1))
    for slot, ref, i in pieces:
        there = pl.ds(pl.multiple_of(s_ref[10 + slot] * few, 16), few)
        for k in range(3):
            for side in range(2):
                first = (2 * k + side) * few
                lanes = slice(side * (D // 2), (side + 1) * (D // 2))
                wo_ref[k + 1, there, lanes] = ref[i, first : first + few, :]
    residual = part_ref[...]
    for k in range(3):
        residual += dot(context_ref[k], wo_ref[k + 1])
    res_ref[...] = residual[:BLOCK]
    branch_ref[:BLOCK, :] = residual[:BLOCK]
    branch_ref[BLOCK:, :] = jnp.zeros((BLOCK, D), F32)
    unit, _ = normalize(residual)
    normed_ref[...] = (unit * gain_ref[...]).astype(BF16)
    branch, back = gated(
        normed_ref[...], act_back_ref[...], gw_ref[...], dw_ref[...], act_ref, gb_ref, dw_ref.shape[0]
    )
    branch_ref[...] += branch
    back_ref[...] = back


def partner_kernel(
    s_ref, normed_ref, cot_ref, branch_in, back_in, f0, f1, f2, f3,
    act_ref, gb_ref, branch_ref, back_ref, other_ref,
):
    width = act_ref.shape[1]
    place_slots(s_ref, (f0, f1, f2, f3), other_ref)
    branch, back = gated(
        normed_ref[BLOCK:, :], dot(cot_ref[BLOCK:, :], other_ref[2 * width : 3 * width, :], NT), other_ref[: 2 * width, :],
        other_ref[2 * width : 3 * width, :], act_ref, gb_ref, width,
    )
    branch_ref[...] = (branch_in[BLOCK:, :] + branch).astype(BF16)
    back_ref[...] = (back_in[BLOCK:, :] + back).astype(BF16)


def own_kernel(
    s_ref, normed_ref, cot_ref, branch_in, back_in, other_ref, act_ref, gb_ref, act_par, gb_par,
    branch_ref, back_ref, whole_ref,
    act_own, gb_own,
):
    width = act_ref.shape[1]
    branch, back = gated(
        normed_ref[:BLOCK, :], dot(cot_ref[:BLOCK, :], other_ref[2 * width : 3 * width, :], NT), other_ref[: 2 * width, :],
        other_ref[2 * width : 3 * width, :], act_own, gb_own, width,
    )
    branch_ref[...] = branch_in[:BLOCK, :] + branch
    back_ref[...] = back_in[:BLOCK, :] + back
    half = whole_ref.shape[1] // 2
    whole_ref[:, : 2 * width] = dot(normed_ref[...], gb_ref[...], TN).astype(BF16)
    whole_ref[:, 2 * width : 3 * width] = dot(cot_ref[...], act_ref[...], TN).astype(BF16)
    part = dot(normed_ref[:BLOCK, :], gb_own[...], TN) + dot(normed_ref[BLOCK:, :], gb_par[...], TN)
    whole_ref[:, half : half + 2 * width] = part.astype(BF16)
    part = dot(cot_ref[:BLOCK, :], act_own[...], TN) + dot(cot_ref[BLOCK:, :], act_par[...], TN)
    whole_ref[:, half + 2 * width : half + 3 * width] = part.astype(BF16)
    pad = jnp.zeros((D, half - 3 * width), BF16)
    whole_ref[:, 3 * width : half] = pad
    whole_ref[:, half + 3 * width :] = pad


def finish_kernel(keep_ref, r1, r2, r3, geglu_ref, down_ref, out_ref, pad_ref):
    half = r2.shape[1] - COLS
    rows, width = geglu_ref.shape[1:]
    ff = keep_ref[:, :half] + r2[:, :half].astype(F32)
    geglu_ref[0] = ff[:, :width]
    geglu_ref[1] = ff[:, width : 2 * width]
    out = keep_ref[:, half:] + r1[...].astype(F32) + r2[:, half:].astype(F32) + r3[...].astype(F32)
    pad_ref[...] = jnp.zeros_like(pad_ref)
    pad_ref[:rows, :width] = ff[:, 2 * width : 3 * width]
    down_ref[...] = jnp.transpose(pad_ref[...])[:width, :rows]
    pad_ref[:rows, :COLS] = out
    out_ref[...] = jnp.transpose(pad_ref[...])[:COLS, :rows]


def qkv_sum_kernel(parts_ref, grad_ref, gains_ref):
    rows = grad_ref.shape[1]
    total = jnp.sum(parts_ref[...].astype(F32), axis=0)
    for s in range(3):
        grad_ref[s] = total[:rows, s * COLS : (s + 1) * COLS]
    for gain in range(2):
        for side in range(2):
            first = rows + 6 * gain + side
            part = total[first : first + 1] + total[first + 2 : first + 3] + total[first + 4 : first + 5]
            gains_ref[gain : gain + 1, side * (D // 2) : (side + 1) * (D // 2)] = part[:, : D // 2]


def residual_kernel(
    keep_ref, recv_ref, res_ref, gain_ref, cot_ref, wo_ref,
    back_ref, low_ref, gain_out, b0, b1, b2, b3,
):
    unit, inverse = normalize(res_ref[...])
    upstream = keep_ref[...] + recv_ref[...].astype(F32)
    back = cot_ref[:BLOCK, :].astype(F32) + norm_back(upstream, unit, inverse, gain_ref[...])
    back_ref[...] = back
    gain_out[...] = jnp.sum(upstream * unit, axis=0, keepdims=True)
    low = back.astype(BF16)
    low_ref[...] = low
    for k, out in enumerate((b0, b1, b2, b3)):
        part = dot(low, wo_ref[k], NT).astype(BF16)
        out[:, :COLS] = part[: BLOCK // 2]
        out[:, COLS:] = part[BLOCK // 2 :]


def output_grad_kernel(s_ref, low_ref, c0, c1, c2, c3, ff_ref, even_ref, odd_ref, whole_ref):
    for k, c in enumerate((c0, c1, c2, c3)):
        whole_ref[:, k * COLS : (k + 1) * COLS] = dot(low_ref[...], c[:, :COLS], TN).astype(BF16)
    rows, ff = even_ref.shape[1], ff_ref.shape[1]
    for i in range(8):
        there = pl.ds(pl.multiple_of(s_ref[2 + i] * rows, 16), rows)
        out = even_ref.at[i] if i < 4 else odd_ref.at[i - 4]
        out[:, :ff] = ff_ref[there, :]
        out[:, ff:] = whole_ref[there, :]


def collect_kernel(own_ref, r1, r2, r3, keep_ref, s1, s2, s3):
    total = own_ref[...] + r1[...].astype(F32) + r2[...].astype(F32) + r3[...].astype(F32)
    half = keep_ref.shape[1] - COLS
    keep_ref[:, :half] = total[:, :half]
    keep_ref[:, half:] = total[:, 2 * half : 2 * half + COLS]
    s2[:, :half] = total[:, half : 2 * half].astype(BF16)
    for k, out in ((1, s1), (2, s2), (3, s3)):
        first = 2 * half + k * COLS
        out[:, out.shape[1] - COLS :] = total[:, first : first + COLS].astype(BF16)


def pack_kernel(s_ref, w_in_ref, w_down_ref, w_out_ref, out_ref, ff_ref, whole_ref):
    slot = s_ref[1]
    there, cols = slot // 2, pl.ds(pl.multiple_of((slot % 2) * (D // 2), 128), D // 2)
    n_in, n_down = w_in_ref.shape[0], w_down_ref.shape[0]
    whole_ref[:n_in, :] = w_in_ref[...]
    whole_ref[n_in : n_in + n_down, :] = w_down_ref[...]
    whole_ref[n_in + n_down :, :] = jnp.zeros((whole_ref.shape[0] - n_in - n_down, D), BF16)
    rows = whole_ref.shape[0] // 4
    few = w_out_ref.shape[0] // 4
    here = pl.ds(pl.multiple_of(slot % 4 * few, 16), few)
    ff_ref[...] = whole_ref[pl.ds(pl.multiple_of(there * rows, 16), rows), cols]
    for side in range(2):
        mine = w_out_ref[here, side * (D // 2) : (side + 1) * (D // 2)]
        out_ref[side * few : (side + 1) * few, :] = mine


def arrived_kernel(s_ref, f1, f2, f3, out_ref):
    few = f1.shape[0]
    for i, piece in enumerate((f1, f2, f3)):
        out_ref[i * few : (i + 1) * few, :] = piece[...]


def pair_kernel(s_ref, a0, a1, out_ref):
    out_ref[0] = a0[...]
    out_ref[1] = a1[...]


def backward_steps(
    first, count, seg_ref, segc_ref, q_ref, k_ref, v_ref, lse_ref, back_ref, dq_ref, dk_ref, dv_ref
):
    head = lane_head(QB)
    scale = jnp.asarray(1.0 / math.sqrt(HEAD), BF16)
    for j in range(count):
        i = first + j
        rows = pl.ds(pl.multiple_of(i * QB, QB), QB)
        keys = pl.ds(pl.multiple_of(own_window(i), QB), WINDOW)
        stacked = by_head(q_ref[rows, :] * scale, head)
        upstream = by_head(back_ref[rows, :], head)
        scores = dot(stacked, k_ref[keys, :], NT)
        prob_back = dot(upstream, v_ref[keys, :], NT)
        same = segc_ref[rows, 0:1] == seg_ref[0:1, keys].astype(F32)
        probs, grads = [], []
        for h in range(HEADS_HERE):
            at = slice(h * QB, (h + 1) * QB)
            prob = jnp.exp(jnp.where(same, scores[at], NEGATIVE) - lse_ref[rows, h : h + 1])
            inner = jnp.sum(prob * prob_back[at], axis=-1, keepdims=True)
            probs.append(prob.astype(BF16))
            grads.append((prob * (prob_back[at] - inner)).astype(BF16))
        prob = jnp.concatenate(probs, axis=0)
        grad = jnp.concatenate(grads, axis=0)
        dv_ref[keys, :] += dot(prob, upstream, TN)
        dk_ref[keys, :] += dot(grad, stacked, TN)
        dq_ref[rows, :] = merge_heads(dot(grad, k_ref[keys, :]), head) * (1.0 / math.sqrt(HEAD))


def rows_back(base, dq_ref, dk_ref, dv_ref, trig_ref, w_ref, qkv_ref):
    rows = pl.ds(pl.multiple_of(base, BLOCK), BLOCK)
    cosine, signed = trig_ref[rows, :LANES], trig_ref[rows, LANES:]
    total = None
    for part, grad_ref in enumerate((dq_ref, dk_ref, dv_ref)):
        g = grad_ref[rows, :]
        if part < 2:
            g = g * cosine - swap_halves(g) * signed
        low = g[:, :COLS].astype(BF16)
        qkv_ref[:, part * COLS : (part + 1) * COLS] = low
        product = dot(low, w_ref[part])
        total = product if total is None else total + product
    return total


def backward_far_kernel(
    s_ref, seg_ref, segc_ref, q_ref, k_ref, v_ref, lse_ref, trig_ref, b0, b1, b2, b3, w_ref,
    n2, n3, qkv_ref, back_ref, dq_ref, dk_ref, dv_ref,
):
    z = s_ref[0]
    pair = z // 2
    half = BLOCK // 2
    back_ref[:, COLS:] = jnp.zeros((LEN, LANES - COLS), BF16)
    for k, b in enumerate((b0, b1, b2, b3)):
        base = pl.multiple_of((z ^ k) * BLOCK, BLOCK)
        back_ref[pl.ds(base, half), :COLS] = b[:, :COLS]
        back_ref[pl.ds(pl.multiple_of(base + half, half), half), :COLS] = b[:, COLS:]
    dk_ref[...] = jnp.zeros_like(dk_ref)
    dv_ref[...] = jnp.zeros_like(dv_ref)
    refs = (seg_ref, segc_ref, q_ref, k_ref, v_ref, lse_ref, back_ref, dq_ref, dk_ref, dv_ref)
    steps = LEN // QB
    reach = DOC // QB
    backward_steps((1 - pair) * (steps // 2 - reach), steps // 2 + reach, *refs)
    for k, out in ((2, n2), (3, n3)):
        at = qkv_ref.at[(k - 2) * BLOCK : (k - 1) * BLOCK]
        part = rows_back((z ^ k) * BLOCK, dq_ref, dk_ref, dv_ref, trig_ref, w_ref, at)
        out[...] = part.astype(out.dtype)


def add_kernel(mine_ref, recv_ref, out_ref):
    out_ref[...] = (mine_ref[...] + recv_ref[...].astype(F32)).astype(out_ref.dtype)


def backward_near_kernel(
    s_ref, seg_ref, segc_ref, q_ref, k_ref, v_ref, lse_ref, trig_ref, back_ref, dq_in, dk_in, dv_in,
    w_ref, n0, n1, qkv_ref, dq_ref, dk_ref, dv_ref,
):
    z = s_ref[0]
    pair = z // 2
    dq_ref[...] = dq_in[...]
    dk_ref[...] = dk_in[...]
    dv_ref[...] = dv_in[...]
    refs = (seg_ref, segc_ref, q_ref, k_ref, v_ref, lse_ref, back_ref, dq_ref, dk_ref, dv_ref)
    steps = LEN // QB
    reach = DOC // QB
    backward_steps(pair * (steps // 2 + reach), steps // 2 - reach, *refs)
    for k, out in ((0, n0), (1, n1)):
        at = qkv_ref.at[k * BLOCK : (k + 1) * BLOCK]
        part = rows_back((z ^ k) * BLOCK, dq_ref, dk_ref, dv_ref, trig_ref, w_ref, at)
        out[...] = part.astype(out.dtype)


def qkv_grad_kernel(
    s_ref, normed_ref, near_ref, far_ref, w_ref, gain_ref, gain_two_ref, out_ref, whole_ref, rows_ref
):
    for k in range(NARROW):
        base = pl.multiple_of((s_ref[0] ^ k) * BLOCK, BLOCK)
        rows_ref[k * BLOCK : (k + 1) * BLOCK, :] = normed_ref[pl.ds(base, BLOCK), :]
    pair = 2 * BLOCK
    total = None
    for s in range(3):
        cols = slice(s * COLS, (s + 1) * COLS)
        part = dot(rows_ref[:pair, :], near_ref[:, cols], TN)
        part += dot(rows_ref[pair:, :], far_ref[:, cols], TN)
        whole_ref[:, cols] = part.astype(BF16)
        weighted = part * jnp.transpose(w_ref[s].astype(F32))
        total = weighted if total is None else total + weighted
    column = jnp.broadcast_to(jnp.sum(total, axis=1, keepdims=True), (D, 128))
    gains = (jnp.transpose(column)[:1, :] / gain_ref[...], gain_two_ref[...])
    extra = jnp.zeros((GAIN_ROWS, D // 2), F32)
    row = lax.broadcasted_iota(jnp.int32, extra.shape, 0)
    at = 0
    for gain in gains:
        rest = gain
        for _ in range(3):
            term = rest.astype(BF16).astype(F32)
            rest = rest - term
            for side in range(2):
                extra = jnp.where(row == at, term[:, side * (D // 2) : (side + 1) * (D // 2)], extra)
                at += 1
    blocks, rows, cols = out_ref.shape
    rows -= GAIN_ROWS
    for i in range(blocks):
        if rows % 16 == 0:
            out_ref[i, :rows, :] = whole_ref[i * rows : (i + 1) * rows, :]
            out_ref[i, rows:, :] = jnp.zeros((GAIN_ROWS, cols), BF16)
            out_ref[i, rows:, : D // 2] = extra.astype(BF16)
        else:
            lines = [whole_ref[i * rows : (i + 1) * rows, :].astype(F32)]
            pad = jnp.zeros((GAIN_ROWS, cols - D // 2), F32)
            lines.append(jnp.concatenate([extra, pad], axis=1))
            out_ref[i] = jnp.concatenate(lines, axis=0).astype(BF16)


def final_kernel(s_ref, tok_ref, gain_ref, back_ref, n0, n1, n2, out_ref):
    upstream = n0[...] + n1[...].astype(F32) + n2[...].astype(F32)
    rows = pl.ds(pl.multiple_of(s_ref[0] * BLOCK, BLOCK), BLOCK)
    unit, inverse = normalize(tok_ref[rows, :].astype(F32))
    out_ref[...] = back_ref[...] + norm_back(upstream, unit, inverse, gain_ref[...])


def fold_kernel(even_ref, recv_ref, own_ref, s1_ref, s2_ref, s3_ref):
    for i, out in enumerate((own_ref, s1_ref, s2_ref, s3_ref)):
        out[...] = (even_ref[i].astype(F32) + recv_ref[i].astype(F32)).astype(out.dtype)


def along_narrow(x, k):
    return lax.ppermute(x, "narrow", [(i, i ^ k) for i in range(NARROW)])


def along_wide(x, k):
    return lax.ppermute(x, "wide", [(i, i ^ k) for i in range(lax.axis_size("wide"))])


def tie(x, *others):
    return lax.optimization_barrier((x, *others))[0]


def quarter_slice(x, slot):
    rows, cols = x.shape[-2] // 4, x.shape[-1] // 2
    x = lax.dynamic_slice_in_dim(x, (slot // 2) * rows, rows, x.ndim - 2)
    return lax.dynamic_slice_in_dim(x, (slot % 2) * cols, cols, x.ndim - 1)


def all_slots(x, hops):
    whole = jnp.stack([along_narrow(x, k) for k in hops])
    slots = jnp.stack([quarter_slice(whole, i) for i in range(8)])
    return slots[:4], slots[4:]


def sum_wide(x):
    return jnp.sum(lax.all_to_all(x, "wide", 0, 0).astype(F32), axis=0)


def per_device(
    tokens, segments, first_gain, qkv_weight, output_weight, second_gain, geglu_weight, down_weight,
    cotangent,
):
    size = lax.axis_size("wide")
    plane = size == 8
    mine = lax.axis_index("wide").astype(jnp.int32)
    z = lax.axis_index("narrow").astype(jnp.int32)
    order = jnp.asarray([0, 2, 4, 6, 1, 3, 5, 7], jnp.int32)
    slots = (mine ^ order) if plane else jnp.arange(8, dtype=jnp.int32)
    quarters = jnp.asarray([0, 2, 1, 3], jnp.int32)
    quarters = ((mine % 4) ^ quarters) if plane else jnp.arange(4, dtype=jnp.int32)
    scalars = jnp.concatenate([z[None], mine[None], slots, quarters])
    hidden = geglu_weight.shape[2]
    padded = -(-3 * hidden // 64) * 64
    rows_d = D // size
    gain_one = first_gain.reshape(1, D)
    gain_two = second_gain.reshape(1, D)
    w_qkv = qkv_weight.transpose(0, 2, 1)
    w_in = geglu_weight.transpose(0, 2, 1).reshape(2 * hidden, D)

    few, many = COLS // 4, padded // 4
    now = scalars
    if plane:
        slot_out, slot_ff = call(
            pack_kernel,
            (scalars, w_in, down_weight, output_weight),
            (sds((2 * few, D // 2), BF16), sds((many, D // 2), BF16)),
            [pltpu.VMEM((padded, D), BF16)],
        )
        out_fetched = [along_narrow(slot_out, k) for k in (1, 2, 3)]
        ff_fetched = along_narrow(slot_ff, 2)
    wide_rows = sds((LEN, LANES), BF16)
    q, k, v, normed_one, trig, segc = call(
        project_kernel,
        (tokens, segments, gain_one, w_qkv, jnp.asarray(rotary_table())),
        (wide_rows, wide_rows, wide_rows, sds((LEN, D), BF16), sds((LEN, 2 * LANES), F32),
         sds((LEN, 128), F32)),
        [pltpu.VMEM((LEN, LANES), F32)],
        scalars=0,
    )
    piece = sds((BLOCK, 2 * COLS), BF16)
    c0, c1, c2, c3, lse = call(
        attend_kernel,
        (now, segments, segc, q, k, v),
        (piece, piece, piece, piece, sds((LEN, 128), F32)),
        [pltpu.VMEM((NARROW, BLOCK, 2 * COLS), BF16)],
    )
    context = (c0, *(along_narrow(c, k) for k, c in ((1, c1), (2, c2), (3, c3))))
    if plane:
        ff0 = tie(ff_fetched, lse)
        slots_two = sds((2, many, D // 2), BF16)
        (out0,) = call(
            arrived_kernel, (tie(scalars, lse), *out_fetched), (sds((6 * few, D // 2), BF16),)
        )
        (out_here,) = call(
            pair_kernel, (scalars, out0, along_wide(out0, 2)), (sds((2, 6 * few, D // 2), BF16),)
        )
        out_there = along_wide(out_here, 1)
        (ff_pair,) = call(pair_kernel, (scalars, ff0, along_wide(ff0, 4)), (slots_two,))
        ff_x = along_wide(ff_pair, 2)
        ff_slots = (ff_pair, ff_x, along_wide(ff_pair, 1), along_wide(ff_x, 1))
    else:
        everything = jnp.concatenate(
            [w_in, down_weight, jnp.zeros((padded - 3 * hidden, D), BF16)], axis=0
        )
        even, odd = (x[:, 0] for x in all_slots(everything, (2,)))
        ff_slots = (even[::2], even[1::2], odd[::2], odd[1::2])
        others = jnp.stack([along_narrow(output_weight, k) for k in (1, 2, 3)])
        others = others.reshape(3, 4, few, 2, D // 2).transpose(1, 0, 3, 2, 4)
        others = others.reshape(4, 6 * few, D // 2)
        out_here, out_there = others[:2], others[2:]

    whole = sds((2 * BLOCK, D), F32)
    own = sds((BLOCK, D), F32)
    own_low = sds((BLOCK, D), BF16)
    part, contexts, cot, act_back = call(
        begin_kernel,
        (scalars, tokens, cotangent, *context, output_weight, down_weight),
        (whole, sds((3, 2 * BLOCK, COLS), BF16), sds((2 * BLOCK, D), BF16),
         sds((2 * BLOCK, hidden), F32)),
    )
    res, normed_two, act, gb, branch, back, wo = call(
        middle_kernel,
        (scalars, part, contexts, cot, act_back, output_weight, out_here, out_there, gain_two, w_in,
         down_weight),
        (own, sds((2 * BLOCK, D), BF16), sds((2 * BLOCK, hidden), BF16),
         sds((2 * BLOCK, 2 * hidden), BF16), whole, whole, sds((NARROW, COLS, D), BF16)),
    )
    part_act, part_gb = sds((BLOCK, hidden), BF16), sds((BLOCK, 2 * hidden), BF16)
    act_par, gb_par, out_send, send, other = call(
        partner_kernel,
        (scalars, normed_two, cot, branch, back, *ff_slots),
        (part_act, part_gb, own_low, own_low, sds((padded, D), BF16)),
    )
    recv = along_narrow(send, 1)
    half = -(-3 * hidden // 128) * 128
    out_keep, keep, ff_part = call(
        own_kernel,
        (scalars, normed_two, cot, branch, back, other, act, gb, act_par, gb_par),
        (own, own, sds((D, 2 * half), BF16)),
        [pltpu.VMEM((BLOCK, hidden), BF16), pltpu.VMEM((BLOCK, 2 * hidden), BF16)],
    )
    low_piece = sds((BLOCK // 2, 2 * COLS), BF16)
    back, low, gain_two_part, b0, b1, b2, b3 = call(
        residual_kernel,
        (keep, recv, res, gain_two, cot, wo),
        (own, own_low, sds((1, D), F32), low_piece, low_piece, low_piece, low_piece),
        scalars=0,
    )
    upstream = (b0, *(along_narrow(b, k) for k, b in ((1, b1), (2, b2), (3, b3))))
    grad_cols = 2 * half + NARROW * COLS
    even_part, odd_part = call(
        output_grad_kernel,
        (scalars, low, *context, ff_part),
        (sds((4, D // 8, grad_cols), BF16),) * 2,
        [pltpu.VMEM((D, NARROW * COLS), BF16)],
    )
    block = sds((rows_d, grad_cols), F32)
    if plane:
        block_low = sds((rows_d, grad_cols), BF16)
        grad_sum, *grad_sends = call(
            fold_kernel,
            (even_part, along_wide(odd_part, 1)),
            (block, block_low, block_low, block_low),
            scalars=0,
        )
        grad_recv = [along_wide(x, 2 * (i + 1)) for i, x in enumerate(grad_sends)]
        now = tie(scalars, *grad_sends)
    else:
        blocks = jnp.concatenate([even_part, odd_part], axis=0)
        grad_sum = sum_wide(blocks.reshape(size, rows_d, grad_cols))
        grad_recv, grad_sends = [jnp.zeros((rows_d, grad_cols), BF16)] * 3, ()
        now = tie(scalars, even_part)

    rows_f32 = sds((LEN, LANES), F32)
    pair_qkv = sds((2 * BLOCK, 3 * COLS), BF16)
    n2, n3, qkv_far, back_rows, *grads = call(
        backward_far_kernel,
        (now, segments, segc, q, k, v, lse, trig, *upstream, w_qkv),
        (own, own_low, pair_qkv, wide_rows, rows_f32, rows_f32, rows_f32),
    )
    exchanged = along_narrow(n3, 1)
    branch_recv = along_narrow(tie(out_send, upstream[1], *grad_sends), 1)
    n0, n1, qkv_near = call(
        backward_near_kernel,
        (scalars, segments, segc, q, k, v, lse, trig, back_rows, *grads, w_qkv),
        (own, own_low, pair_qkv),
        [pltpu.VMEM((LEN, LANES), F32)] * 3,
    )
    (qkv_part,) = call(
        qkv_grad_kernel,
        (tie(scalars, n1, branch_recv), normed_one, qkv_near, qkv_far, w_qkv, gain_one, gain_two_part),
        (sds((size, rows_d + GAIN_ROWS, 3 * COLS), BF16),),
        [pltpu.VMEM((D, 3 * COLS), BF16), pltpu.VMEM((LEN, D), BF16)],
    )
    near_recv = along_narrow(n1, 1)
    (pair_sum,) = call(add_kernel, (tie(n2, qkv_part), exchanged), (own_low,), scalars=0)
    far_recv = along_narrow(pair_sum, 2)
    qkv_grad, gains = call(
        qkv_sum_kernel,
        (lax.all_to_all(qkv_part, "wide", 0, 0),),
        (sds((3, rows_d, COLS), F32), sds((2, D), F32)),
        scalars=0,
    )
    few_cols = sds((rows_d, COLS), BF16)
    grad_keep, *there = call(
        collect_kernel,
        (tie(grad_sum, near_recv, pair_sum), *grad_recv),
        (sds((rows_d, half + COLS), F32), few_cols, sds((rows_d, half + COLS), BF16), few_cols),
        scalars=0,
    )
    there = [along_narrow(x, k) for k, x in zip((1, 2, 3), there)]
    (tokens_grad,) = call(
        final_kernel,
        (scalars, tokens, gain_one, back, n0, near_recv, far_recv),
        (own,),
    )
    gains = gains + along_narrow(gains, 1) + along_narrow(gains, 2) + along_narrow(gains, 3)
    geglu_grad, down_grad, out_grad = call(
        finish_kernel,
        (tie(grad_keep, tokens_grad), *there),
        (sds((2, rows_d, hidden), F32), sds((hidden, rows_d), F32), sds((COLS, rows_d), F32)),
        [pltpu.VMEM((128, -(-hidden // 128) * 128), F32)],
        scalars=0,
    )
    layer_out = (out_keep + branch_recv.astype(F32)).astype(BF16)
    return (
        layer_out, tokens_grad, gains[0], qkv_grad, out_grad, gains[1], geglu_grad, down_grad,
    )


def solution(mesh):
    return jax.shard_map(
        per_device,
        mesh=mesh,
        in_specs=(
            P("wide", None),
            P("wide", None),
            P(),
            P(None, None, "narrow"),
            P("narrow", None),
            P(),
            P(None, None, "narrow"),
            P("narrow", None),
            P("wide", None),
        ),
        out_specs=(
            P(("wide", "narrow"), None),
            P(("wide", "narrow"), None),
            P(),
            P(None, "wide", "narrow"),
            P("narrow", "wide"),
            P(),
            P(None, "wide", "narrow"),
            P("narrow", "wide"),
        ),
        check_vma=False,
    )
```

```python
import functools
import math

import jax
import jax.numpy as jnp
import numpy as np
from jax import lax
from jax.experimental import pallas as pl
from jax.experimental.pallas import tpu as pltpu
from jax.sharding import PartitionSpec as P

HEAD = 64
LEN = 1024
D = 768
HEADS_HERE = 3
COLS = HEADS_HERE * HEAD
LANES = 256
DOC = 256
QB = 128
WINDOW = QB + 2 * DOC
EPSILON = 1e-05
ROPE_BASE = 160000.0
NARROW = 4
BLOCK = LEN // NARROW
ORDER = (0, 2, 4, 6, 1, 3, 5, 7)
F32 = jnp.float32
GAIN_ROWS = 16
BF16 = jnp.bfloat16
NEGATIVE = -1e30
MIB = 1024 * 1024
COST = {
    "finish_kernel": 1,
    "qkv_sum_kernel": 1,
    "pack_kernel": 1,
    "arrived_kernel": 1,
    "pair_kernel": 1,
    "begin_kernel": 100,
    "project_kernel": 6,
    "attend_kernel": 100,
    "middle_kernel": 5,
    "partner_kernel": 3,
    "own_kernel": 10,
    "residual_kernel": 100,
    "output_grad_kernel": 2,
    "fold_kernel": 2,
    "backward_far_kernel": 100,
    "backward_near_kernel": 100,
    "add_kernel": 100,
    "qkv_grad_kernel": 1,
    "collect_kernel": 1,
    "final_kernel": 100,
}

NN = (((1,), (0,)), ((), ()))
NT = (((1,), (1,)), ((), ()))
TN = (((0,), (0,)), ((), ()))


def dot(a, b, dims=NN):
    return lax.dot_general(a, b, dims, preferred_element_type=F32)


def call(body, ins, outs, scratch=(), scalars=1):
    name = getattr(body, "func", body).__name__
    specs = [pl.BlockSpec(memory_space=pltpu.SMEM)] * scalars
    specs += [pl.BlockSpec(memory_space=pltpu.VMEM)] * (len(ins) - scalars)
    size = sum(math.prod(x.shape) * x.dtype.itemsize for x in (*ins, *outs))
    held = sum(math.prod(x.shape) * x.dtype.itemsize for x in scratch)
    return pl.pallas_call(
        body,
        name=name,
        out_shape=tuple(jax.ShapeDtypeStruct(o.shape, o.dtype) for o in outs),
        in_specs=specs,
        out_specs=tuple(pl.BlockSpec(memory_space=pltpu.VMEM) for _ in outs),
        scratch_shapes=list(scratch),
        compiler_params=pltpu.CompilerParams(vmem_limit_bytes=size + size // 4 + held + 8 * MIB),
        cost_estimate=pl.CostEstimate(flops=COST[name] * 10**9, bytes_accessed=size, transcendentals=0),
    )(*ins)


def sds(shape, dtype):
    return jax.ShapeDtypeStruct(shape, dtype)


def rotary_table():
    position = np.arange(DOC, dtype=np.float64)
    frequency = ROPE_BASE ** (-2.0 * np.arange(HEAD // 2, dtype=np.float64) / HEAD)
    angle = position[:, None] * frequency[None, :]
    cosine, sine = np.cos(angle), np.sin(angle)
    table = np.zeros((DOC, 2 * 128), np.float32)
    for h in range(2):
        base = h * HEAD
        table[:, base : base + 32] = cosine
        table[:, base + 32 : base + 64] = cosine
        table[:, 128 + base : 128 + base + 32] = -sine
        table[:, 128 + base + 32 : 128 + base + 64] = sine
    high = table.astype(jnp.bfloat16)
    low = (table - high.astype(np.float32)).astype(jnp.bfloat16)
    return np.stack([high, low])


def normalize(values):
    centre = values - jnp.mean(values, axis=-1, keepdims=True)
    spread = jnp.mean(centre * centre, axis=-1, keepdims=True)
    inverse = lax.rsqrt(spread + EPSILON)
    return centre * inverse, inverse


def norm_back(upstream, unit_rows, inverse, gain):
    scaled = upstream * gain
    first_mean = jnp.mean(scaled, axis=-1, keepdims=True)
    second_mean = jnp.mean(scaled * unit_rows, axis=-1, keepdims=True)
    return inverse * (scaled - first_mean - unit_rows * second_mean)


def lane_head(rows):
    return lax.broadcasted_iota(jnp.int32, (rows, LANES), 1) // HEAD


def swap_halves(x):
    lane = lax.broadcasted_iota(jnp.int32, x.shape, 1)
    return jnp.where(
        lane % HEAD < HEAD // 2,
        pltpu.roll(x, LANES - HEAD // 2, 1),
        pltpu.roll(x, HEAD // 2, 1),
    )


def turn(x, trig, sign):
    swapped = swap_halves(x)
    cosine, sine = trig[:, :128], sign * trig[:, 128:]
    parts = [
        x[:, i : i + 128] * cosine + swapped[:, i : i + 128] * sine for i in range(0, LANES, 128)
    ]
    return jnp.concatenate(parts, axis=1)


def by_head(block, head):
    return jnp.concatenate(
        [jnp.where(head == h, block, jnp.zeros_like(block)) for h in range(HEADS_HERE)], axis=0
    )


def merge_heads(stacked, head):
    parts = jnp.split(stacked, HEADS_HERE, axis=0)
    return jnp.where(head == 0, parts[0], jnp.where(head == 1, parts[1], parts[2]))


def static_window(i):
    reach = DOC // QB
    return max(0, i - reach) * QB, min(LEN // QB, i + reach + 1) * QB


def project_kernel(
    tok_ref, seg_ref, gain_ref, w_ref, table_ref,
    q_ref, k_ref, v_ref, normed_ref, trig_ref, segc_ref,
    proj_ref,
):
    seg = jnp.broadcast_to(seg_ref[...].astype(F32), (8, LEN))
    index = lax.broadcasted_iota(jnp.int32, (8, LEN), 1)
    first = jnp.where(seg != pltpu.roll(seg, 1, 1), index, 0)
    first = jnp.where(index == 0, 0, first).astype(F32)
    shift = 1
    while shift < DOC:
        first = jnp.maximum(first, jnp.where(index >= shift, pltpu.roll(first, shift, 1), 0.0))
        shift *= 2
    place = index.astype(F32) - first
    segc_ref[...] = jnp.transpose(jnp.broadcast_to(seg[:1], (128, LEN)))
    placec = jnp.transpose(jnp.broadcast_to(place[:1], (128, LEN)))
    lane = lax.broadcasted_iota(jnp.int32, (LEN, 128), 1).astype(F32)
    hot = jnp.concatenate(
        [jnp.where(placec == lane + 128.0 * j, 1.0, 0.0) for j in range(DOC // 128)], axis=1
    ).astype(BF16)
    trig_ref[...] = dot(hot, table_ref[0]) + dot(hot, table_ref[1])

    step = LEN // 4
    proj_ref[:, COLS:] = jnp.zeros((step, LANES - COLS), F32)
    for i in range(4):
        rows = slice(i * step, (i + 1) * step)
        unit, _ = normalize(tok_ref[rows, :].astype(F32))
        normed = (unit * gain_ref[...]).astype(BF16)
        normed_ref[rows, :] = normed
        for s, out in enumerate((q_ref, k_ref, v_ref)):
            proj_ref[:, :COLS] = dot(normed, w_ref[s], NT)
            x = proj_ref[...]
            out[rows, :] = (turn(x, trig_ref[rows, :], 1.0) if s < 2 else x).astype(BF16)


def attend_kernel(
    s_ref, seg_ref, segc_ref, q_ref, k_ref, v_ref, c0_ref, c1_ref, c2_ref, c3_ref, lse_ref, ctx_ref
):
    z = s_ref[0]
    head = lane_head(QB)
    column = lax.broadcasted_iota(jnp.int32, (QB, 128), 1)
    for i in range(LEN // QB):
        low, high = static_window(i)
        rows = slice(i * QB, (i + 1) * QB)
        stacked = by_head(q_ref[rows, :] * jnp.asarray(1.0 / math.sqrt(HEAD), BF16), head)
        scores = dot(stacked, k_ref[low:high, :], NT)
        same = segc_ref[rows, 0:1] == seg_ref[0:1, low:high].astype(F32)
        parts, logs = [], []
        for h in range(HEADS_HERE):
            mine = jnp.where(same, scores[h * QB : (h + 1) * QB], NEGATIVE)
            top = jnp.max(mine, axis=-1, keepdims=True)
            weights = jnp.exp(mine - top)
            total = jnp.sum(weights, axis=-1, keepdims=True)
            parts.append((weights * (1.0 / total)).astype(BF16))
            logs.append(top + jnp.log(total))
        lse_ref[rows, :] = jnp.where(column == 0, logs[0], jnp.where(column == 1, logs[1], logs[2]))
        mixed = dot(jnp.concatenate(parts, axis=0), v_ref[low:high, :])
        context = merge_heads(mixed, head)[:, :COLS].astype(BF16)
        block, r = i * QB // BLOCK, i * QB % BLOCK
        ctx_ref[block, r : r + QB, :COLS] = context
        ctx_ref[block ^ 1, r : r + QB, COLS:] = context
    for k, out in enumerate((c0_ref, c1_ref, c2_ref, c3_ref)):
        out[...] = ctx_ref[z ^ k]


def place_slots(s_ref, refs, out_ref):
    rows, cols = refs[0].shape[1:]
    for group, ref in enumerate(refs):
        for i in range(2):
            slot = s_ref[1] ^ ORDER[4 * (group // 2) + 2 * i + group % 2]
            there = pl.ds(pl.multiple_of((slot // 2) * rows, 16), rows)
            out_ref[there, pl.ds(pl.multiple_of((slot % 2) * cols, 128), cols)] = ref[i]


def gated(normed, act_back, w_in, w_down, act_ref, gb_ref, width):
    both = dot(normed, w_in, NT)
    gate, linear = both[:, :width], both[:, width:]
    cdf = 0.5 * (1.0 + lax.erf(gate * math.sqrt(0.5)))
    slope = cdf + gate * (jnp.exp(-0.5 * gate * gate) * (1.0 / math.sqrt(2.0 * math.pi)))
    gelu = gate * cdf
    act_ref[...] = (gelu * linear).astype(BF16)
    gb_ref[:, :width] = (act_back * linear * slope).astype(BF16)
    gb_ref[:, width:] = (act_back * gelu).astype(BF16)
    return dot(act_ref[...], w_down), dot(gb_ref[...], w_in)


def begin_kernel(
    s_ref, tok_ref, cot_ref, c0, c1, c2, c3, w_ref, dw_ref, res_ref, context_ref, cot_out, back_ref
):
    z = s_ref[0]
    for half in range(2):
        base = (z if half == 0 else z ^ 1) * BLOCK
        there = pl.ds(pl.multiple_of(base, BLOCK), BLOCK)
        rows = slice(half * BLOCK, (half + 1) * BLOCK)
        mine = slice(half * COLS, (half + 1) * COLS)
        res_ref[rows, :] = tok_ref[there, :].astype(F32) + dot(c0[:, mine], w_ref[...])
        for k, c in enumerate((c1, c2, c3)):
            context_ref[k, rows, :] = c[:, mine]
        cot_out[rows, :] = cot_ref[there, :]
    back_ref[...] = dot(cot_out[...], dw_ref[...], NT)


def middle_kernel(
    s_ref, part_ref, context_ref, cot_ref, act_back_ref, w_ref, here_ref, there_ref, gain_ref, gw_ref, dw_ref,
    res_ref, normed_ref, act_ref, gb_ref, branch_ref, back_ref, wo_ref,
):
    wo_ref[0] = w_ref[...]
    few = COLS // 4
    pieces = ((0, here_ref, 0), (2, here_ref, 1), (1, there_ref, 0), (3, there_ref, 1))
    for slot, ref, i in pieces:
        there = pl.ds(pl.multiple_of((s_ref[1] % 4 ^ slot) * few, 16), few)
        for k in range(3):
            for side in range(2):
                first = (2 * k + side) * few
                lanes = slice(side * (D // 2), (side + 1) * (D // 2))
                wo_ref[k + 1, there, lanes] = ref[i, first : first + few, :]
    residual = part_ref[...]
    for k in range(3):
        residual += dot(context_ref[k], wo_ref[k + 1])
    res_ref[...] = residual[:BLOCK]
    unit, _ = normalize(residual)
    normed_ref[...] = (unit * gain_ref[...]).astype(BF16)
    branch_ref[...], back_ref[...] = gated(
        normed_ref[BLOCK:, :], act_back_ref[BLOCK:, :], gw_ref[...], dw_ref[...], act_ref, gb_ref, dw_ref.shape[0]
    )


def partner_kernel(
    s_ref, normed_ref, cot_ref, branch_in, back_in, f0, f1, f2, f3,
    act_ref, gb_ref, branch_ref, back_ref, other_ref,
):
    width = act_ref.shape[1]
    place_slots(s_ref, (f0, f1, f2, f3), other_ref)
    branch, back = gated(
        normed_ref[BLOCK:, :], dot(cot_ref[BLOCK:, :], other_ref[2 * width : 3 * width, :], NT), other_ref[: 2 * width, :],
        other_ref[2 * width : 3 * width, :], act_ref, gb_ref, width,
    )
    branch_ref[...] = (branch_in[...] + branch).astype(BF16)
    back_ref[...] = (back_in[...] + back).astype(BF16)


def own_kernel(
    s_ref, normed_ref, cot_ref, act_back_ref, res_ref, gw_ref, dw_ref, other_ref,
    act_par, gb_par, act_par_two, gb_par_two,
    branch_ref, back_ref, whole_ref,
    act_one, gb_one, act_two, gb_two,
):
    width = act_par.shape[1]
    normed, cot = normed_ref[:BLOCK, :], cot_ref[:BLOCK, :]
    w_down = other_ref[2 * width : 3 * width, :]
    branch, back = gated(normed, act_back_ref[:BLOCK, :], gw_ref[...], dw_ref[...], act_one, gb_one, width)
    more, back_more = gated(normed, dot(cot, w_down, NT), other_ref[: 2 * width, :], w_down, act_two, gb_two, width)
    branch_ref[...] = res_ref[...] + branch + more
    back_ref[...] = back + back_more
    half = whole_ref.shape[1] // 2
    shards = ((act_one, gb_one, act_par, gb_par), (act_two, gb_two, act_par_two, gb_par_two))
    for shard, (act, gb, act_there, gb_there) in enumerate(shards):
        at = shard * half
        part = dot(normed, gb[...], TN) + dot(normed_ref[BLOCK:, :], gb_there[...], TN)
        whole_ref[:, at : at + 2 * width] = part.astype(BF16)
        part = dot(cot, act[...], TN) + dot(cot_ref[BLOCK:, :], act_there[...], TN)
        whole_ref[:, at + 2 * width : at + 3 * width] = part.astype(BF16)
        whole_ref[:, at + 3 * width : at + half] = jnp.zeros((D, half - 3 * width), BF16)


def finish_kernel(keep_ref, r1, r2, r3, geglu_ref, down_ref, out_ref, pad_ref):
    half = r2.shape[1] - COLS
    rows, width = geglu_ref.shape[1:]
    ff = keep_ref[:, :half] + r2[:, :half].astype(F32)
    geglu_ref[0] = ff[:, :width]
    geglu_ref[1] = ff[:, width : 2 * width]
    out = keep_ref[:, half:] + r1[...].astype(F32) + r2[:, half:].astype(F32) + r3[...].astype(F32)
    pad_ref[...] = jnp.zeros_like(pad_ref)
    pad_ref[:rows, :width] = ff[:, 2 * width : 3 * width]
    down_ref[...] = jnp.transpose(pad_ref[...])[:width, :rows]
    pad_ref[:rows, :COLS] = out
    out_ref[...] = jnp.transpose(pad_ref[...])[:COLS, :rows]


def qkv_sum_kernel(parts_ref, grad_ref, gains_ref):
    rows = grad_ref.shape[1]
    total = jnp.sum(parts_ref[...].astype(F32), axis=0)
    for s in range(3):
        grad_ref[s] = total[:rows, s * COLS : (s + 1) * COLS]
    for gain in range(2):
        for side in range(2):
            first = rows + 6 * gain + side
            part = total[first : first + 1] + total[first + 2 : first + 3] + total[first + 4 : first + 5]
            gains_ref[gain : gain + 1, side * (D // 2) : (side + 1) * (D // 2)] = part[:, : D // 2]


def residual_kernel(
    keep_ref, recv_ref, res_ref, gain_ref, cot_ref, wo_ref,
    back_ref, low_ref, gain_out, b0, b1, b2, b3,
):
    unit, inverse = normalize(res_ref[...])
    upstream = keep_ref[...] + recv_ref[...].astype(F32)
    back = cot_ref[:BLOCK, :].astype(F32) + norm_back(upstream, unit, inverse, gain_ref[...])
    back_ref[...] = back
    gain_out[...] = jnp.sum(upstream * unit, axis=0, keepdims=True)
    low = back.astype(BF16)
    low_ref[...] = low
    for k, out in enumerate((b0, b1, b2, b3)):
        part = dot(low, wo_ref[k], NT).astype(BF16)
        out[:, :COLS] = part[: BLOCK // 2]
        out[:, COLS:] = part[BLOCK // 2 :]


def output_grad_kernel(s_ref, low_ref, c0, c1, c2, c3, ff_ref, even_ref, odd_ref, whole_ref):
    for k, c in enumerate((c0, c1, c2, c3)):
        whole_ref[:, k * COLS : (k + 1) * COLS] = dot(low_ref[...], c[:, :COLS], TN).astype(BF16)
    rows, ff = even_ref.shape[1], ff_ref.shape[1]
    for i in range(8):
        there = pl.ds(pl.multiple_of((s_ref[1] ^ ORDER[i]) * rows, 16), rows)
        out = even_ref.at[i] if i < 4 else odd_ref.at[i - 4]
        out[:, :ff] = ff_ref[there, :]
        out[:, ff:] = whole_ref[there, :]


def collect_kernel(own_ref, r1, r2, r3, keep_ref, s1, s2, s3):
    total = own_ref[...] + r1[...].astype(F32) + r2[...].astype(F32) + r3[...].astype(F32)
    half = keep_ref.shape[1] - COLS
    keep_ref[:, :half] = total[:, :half]
    keep_ref[:, half:] = total[:, 2 * half : 2 * half + COLS]
    s2[:, :half] = total[:, half : 2 * half].astype(BF16)
    for k, out in ((1, s1), (2, s2), (3, s3)):
        first = 2 * half + k * COLS
        out[:, out.shape[1] - COLS :] = total[:, first : first + COLS].astype(BF16)


def pack_kernel(s_ref, w_in_ref, w_down_ref, w_out_ref, out_ref, ff_ref, whole_ref):
    slot = s_ref[1]
    there, cols = slot // 2, pl.ds(pl.multiple_of((slot % 2) * (D // 2), 128), D // 2)
    n_in, n_down = w_in_ref.shape[0], w_down_ref.shape[0]
    whole_ref[:n_in, :] = w_in_ref[...]
    whole_ref[n_in : n_in + n_down, :] = w_down_ref[...]
    whole_ref[n_in + n_down :, :] = jnp.zeros((whole_ref.shape[0] - n_in - n_down, D), BF16)
    rows = whole_ref.shape[0] // 4
    few = w_out_ref.shape[0] // 4
    here = pl.ds(pl.multiple_of(slot % 4 * few, 16), few)
    ff_ref[...] = whole_ref[pl.ds(pl.multiple_of(there * rows, 16), rows), cols]
    for side in range(2):
        mine = w_out_ref[here, side * (D // 2) : (side + 1) * (D // 2)]
        out_ref[side * few : (side + 1) * few, :] = mine


def arrived_kernel(s_ref, f1, f2, f3, out_ref):
    few = f1.shape[0]
    for i, piece in enumerate((f1, f2, f3)):
        out_ref[i * few : (i + 1) * few, :] = piece[...]


def pair_kernel(s_ref, a0, a1, out_ref):
    out_ref[0] = a0[...]
    out_ref[1] = a1[...]


def backward_steps(
    mirror, steps, seg_ref, segc_ref, q_ref, k_ref, v_ref, lse_ref, back_ref, dq_ref, dk_ref, dv_ref
):
    last = LEN // QB - 1
    head = lane_head(QB)
    scale = jnp.asarray(1.0 / math.sqrt(HEAD), BF16)
    for step in steps:
        low, high = static_window(step)
        i = jnp.where(mirror == 1, last - step, step)
        rows = pl.ds(pl.multiple_of(i * QB, QB), QB)
        keys = jnp.where(mirror == 1, LEN - high, low)
        keys = pl.ds(pl.multiple_of(keys, QB), high - low)
        stacked = by_head(q_ref[rows, :] * scale, head)
        upstream = by_head(back_ref[rows, :], head)
        scores = dot(stacked, k_ref[keys, :], NT)
        prob_back = dot(upstream, v_ref[keys, :], NT)
        same = segc_ref[rows, 0:1] == seg_ref[0:1, keys].astype(F32)
        probs, grads = [], []
        for h in range(HEADS_HERE):
            at = slice(h * QB, (h + 1) * QB)
            prob = jnp.exp(jnp.where(same, scores[at], NEGATIVE) - lse_ref[rows, h : h + 1])
            inner = jnp.sum(prob * prob_back[at], axis=-1, keepdims=True)
            probs.append(prob.astype(BF16))
            grads.append((prob * (prob_back[at] - inner)).astype(BF16))
        prob = jnp.concatenate(probs, axis=0)
        grad = jnp.concatenate(grads, axis=0)
        dv_ref[keys, :] += dot(prob, upstream, TN)
        dk_ref[keys, :] += dot(grad, stacked, TN)
        dq_ref[rows, :] = merge_heads(dot(grad, k_ref[keys, :]), head) * (1.0 / math.sqrt(HEAD))


def rows_back(base, dq_ref, dk_ref, dv_ref, trig_ref, w_ref, qkv_ref):
    rows = pl.ds(pl.multiple_of(base, BLOCK), BLOCK)
    trig = trig_ref[rows, :]
    total = None
    for part, grad_ref in enumerate((dq_ref, dk_ref, dv_ref)):
        g = grad_ref[rows, :]
        if part < 2:
            g = turn(g, trig, -1.0)
        low = g[:, :COLS].astype(BF16)
        qkv_ref[:, part * COLS : (part + 1) * COLS] = low
        product = dot(low, w_ref[part])
        total = product if total is None else total + product
    return total


def backward_far_kernel(
    s_ref, seg_ref, segc_ref, q_ref, k_ref, v_ref, lse_ref, trig_ref, b0, b1, b2, b3, w_ref,
    n2, n3, qkv_ref, back_ref, dq_ref, dk_ref, dv_ref,
):
    z = s_ref[0]
    pair = z // 2
    half = BLOCK // 2
    back_ref[:, COLS:] = jnp.zeros((LEN, LANES - COLS), BF16)
    for k, b in enumerate((b0, b1, b2, b3)):
        base = pl.multiple_of((z ^ k) * BLOCK, BLOCK)
        back_ref[pl.ds(base, half), :COLS] = b[:, :COLS]
        back_ref[pl.ds(pl.multiple_of(base + half, half), half), :COLS] = b[:, COLS:]
    dk_ref[...] = jnp.zeros_like(dk_ref)
    dv_ref[...] = jnp.zeros_like(dv_ref)
    refs = (seg_ref, segc_ref, q_ref, k_ref, v_ref, lse_ref, back_ref, dq_ref, dk_ref, dv_ref)
    steps = LEN // QB
    reach = DOC // QB
    backward_steps(1 - pair, range(steps // 2 + reach), *refs)
    for k, out in ((2, n2), (3, n3)):
        at = qkv_ref.at[(k - 2) * BLOCK : (k - 1) * BLOCK]
        part = rows_back((z ^ k) * BLOCK, dq_ref, dk_ref, dv_ref, trig_ref, w_ref, at)
        out[...] = part.astype(out.dtype)


def add_kernel(mine_ref, recv_ref, out_ref):
    out_ref[...] = (mine_ref[...] + recv_ref[...].astype(F32)).astype(out_ref.dtype)


def backward_near_kernel(
    s_ref, seg_ref, segc_ref, q_ref, k_ref, v_ref, lse_ref, trig_ref, back_ref, dq_in, dk_in, dv_in,
    w_ref, n0, n1, qkv_ref, dq_ref, dk_ref, dv_ref,
):
    z = s_ref[0]
    pair = z // 2
    dq_ref[...] = dq_in[...]
    dk_ref[...] = dk_in[...]
    dv_ref[...] = dv_in[...]
    refs = (seg_ref, segc_ref, q_ref, k_ref, v_ref, lse_ref, back_ref, dq_ref, dk_ref, dv_ref)
    steps = LEN // QB
    reach = DOC // QB
    backward_steps(pair, range(steps // 2 - reach), *refs)
    for k, out in ((0, n0), (1, n1)):
        at = qkv_ref.at[k * BLOCK : (k + 1) * BLOCK]
        part = rows_back((z ^ k) * BLOCK, dq_ref, dk_ref, dv_ref, trig_ref, w_ref, at)
        out[...] = part.astype(out.dtype)


def qkv_grad_kernel(
    s_ref, normed_ref, near_ref, far_ref, w_ref, gain_ref, gain_two_ref, out_ref, whole_ref, rows_ref
):
    for k in range(NARROW):
        base = pl.multiple_of((s_ref[0] ^ k) * BLOCK, BLOCK)
        rows_ref[k * BLOCK : (k + 1) * BLOCK, :] = normed_ref[pl.ds(base, BLOCK), :]
    pair = 2 * BLOCK
    total = None
    for s in range(3):
        cols = slice(s * COLS, (s + 1) * COLS)
        part = dot(rows_ref[:pair, :], near_ref[:, cols], TN)
        part += dot(rows_ref[pair:, :], far_ref[:, cols], TN)
        whole_ref[:, cols] = part.astype(BF16)
        weighted = part * jnp.transpose(w_ref[s].astype(F32))
        total = weighted if total is None else total + weighted
    column = jnp.broadcast_to(jnp.sum(total, axis=1, keepdims=True), (D, 128))
    gains = (jnp.transpose(column)[:1, :] / gain_ref[...], gain_two_ref[...])
    extra = jnp.zeros((GAIN_ROWS, D // 2), F32)
    row = lax.broadcasted_iota(jnp.int32, extra.shape, 0)
    at = 0
    for gain in gains:
        rest = gain
        for _ in range(3):
            term = rest.astype(BF16).astype(F32)
            rest = rest - term
            for side in range(2):
                extra = jnp.where(row == at, term[:, side * (D // 2) : (side + 1) * (D // 2)], extra)
                at += 1
    blocks, rows, cols = out_ref.shape
    rows -= GAIN_ROWS
    for i in range(blocks):
        if rows % 16 == 0:
            out_ref[i, :rows, :] = whole_ref[i * rows : (i + 1) * rows, :]
            out_ref[i, rows:, :] = jnp.zeros((GAIN_ROWS, cols), BF16)
            out_ref[i, rows:, : D // 2] = extra.astype(BF16)
        else:
            lines = [whole_ref[i * rows : (i + 1) * rows, :].astype(F32)]
            pad = jnp.zeros((GAIN_ROWS, cols - D // 2), F32)
            lines.append(jnp.concatenate([extra, pad], axis=1))
            out_ref[i] = jnp.concatenate(lines, axis=0).astype(BF16)


def final_kernel(s_ref, tok_ref, gain_ref, back_ref, n0, n1, n2, out_ref):
    upstream = n0[...] + n1[...].astype(F32) + n2[...].astype(F32)
    rows = pl.ds(pl.multiple_of(s_ref[0] * BLOCK, BLOCK), BLOCK)
    unit, inverse = normalize(tok_ref[rows, :].astype(F32))
    out_ref[...] = back_ref[...] + norm_back(upstream, unit, inverse, gain_ref[...])


def fold_kernel(even_ref, recv_ref, own_ref, s1_ref, s2_ref, s3_ref):
    for i, out in enumerate((own_ref, s1_ref, s2_ref, s3_ref)):
        out[...] = (even_ref[i].astype(F32) + recv_ref[i].astype(F32)).astype(out.dtype)


def along_narrow(x, k):
    return lax.ppermute(x, "narrow", [(i, i ^ k) for i in range(NARROW)])


def along_wide(x, k):
    return lax.ppermute(x, "wide", [(i, i ^ k) for i in range(lax.axis_size("wide"))])


def tie(x, *others):
    return lax.optimization_barrier((x, *others))[0]


def quarter_slice(x, slot):
    rows, cols = x.shape[-2] // 4, x.shape[-1] // 2
    x = lax.dynamic_slice_in_dim(x, (slot // 2) * rows, rows, x.ndim - 2)
    return lax.dynamic_slice_in_dim(x, (slot % 2) * cols, cols, x.ndim - 1)


def all_slots(x, hops):
    whole = jnp.stack([along_narrow(x, k) for k in hops])
    slots = jnp.stack([quarter_slice(whole, i) for i in ORDER])
    return slots[:4], slots[4:]


def sum_wide(x):
    return jnp.sum(lax.all_to_all(x, "wide", 0, 0).astype(F32), axis=0)


def per_device(
    tokens, segments, first_gain, qkv_weight, output_weight, second_gain, geglu_weight, down_weight,
    cotangent,
):
    size = lax.axis_size("wide")
    plane = size == 8
    mine = lax.axis_index("wide").astype(jnp.int32)
    z = lax.axis_index("narrow").astype(jnp.int32)
    scalars = jnp.stack([z, mine if plane else jnp.zeros_like(mine)])
    hidden = geglu_weight.shape[2]
    padded = -(-3 * hidden // 64) * 64
    rows_d = D // size
    gain_one = first_gain.reshape(1, D)
    gain_two = second_gain.reshape(1, D)
    w_qkv = qkv_weight.transpose(0, 2, 1)
    w_in = geglu_weight.transpose(0, 2, 1).reshape(2 * hidden, D)

    few, many = COLS // 4, padded // 4
    now = scalars
    if plane:
        slot_out, slot_ff = call(
            pack_kernel,
            (scalars, w_in, down_weight, output_weight),
            (sds((2 * few, D // 2), BF16), sds((many, D // 2), BF16)),
            [pltpu.VMEM((padded, D), BF16)],
        )
        out_fetched = [along_narrow(slot_out, k) for k in (1, 2, 3)]
        ff_fetched = along_narrow(slot_ff, 2)
    wide_rows = sds((LEN, LANES), BF16)
    q, k, v, normed_one, trig, segc = call(
        project_kernel,
        (tokens, segments, gain_one, w_qkv, jnp.asarray(rotary_table())),
        (wide_rows, wide_rows, wide_rows, sds((LEN, D), BF16), sds((LEN, 2 * 128), F32),
         sds((LEN, 128), F32)),
        [pltpu.VMEM((LEN // 4, LANES), F32)],
        scalars=0,
    )
    piece = sds((BLOCK, 2 * COLS), BF16)
    c0, c1, c2, c3, lse = call(
        attend_kernel,
        (now, segments, segc, q, k, v),
        (piece, piece, piece, piece, sds((LEN, 128), F32)),
        [pltpu.VMEM((NARROW, BLOCK, 2 * COLS), BF16)],
    )
    context = (c0, *(along_narrow(c, k) for k, c in ((1, c1), (2, c2), (3, c3))))
    if plane:
        ff0 = tie(ff_fetched, lse)
        slots_two = sds((2, many, D // 2), BF16)
        (out0,) = call(
            arrived_kernel, (tie(scalars, lse), *out_fetched), (sds((6 * few, D // 2), BF16),)
        )
        (out_here,) = call(
            pair_kernel, (scalars, out0, along_wide(out0, 2)), (sds((2, 6 * few, D // 2), BF16),)
        )
        out_there = along_wide(out_here, 1)
        (ff_pair,) = call(pair_kernel, (scalars, ff0, along_wide(ff0, 4)), (slots_two,))
        ff_x = along_wide(ff_pair, 2)
        ff_slots = (ff_pair, ff_x, along_wide(ff_pair, 1), along_wide(ff_x, 1))
    else:
        everything = jnp.concatenate(
            [w_in, down_weight, jnp.zeros((padded - 3 * hidden, D), BF16)], axis=0
        )
        even, odd = (x[:, 0] for x in all_slots(everything, (2,)))
        ff_slots = (even[::2], even[1::2], odd[::2], odd[1::2])
        others = jnp.stack([along_narrow(output_weight, k) for k in (1, 2, 3)])
        others = others.reshape(3, 4, few, 2, D // 2).transpose(1, 0, 3, 2, 4)
        others = others.reshape(4, 6 * few, D // 2)
        out_here, out_there = others[::2], others[1::2]

    whole = sds((2 * BLOCK, D), F32)
    own = sds((BLOCK, D), F32)
    own_low = sds((BLOCK, D), BF16)
    part, contexts, cot, act_back = call(
        begin_kernel,
        (scalars, tokens, cotangent, *context, output_weight, down_weight),
        (whole, sds((3, 2 * BLOCK, COLS), BF16), sds((2 * BLOCK, D), BF16),
         sds((2 * BLOCK, hidden), F32)),
    )
    part_act, part_gb = sds((BLOCK, hidden), BF16), sds((BLOCK, 2 * hidden), BF16)
    res, normed_two, act_par, gb_par, branch, back, wo = call(
        middle_kernel,
        (scalars, part, contexts, cot, act_back, output_weight, out_here, out_there, gain_two, w_in,
         down_weight),
        (own, sds((2 * BLOCK, D), BF16), part_act, part_gb, own, own, sds((NARROW, COLS, D), BF16)),
    )
    act_par_two, gb_par_two, out_send, send, other = call(
        partner_kernel,
        (scalars, normed_two, cot, branch, back, *ff_slots),
        (part_act, part_gb, own_low, own_low, sds((padded, D), BF16)),
    )
    recv = along_narrow(send, 1)
    half = -(-3 * hidden // 128) * 128
    out_keep, keep, ff_part = call(
        own_kernel,
        (scalars, normed_two, cot, act_back, res, w_in, down_weight, other, act_par, gb_par,
         act_par_two, gb_par_two),
        (own, own, sds((D, 2 * half), BF16)),
        [pltpu.VMEM((BLOCK, hidden), BF16), pltpu.VMEM((BLOCK, 2 * hidden), BF16)] * 2,
    )
    low_piece = sds((BLOCK // 2, 2 * COLS), BF16)
    back, low, gain_two_part, b0, b1, b2, b3 = call(
        residual_kernel,
        (keep, recv, res, gain_two, cot, wo),
        (own, own_low, sds((1, D), F32), low_piece, low_piece, low_piece, low_piece),
        scalars=0,
    )
    upstream = (b0, *(along_narrow(b, k) for k, b in ((1, b1), (2, b2), (3, b3))))
    grad_cols = 2 * half + NARROW * COLS
    even_part, odd_part = call(
        output_grad_kernel,
        (scalars, low, *context, ff_part),
        (sds((4, D // 8, grad_cols), BF16),) * 2,
        [pltpu.VMEM((D, NARROW * COLS), BF16)],
    )
    block = sds((rows_d, grad_cols), F32)
    if plane:
        block_low = sds((rows_d, grad_cols), BF16)
        grad_sum, *grad_sends = call(
            fold_kernel,
            (even_part, along_wide(odd_part, 1)),
            (block, block_low, block_low, block_low),
            scalars=0,
        )
        grad_recv = [along_wide(x, 2 * (i + 1)) for i, x in enumerate(grad_sends)]
        now = tie(scalars, *grad_sends)
    else:
        blocks = jnp.stack([even_part, odd_part], axis=1)
        grad_sum = sum_wide(blocks.reshape(size, rows_d, grad_cols))
        grad_recv, grad_sends = [jnp.zeros((rows_d, grad_cols), BF16)] * 3, ()
        now = tie(scalars, even_part)

    rows_f32 = sds((LEN, LANES), F32)
    pair_qkv = sds((2 * BLOCK, 3 * COLS), BF16)
    n2, n3, qkv_far, back_rows, *grads = call(
        backward_far_kernel,
        (now, segments, segc, q, k, v, lse, trig, *upstream, w_qkv),
        (own, own_low, pair_qkv, wide_rows, rows_f32, rows_f32, rows_f32),
    )
    exchanged = along_narrow(n3, 1)
    branch_recv = along_narrow(tie(out_send, upstream[1], *grad_sends), 1)
    n0, n1, qkv_near = call(
        backward_near_kernel,
        (scalars, segments, segc, q, k, v, lse, trig, back_rows, *grads, w_qkv),
        (own, own_low, pair_qkv),
        [pltpu.VMEM((LEN, LANES), F32)] * 3,
    )
    (qkv_part,) = call(
        qkv_grad_kernel,
        (tie(scalars, n1, branch_recv), normed_one, qkv_near, qkv_far, w_qkv, gain_one, gain_two_part),
        (sds((size, rows_d + GAIN_ROWS, 3 * COLS), BF16),),
        [pltpu.VMEM((D, 3 * COLS), BF16), pltpu.VMEM((LEN, D), BF16)],
    )
    near_recv = along_narrow(n1, 1)
    (pair_sum,) = call(add_kernel, (tie(n2, qkv_part), exchanged), (own_low,), scalars=0)
    far_recv = along_narrow(pair_sum, 2)
    qkv_grad, gains = call(
        qkv_sum_kernel,
        (lax.all_to_all(qkv_part, "wide", 0, 0),),
        (sds((3, rows_d, COLS), F32), sds((2, D), F32)),
        scalars=0,
    )
    few_cols = sds((rows_d, COLS), BF16)
    grad_keep, *there = call(
        collect_kernel,
        (tie(grad_sum, near_recv, pair_sum), *grad_recv),
        (sds((rows_d, half + COLS), F32), few_cols, sds((rows_d, half + COLS), BF16), few_cols),
        scalars=0,
    )
    there = [along_narrow(x, k) for k, x in zip((1, 2, 3), there)]
    (tokens_grad,) = call(
        final_kernel,
        (scalars, tokens, gain_one, back, n0, near_recv, far_recv),
        (own,),
    )
    gains = gains + along_narrow(gains, 1) + along_narrow(gains, 2) + along_narrow(gains, 3)
    geglu_grad, down_grad, out_grad = call(
        finish_kernel,
        (tie(grad_keep, tokens_grad), *there),
        (sds((2, rows_d, hidden), F32), sds((hidden, rows_d), F32), sds((COLS, rows_d), F32)),
        [pltpu.VMEM((128, -(-hidden // 128) * 128), F32)],
        scalars=0,
    )
    layer_out = (out_keep + branch_recv.astype(F32)).astype(BF16)
    return (
        layer_out, tokens_grad, gains[0], qkv_grad, out_grad, gains[1], geglu_grad, down_grad,
    )


def solution(mesh):
    return jax.shard_map(
        per_device,
        mesh=mesh,
        in_specs=(
            P("wide", None),
            P("wide", None),
            P(),
            P(None, None, "narrow"),
            P("narrow", None),
            P(),
            P(None, None, "narrow"),
            P("narrow", None),
            P("wide", None),
        ),
        out_specs=(
            P(("wide", "narrow"), None),
            P(("wide", "narrow"), None),
            P(),
            P(None, "wide", "narrow"),
            P("narrow", "wide"),
            P(),
            P(None, "wide", "narrow"),
            P("narrow", "wide"),
        ),
        check_vma=False,
    )
```

```python
import functools
import math

import jax
import jax.numpy as jnp
import numpy as np
from jax import lax
from jax.experimental import pallas as pl
from jax.experimental.pallas import tpu as pltpu
from jax.sharding import PartitionSpec as P

HEAD = 64
LEN = 1024
D = 768
HEADS_HERE = 3
COLS = HEADS_HERE * HEAD
LANES = 256
DOC = 256
QB = 128
PART = 32
WINDOW = QB + 2 * DOC
EPSILON = 1e-05
ROPE_BASE = 160000.0
NARROW = 4
BLOCK = LEN // NARROW
ORDER = (0, 2, 4, 6, 1, 3, 5, 7)
F32 = jnp.float32
GAIN_ROWS = 16
BF16 = jnp.bfloat16
NEGATIVE = -1e30
MIB = 1024 * 1024
COST = {
    "finish_kernel": 1,
    "qkv_sum_kernel": 1,
    "pack_kernel": 1,
    "arrived_kernel": 1,
    "pair_kernel": 1,
    "begin_kernel": 100,
    "project_kernel": 6,
    "attend_kernel": 100,
    "middle_kernel": 5,
    "partner_kernel": 3,
    "own_kernel": 10,
    "residual_kernel": 100,
    "output_grad_kernel": 2,
    "fold_kernel": 2,
    "backward_far_kernel": 100,
    "backward_near_kernel": 100,
    "add_kernel": 100,
    "qkv_grad_kernel": 1,
    "collect_kernel": 1,
    "final_kernel": 100,
}

NN = (((1,), (0,)), ((), ()))
NT = (((1,), (1,)), ((), ()))
TN = (((0,), (0,)), ((), ()))


def dot(a, b, dims=NN):
    return lax.dot_general(a, b, dims, preferred_element_type=F32)


def call(body, ins, outs, scratch=(), scalars=1, place=pltpu.VMEM):
    name = getattr(body, "func", body).__name__
    specs = [pl.BlockSpec(memory_space=pltpu.SMEM)] * scalars
    specs += [pl.BlockSpec(memory_space=place)] * (len(ins) - scalars)
    size = sum(math.prod(x.shape) * x.dtype.itemsize for x in (*ins, *outs))
    held = sum(math.prod(x.shape) * x.dtype.itemsize for x in scratch if hasattr(x.dtype, "itemsize"))
    return pl.pallas_call(
        body,
        name=name,
        out_shape=tuple(jax.ShapeDtypeStruct(o.shape, o.dtype) for o in outs),
        in_specs=specs,
        out_specs=tuple(pl.BlockSpec(memory_space=pltpu.VMEM) for _ in outs),
        scratch_shapes=list(scratch),
        compiler_params=pltpu.CompilerParams(vmem_limit_bytes=size + size // 4 + held + 8 * MIB),
        cost_estimate=pl.CostEstimate(flops=COST[name] * 10**9, bytes_accessed=size, transcendentals=0),
    )(*ins)


def sds(shape, dtype):
    return jax.ShapeDtypeStruct(shape, dtype)


def rotary_table():
    position = np.arange(DOC, dtype=np.float64)
    frequency = ROPE_BASE ** (-2.0 * np.arange(HEAD // 2, dtype=np.float64) / HEAD)
    angle = position[:, None] * frequency[None, :]
    cosine, sine = np.cos(angle), np.sin(angle)
    table = np.zeros((DOC, 2 * 128), np.float32)
    for h in range(2):
        base = h * HEAD
        table[:, base : base + 32] = cosine
        table[:, base + 32 : base + 64] = cosine
        table[:, 128 + base : 128 + base + 32] = -sine
        table[:, 128 + base + 32 : 128 + base + 64] = sine
    high = table.astype(jnp.bfloat16)
    low = (table - high.astype(np.float32)).astype(jnp.bfloat16)
    return np.stack([high, low])


def normalize(values):
    centre = values - jnp.mean(values, axis=-1, keepdims=True)
    spread = jnp.mean(centre * centre, axis=-1, keepdims=True)
    inverse = lax.rsqrt(spread + EPSILON)
    return centre * inverse, inverse


def norm_back(upstream, unit_rows, inverse, gain):
    scaled = upstream * gain
    first_mean = jnp.mean(scaled, axis=-1, keepdims=True)
    second_mean = jnp.mean(scaled * unit_rows, axis=-1, keepdims=True)
    return inverse * (scaled - first_mean - unit_rows * second_mean)


def lane_head(rows):
    return lax.broadcasted_iota(jnp.int32, (rows, LANES), 1) // HEAD


def swap_halves(x):
    lane = lax.broadcasted_iota(jnp.int32, x.shape, 1)
    return jnp.where(
        lane % HEAD < HEAD // 2,
        pltpu.roll(x, LANES - HEAD // 2, 1),
        pltpu.roll(x, HEAD // 2, 1),
    )


def turn(x, trig, sign):
    swapped = swap_halves(x)
    cosine, sine = trig[:, :128], sign * trig[:, 128:]
    parts = [
        x[:, i : i + 128] * cosine + swapped[:, i : i + 128] * sine for i in range(0, LANES, 128)
    ]
    return jnp.concatenate(parts, axis=1)


def by_head(block, head):
    return jnp.concatenate(
        [jnp.where(head == h, block, jnp.zeros_like(block)) for h in range(HEADS_HERE)], axis=0
    )


def merge_heads(stacked, head):
    parts = jnp.split(stacked, HEADS_HERE, axis=0)
    return jnp.where(head == 0, parts[0], jnp.where(head == 1, parts[1], parts[2]))


def static_window(i):
    reach = DOC // QB
    return max(0, i - reach) * QB, min(LEN // QB, i + reach + 1) * QB


def project_kernel(
    tok_ref, seg_ref, gain_ref, w_ref, table_ref,
    q_ref, k_ref, v_ref, normed_ref, trig_ref, segc_ref,
    proj_ref,
):
    seg = jnp.broadcast_to(seg_ref[...].astype(F32), (8, LEN))
    index = lax.broadcasted_iota(jnp.int32, (8, LEN), 1)
    first = jnp.where(seg != pltpu.roll(seg, 1, 1), index, 0)
    first = jnp.where(index == 0, 0, first).astype(F32)
    shift = 1
    while shift < DOC:
        first = jnp.maximum(first, jnp.where(index >= shift, pltpu.roll(first, shift, 1), 0.0))
        shift *= 2
    place = index.astype(F32) - first
    segc_ref[...] = jnp.transpose(jnp.broadcast_to(seg[:1], (128, LEN)))
    placec = jnp.transpose(jnp.broadcast_to(place[:1], (128, LEN)))
    lane = lax.broadcasted_iota(jnp.int32, (LEN, 128), 1).astype(F32)
    hot = jnp.concatenate(
        [jnp.where(placec == lane + 128.0 * j, 1.0, 0.0) for j in range(DOC // 128)], axis=1
    ).astype(BF16)
    trig_ref[...] = dot(hot, table_ref[0]) + dot(hot, table_ref[1])

    step = LEN // 4
    proj_ref[:, COLS:] = jnp.zeros((step, LANES - COLS), F32)
    for i in range(4):
        rows = slice(i * step, (i + 1) * step)
        unit, _ = normalize(tok_ref[rows, :].astype(F32))
        normed = (unit * gain_ref[...]).astype(BF16)
        normed_ref[rows, :] = normed
        for s, out in enumerate((q_ref, k_ref, v_ref)):
            proj_ref[:, :COLS] = dot(normed, w_ref[s], NT)
            x = proj_ref[...]
            out[rows, :] = (turn(x, trig_ref[rows, :], 1.0) if s < 2 else x).astype(BF16)


def attend_kernel(
    s_ref, seg_ref, segc_ref, q_ref, k_ref, v_ref, c0_ref, c1_ref, c2_ref, c3_ref, lse_ref, ctx_ref
):
    z = s_ref[0]
    head = lane_head(QB)
    column = lax.broadcasted_iota(jnp.int32, (QB, 128), 1)

    def products(i):
        low, high = static_window(i)
        block = q_ref[i * QB : (i + 1) * QB, :] * jnp.asarray(1.0 / math.sqrt(HEAD), BF16)
        return dot(by_head(block, head), k_ref[low:high, :], NT)

    ahead = products(0)
    for i in range(LEN // QB):
        low, high = static_window(i)
        rows = slice(i * QB, (i + 1) * QB)
        scores = ahead
        if (i + 1) * QB < LEN:
            ahead = products(i + 1)
        same = segc_ref[rows, 0:1] == seg_ref[0:1, low:high].astype(F32)
        parts, logs = [], []
        for h in range(HEADS_HERE):
            mine = jnp.where(same, scores[h * QB : (h + 1) * QB], NEGATIVE)
            top = jnp.max(mine, axis=-1, keepdims=True)
            weights = jnp.exp(mine - top)
            total = jnp.sum(weights, axis=-1, keepdims=True)
            parts.append((weights * (1.0 / total)).astype(BF16))
            logs.append(top + jnp.log(total))
        lse_ref[rows, :] = jnp.where(column == 0, logs[0], jnp.where(column == 1, logs[1], logs[2]))
        mixed = dot(jnp.concatenate(parts, axis=0), v_ref[low:high, :])
        context = merge_heads(mixed, head)[:, :COLS].astype(BF16)
        block, r = i * QB // BLOCK, i * QB % BLOCK
        ctx_ref[block, r : r + QB, :COLS] = context
        ctx_ref[block ^ 1, r : r + QB, COLS:] = context
    for k, out in enumerate((c0_ref, c1_ref, c2_ref, c3_ref)):
        out[...] = ctx_ref[z ^ k]


def place_slots(s_ref, refs, out_ref):
    rows, cols = refs[0].shape[1:]
    for group, ref in enumerate(refs):
        for i in range(2):
            slot = s_ref[1] ^ ORDER[4 * (group // 2) + 2 * i + group % 2]
            there = pl.ds(pl.multiple_of((slot // 2) * rows, 16), rows)
            out_ref[there, pl.ds(pl.multiple_of((slot % 2) * cols, 128), cols)] = ref[i]


def gated(normed, act_back, w_in, w_down, act_ref, gb_ref, width):
    both = dot(normed, w_in, NT)
    gate, linear = both[:, :width], both[:, width:]
    cdf = 0.5 * (1.0 + lax.erf(gate * math.sqrt(0.5)))
    slope = cdf + gate * (jnp.exp(-0.5 * gate * gate) * (1.0 / math.sqrt(2.0 * math.pi)))
    gelu = gate * cdf
    act_ref[...] = (gelu * linear).astype(BF16)
    gb_ref[:, :width] = (act_back * linear * slope).astype(BF16)
    gb_ref[:, width:] = (act_back * gelu).astype(BF16)
    return dot(act_ref[...], w_down), dot(gb_ref[...], w_in)


def begin_kernel(
    s_ref, tok_ref, cot_ref, c0, c1, c2, c3, w_ref, dw_ref, res_ref, context_ref, cot_out, back_ref
):
    z = s_ref[0]
    for half in range(2):
        base = (z if half == 0 else z ^ 1) * BLOCK
        there = pl.ds(pl.multiple_of(base, BLOCK), BLOCK)
        rows = slice(half * BLOCK, (half + 1) * BLOCK)
        mine = slice(half * COLS, (half + 1) * COLS)
        res_ref[rows, :] = tok_ref[there, :].astype(F32) + dot(c0[:, mine], w_ref[...])
        for k, c in enumerate((c1, c2, c3)):
            context_ref[k, rows, :] = c[:, mine]
        cot_out[rows, :] = cot_ref[there, :]
    back_ref[...] = dot(cot_out[...], dw_ref[...], NT)


def middle_kernel(
    s_ref, part_ref, context_ref, cot_ref, act_back_ref, w_ref, here_ref, there_ref, gain_ref, gw_ref, dw_ref,
    res_ref, normed_ref, act_ref, gb_ref, branch_ref, back_ref, wo_ref,
):
    wo_ref[0] = w_ref[...]
    few = COLS // 4
    pieces = ((0, here_ref, 0), (2, here_ref, 1), (1, there_ref, 0), (3, there_ref, 1))
    for slot, ref, i in pieces:
        there = pl.ds(pl.multiple_of((s_ref[1] % 4 ^ slot) * few, 16), few)
        for k in range(3):
            for side in range(2):
                first = (2 * k + side) * few
                lanes = slice(side * (D // 2), (side + 1) * (D // 2))
                wo_ref[k + 1, there, lanes] = ref[i, first : first + few, :]
    residual = part_ref[...]
    for k in range(3):
        residual += dot(context_ref[k], wo_ref[k + 1])
    res_ref[...] = residual[:BLOCK]
    unit, _ = normalize(residual)
    normed_ref[...] = (unit * gain_ref[...]).astype(BF16)
    branch_ref[...], back_ref[...] = gated(
        normed_ref[BLOCK:, :], act_back_ref[BLOCK:, :], gw_ref[...], dw_ref[...], act_ref, gb_ref, dw_ref.shape[0]
    )


def partner_kernel(
    s_ref, normed_ref, cot_ref, branch_in, back_in, f0, f1, f2, f3,
    act_ref, gb_ref, branch_ref, back_ref, other_ref,
):
    width = act_ref.shape[1]
    place_slots(s_ref, (f0, f1, f2, f3), other_ref)
    branch, back = gated(
        normed_ref[BLOCK:, :], dot(cot_ref[BLOCK:, :], other_ref[2 * width : 3 * width, :], NT), other_ref[: 2 * width, :],
        other_ref[2 * width : 3 * width, :], act_ref, gb_ref, width,
    )
    branch_ref[...] = (branch_in[...] + branch).astype(BF16)
    back_ref[...] = (back_in[...] + back).astype(BF16)


def own_kernel(
    s_ref, normed_ref, cot_ref, act_back_ref, res_ref, gw_ref, dw_ref, other_ref,
    act_par, gb_par, act_par_two, gb_par_two,
    branch_ref, back_ref, whole_ref,
    act_one, gb_one, act_two, gb_two,
):
    width = act_par.shape[1]
    normed, cot = normed_ref[:BLOCK, :], cot_ref[:BLOCK, :]
    w_down = other_ref[2 * width : 3 * width, :]
    branch, back = gated(normed, act_back_ref[:BLOCK, :], gw_ref[...], dw_ref[...], act_one, gb_one, width)
    more, back_more = gated(normed, dot(cot, w_down, NT), other_ref[: 2 * width, :], w_down, act_two, gb_two, width)
    branch_ref[...] = res_ref[...] + branch + more
    back_ref[...] = back + back_more
    half = whole_ref.shape[1] // 2
    shards = ((act_one, gb_one, act_par, gb_par), (act_two, gb_two, act_par_two, gb_par_two))
    for shard, (act, gb, act_there, gb_there) in enumerate(shards):
        at = shard * half
        part = dot(normed, gb[...], TN) + dot(normed_ref[BLOCK:, :], gb_there[...], TN)
        whole_ref[:, at : at + 2 * width] = part.astype(BF16)
        part = dot(cot, act[...], TN) + dot(cot_ref[BLOCK:, :], act_there[...], TN)
        whole_ref[:, at + 2 * width : at + 3 * width] = part.astype(BF16)
        whole_ref[:, at + 3 * width : at + half] = jnp.zeros((D, half - 3 * width), BF16)


def finish_kernel(keep_ref, r1, r2, r3, geglu_ref, down_ref, out_ref, pad_ref):
    half = r2.shape[1] - COLS
    rows, width = geglu_ref.shape[1:]
    ff = keep_ref[:, :half] + r2[:, :half].astype(F32)
    geglu_ref[0] = ff[:, :width]
    geglu_ref[1] = ff[:, width : 2 * width]
    out = keep_ref[:, half:] + r1[...].astype(F32) + r2[:, half:].astype(F32) + r3[...].astype(F32)
    pad_ref[...] = jnp.zeros_like(pad_ref)
    pad_ref[:rows, :width] = ff[:, 2 * width : 3 * width]
    down_ref[...] = jnp.transpose(pad_ref[...])[:width, :rows]
    pad_ref[:rows, :COLS] = out
    out_ref[...] = jnp.transpose(pad_ref[...])[:COLS, :rows]


def qkv_sum_kernel(parts_ref, grad_ref, gains_ref):
    rows = grad_ref.shape[1]
    total = jnp.sum(parts_ref[...].astype(F32), axis=0)
    for s in range(3):
        grad_ref[s] = total[:rows, s * COLS : (s + 1) * COLS]
    for gain in range(2):
        for side in range(2):
            first = rows + 6 * gain + side
            part = total[first : first + 1] + total[first + 2 : first + 3] + total[first + 4 : first + 5]
            gains_ref[gain : gain + 1, side * (D // 2) : (side + 1) * (D // 2)] = part[:, : D // 2]


def residual_kernel(
    keep_ref, recv_ref, res_ref, gain_ref, cot_ref, wo_ref,
    back_ref, low_ref, gain_out, b0, b1, b2, b3,
):
    unit, inverse = normalize(res_ref[...])
    upstream = keep_ref[...] + recv_ref[...].astype(F32)
    back = cot_ref[:BLOCK, :].astype(F32) + norm_back(upstream, unit, inverse, gain_ref[...])
    back_ref[...] = back
    gain_out[...] = jnp.sum(upstream * unit, axis=0, keepdims=True)
    low = back.astype(BF16)
    low_ref[...] = low
    for k, out in enumerate((b0, b1, b2, b3)):
        part = dot(low, wo_ref[k], NT).astype(BF16)
        out[:, :COLS] = part[: BLOCK // 2]
        out[:, COLS:] = part[BLOCK // 2 :]


def output_grad_kernel(s_ref, low_ref, c0, c1, c2, c3, ff_ref, even_ref, odd_ref, whole_ref):
    for k, c in enumerate((c0, c1, c2, c3)):
        whole_ref[:, k * COLS : (k + 1) * COLS] = dot(low_ref[...], c[:, :COLS], TN).astype(BF16)
    rows, ff = even_ref.shape[1], ff_ref.shape[1]
    for i in range(8):
        there = pl.ds(pl.multiple_of((s_ref[1] ^ ORDER[i]) * rows, 16), rows)
        out = even_ref.at[i] if i < 4 else odd_ref.at[i - 4]
        out[:, :ff] = ff_ref[there, :]
        out[:, ff:] = whole_ref[there, :]


def collect_kernel(own_ref, r1, r2, r3, keep_ref, s1, s2, s3):
    total = own_ref[...] + r1[...].astype(F32) + r2[...].astype(F32) + r3[...].astype(F32)
    half = keep_ref.shape[1] - COLS
    keep_ref[:, :half] = total[:, :half]
    keep_ref[:, half:] = total[:, 2 * half : 2 * half + COLS]
    s2[:, :half] = total[:, half : 2 * half].astype(BF16)
    for k, out in ((1, s1), (2, s2), (3, s3)):
        first = 2 * half + k * COLS
        out[:, out.shape[1] - COLS :] = total[:, first : first + COLS].astype(BF16)


def pack_kernel(s_ref, w_in_ref, w_down_ref, w_out_ref, out_ref, ff_ref, sems, out_sems):
    slot = s_ref[1]
    cols = pl.ds(pl.multiple_of((slot % 2) * (D // 2), 128), D // 2)
    few = out_ref.shape[0] // 2
    here = pl.ds(pl.multiple_of(slot % 4 * few, 16), few)
    copies = [
        pltpu.make_async_copy(
            w_out_ref.at[here, side * (D // 2) : (side + 1) * (D // 2)],
            out_ref.at[side * few : (side + 1) * few, :],
            out_sems.at[side],
        )
        for side in range(2)
    ]
    for copy in copies:
        copy.start()
    n_in, n_down = w_in_ref.shape[0] // PART, w_down_ref.shape[0] // PART
    parts = ff_ref.shape[0] // PART
    for i in range(parts):
        at = (slot // 2) * parts + i
        there = ff_ref.at[i * PART : (i + 1) * PART, :]

        def fetch(ref, first):
            rows = pl.ds(pl.multiple_of((at - first) * PART, PART), PART)
            return pltpu.make_async_copy(ref.at[rows, cols], there, sems.at[i])

        @pl.when(at < n_in)
        def _():
            fetch(w_in_ref, 0).start()

        @pl.when((at >= n_in) & (at < n_in + n_down))
        def _():
            fetch(w_down_ref, n_in).start()

        @pl.when(at >= n_in + n_down)
        def _():
            there[...] = jnp.zeros(there.shape, BF16)

    for copy in copies:
        copy.wait()
    for i in range(parts):
        there = ff_ref.at[i * PART : (i + 1) * PART, :]

        @pl.when((slot // 2) * parts + i < n_in + n_down)
        def _():
            pltpu.make_async_copy(w_in_ref.at[:PART, : D // 2], there, sems.at[i]).wait()


def arrived_kernel(s_ref, f1, f2, f3, out_ref):
    few = f1.shape[0]
    for i, piece in enumerate((f1, f2, f3)):
        out_ref[i * few : (i + 1) * few, :] = piece[...]


def pair_kernel(s_ref, a0, a1, out_ref):
    out_ref[0] = a0[...]
    out_ref[1] = a1[...]


def backward_steps(
    mirror, steps, seg_ref, segc_ref, q_ref, k_ref, v_ref, lse_ref, back_ref, dq_ref, dk_ref, dv_ref
):
    last = LEN // QB - 1
    head = lane_head(QB)
    scale = jnp.asarray(1.0 / math.sqrt(HEAD), BF16)

    def products(step):
        low, high = static_window(step)
        i = jnp.where(mirror == 1, last - step, step)
        rows = pl.ds(pl.multiple_of(i * QB, QB), QB)
        keys = jnp.where(mirror == 1, LEN - high, low)
        keys = pl.ds(pl.multiple_of(keys, QB), high - low)
        stacked = by_head(q_ref[rows, :] * scale, head)
        upstream = by_head(back_ref[rows, :], head)
        scores = dot(stacked, k_ref[keys, :], NT)
        prob_back = dot(upstream, v_ref[keys, :], NT)
        return rows, keys, stacked, upstream, scores, prob_back

    ahead = products(steps[0])
    for step in steps:
        rows, keys, stacked, upstream, scores, prob_back = ahead
        if step + 1 in steps:
            ahead = products(step + 1)
        same = segc_ref[rows, 0:1] == seg_ref[0:1, keys].astype(F32)
        probs, grads = [], []
        for h in range(HEADS_HERE):
            at = slice(h * QB, (h + 1) * QB)
            prob = jnp.exp(jnp.where(same, scores[at], NEGATIVE) - lse_ref[rows, h : h + 1])
            inner = jnp.sum(prob * prob_back[at], axis=-1, keepdims=True)
            probs.append(prob.astype(BF16))
            grads.append((prob * (prob_back[at] - inner)).astype(BF16))
        prob = jnp.concatenate(probs, axis=0)
        grad = jnp.concatenate(grads, axis=0)
        dv_ref[:, keys] += dot(upstream, prob, TN)
        dk_ref[:, keys] += dot(stacked, grad, TN)
        dq_ref[rows, :] = merge_heads(dot(grad, k_ref[keys, :]), head) * (1.0 / math.sqrt(HEAD))


def rows_back(base, dq_ref, dk_ref, dv_ref, trig_ref, w_ref, qkv_ref):
    rows = pl.ds(pl.multiple_of(base, BLOCK), BLOCK)
    trig = trig_ref[rows, :]
    total = None
    for part, grad_ref in enumerate((dq_ref, dk_ref, dv_ref)):
        g = jnp.transpose(grad_ref[:, rows]) if part else grad_ref[rows, :]
        if part < 2:
            g = turn(g, trig, -1.0)
        low = g[:, :COLS].astype(BF16)
        qkv_ref[:, part * COLS : (part + 1) * COLS] = low
        product = dot(low, w_ref[part])
        total = product if total is None else total + product
    return total


def backward_far_kernel(
    s_ref, seg_ref, segc_ref, q_ref, k_ref, v_ref, lse_ref, trig_ref, b0, b1, b2, b3, w_ref,
    n2, n3, qkv_ref, back_ref, dq_ref, dk_ref, dv_ref,
):
    z = s_ref[0]
    pair = z // 2
    half = BLOCK // 2
    back_ref[:, COLS:] = jnp.zeros((LEN, LANES - COLS), BF16)
    for k, b in enumerate((b0, b1, b2, b3)):
        base = pl.multiple_of((z ^ k) * BLOCK, BLOCK)
        back_ref[pl.ds(base, half), :COLS] = b[:, :COLS]
        back_ref[pl.ds(pl.multiple_of(base + half, half), half), :COLS] = b[:, COLS:]
    dk_ref[...] = jnp.zeros_like(dk_ref)
    dv_ref[...] = jnp.zeros_like(dv_ref)
    refs = (seg_ref, segc_ref, q_ref, k_ref, v_ref, lse_ref, back_ref, dq_ref, dk_ref, dv_ref)
    steps = LEN // QB
    reach = DOC // QB
    backward_steps(1 - pair, range(steps // 2 + reach), *refs)
    for k, out in ((2, n2), (3, n3)):
        at = qkv_ref.at[(k - 2) * BLOCK : (k - 1) * BLOCK]
        part = rows_back((z ^ k) * BLOCK, dq_ref, dk_ref, dv_ref, trig_ref, w_ref, at)
        out[...] = part.astype(out.dtype)


def add_kernel(mine_ref, recv_ref, out_ref):
    out_ref[...] = (mine_ref[...] + recv_ref[...].astype(F32)).astype(out_ref.dtype)


def backward_near_kernel(
    s_ref, seg_ref, segc_ref, q_ref, k_ref, v_ref, lse_ref, trig_ref, back_ref, dq_in, dk_in, dv_in,
    w_ref, n0, n1, qkv_ref, dq_ref, dk_ref, dv_ref,
):
    z = s_ref[0]
    pair = z // 2
    dq_ref[...] = dq_in[...]
    dk_ref[...] = dk_in[...]
    dv_ref[...] = dv_in[...]
    refs = (seg_ref, segc_ref, q_ref, k_ref, v_ref, lse_ref, back_ref, dq_ref, dk_ref, dv_ref)
    steps = LEN // QB
    reach = DOC // QB
    backward_steps(pair, range(steps // 2 - reach), *refs)
    for k, out in ((0, n0), (1, n1)):
        at = qkv_ref.at[k * BLOCK : (k + 1) * BLOCK]
        part = rows_back((z ^ k) * BLOCK, dq_ref, dk_ref, dv_ref, trig_ref, w_ref, at)
        out[...] = part.astype(out.dtype)


def qkv_grad_kernel(
    s_ref, normed_ref, near_ref, far_ref, w_ref, gain_ref, gain_two_ref, out_ref, whole_ref, rows_ref
):
    for k in range(NARROW):
        base = pl.multiple_of((s_ref[0] ^ k) * BLOCK, BLOCK)
        rows_ref[k * BLOCK : (k + 1) * BLOCK, :] = normed_ref[pl.ds(base, BLOCK), :]
    pair = 2 * BLOCK
    total = None
    for s in range(3):
        cols = slice(s * COLS, (s + 1) * COLS)
        part = dot(rows_ref[:pair, :], near_ref[:, cols], TN)
        part += dot(rows_ref[pair:, :], far_ref[:, cols], TN)
        whole_ref[:, cols] = part.astype(BF16)
        weighted = part * jnp.transpose(w_ref[s].astype(F32))
        total = weighted if total is None else total + weighted
    column = jnp.broadcast_to(jnp.sum(total, axis=1, keepdims=True), (D, 128))
    gains = (jnp.transpose(column)[:1, :] / gain_ref[...], gain_two_ref[...])
    extra = jnp.zeros((GAIN_ROWS, D // 2), F32)
    row = lax.broadcasted_iota(jnp.int32, extra.shape, 0)
    at = 0
    for gain in gains:
        rest = gain
        for _ in range(3):
            term = rest.astype(BF16).astype(F32)
            rest = rest - term
            for side in range(2):
                extra = jnp.where(row == at, term[:, side * (D // 2) : (side + 1) * (D // 2)], extra)
                at += 1
    blocks, rows, cols = out_ref.shape
    rows -= GAIN_ROWS
    for i in range(blocks):
        if rows % 16 == 0:
            out_ref[i, :rows, :] = whole_ref[i * rows : (i + 1) * rows, :]
            out_ref[i, rows:, :] = jnp.zeros((GAIN_ROWS, cols), BF16)
            out_ref[i, rows:, : D // 2] = extra.astype(BF16)
        else:
            lines = [whole_ref[i * rows : (i + 1) * rows, :].astype(F32)]
            pad = jnp.zeros((GAIN_ROWS, cols - D // 2), F32)
            lines.append(jnp.concatenate([extra, pad], axis=1))
            out_ref[i] = jnp.concatenate(lines, axis=0).astype(BF16)


def final_kernel(
    s_ref, tok_ref, gain_ref, back_ref, n0, n1, n2, own_ref, branch_ref, out_ref, layer_ref
):
    upstream = n0[...] + n1[...].astype(F32) + n2[...].astype(F32)
    rows = pl.ds(pl.multiple_of(s_ref[0] * BLOCK, BLOCK), BLOCK)
    unit, inverse = normalize(tok_ref[rows, :].astype(F32))
    out_ref[...] = back_ref[...] + norm_back(upstream, unit, inverse, gain_ref[...])
    layer_ref[...] = (own_ref[...] + branch_ref[...].astype(F32)).astype(BF16)


def fold_kernel(even_ref, recv_ref, own_ref, s1_ref, s2_ref, s3_ref):
    for i, out in enumerate((own_ref, s1_ref, s2_ref, s3_ref)):
        out[...] = (even_ref[i].astype(F32) + recv_ref[i].astype(F32)).astype(out.dtype)


def along_narrow(x, k):
    return lax.ppermute(x, "narrow", [(i, i ^ k) for i in range(NARROW)])


def along_wide(x, k):
    return lax.ppermute(x, "wide", [(i, i ^ k) for i in range(lax.axis_size("wide"))])


def tie(x, *others):
    return lax.optimization_barrier((x, *others))[0]


def quarter_slice(x, slot):
    rows, cols = x.shape[-2] // 4, x.shape[-1] // 2
    x = lax.dynamic_slice_in_dim(x, (slot // 2) * rows, rows, x.ndim - 2)
    return lax.dynamic_slice_in_dim(x, (slot % 2) * cols, cols, x.ndim - 1)


def all_slots(x, hops):
    whole = jnp.stack([along_narrow(x, k) for k in hops])
    slots = jnp.stack([quarter_slice(whole, i) for i in ORDER])
    return slots[:4], slots[4:]


def sum_wide(x):
    return jnp.sum(lax.all_to_all(x, "wide", 0, 0).astype(F32), axis=0)


def per_device(
    tokens, segments, first_gain, qkv_weight, output_weight, second_gain, geglu_weight, down_weight,
    cotangent,
):
    size = lax.axis_size("wide")
    plane = size == 8
    mine = lax.axis_index("wide").astype(jnp.int32)
    z = lax.axis_index("narrow").astype(jnp.int32)
    scalars = jnp.stack([z, mine if plane else jnp.zeros_like(mine)])
    hidden = geglu_weight.shape[2]
    padded = -(-3 * hidden // 64) * 64
    rows_d = D // size
    gain_one = first_gain.reshape(1, D)
    gain_two = second_gain.reshape(1, D)
    w_qkv = qkv_weight.transpose(0, 2, 1)
    w_in = geglu_weight.transpose(0, 2, 1).reshape(2 * hidden, D)

    few, many = COLS // 4, padded // 4
    now = scalars
    if plane:
        slot_out, slot_ff = call(
            pack_kernel,
            (scalars, *(pltpu.with_memory_space_constraint(w, pltpu.HBM) for w in (w_in, down_weight, output_weight))),
            (sds((2 * few, D // 2), BF16), sds((many, D // 2), BF16)),
            [pltpu.SemaphoreType.DMA((many // PART,)), pltpu.SemaphoreType.DMA((2,))],
            place=pltpu.HBM,
        )
        out_fetched = [along_narrow(slot_out, k) for k in (1, 2, 3)]
        ff_fetched = along_narrow(slot_ff, 2)
    wide_rows = sds((LEN, LANES), BF16)
    q, k, v, normed_one, trig, segc = call(
        project_kernel,
        (tokens, segments, gain_one, w_qkv, jnp.asarray(rotary_table())),
        (wide_rows, wide_rows, wide_rows, sds((LEN, D), BF16), sds((LEN, 2 * 128), F32),
         sds((LEN, 128), F32)),
        [pltpu.VMEM((LEN // 4, LANES), F32)],
        scalars=0,
    )
    piece = sds((BLOCK, 2 * COLS), BF16)
    c0, c1, c2, c3, lse = call(
        attend_kernel,
        (now, segments, segc, q, k, v),
        (piece, piece, piece, piece, sds((LEN, 128), F32)),
        [pltpu.VMEM((NARROW, BLOCK, 2 * COLS), BF16)],
    )
    context = (c0, *(along_narrow(c, k) for k, c in ((1, c1), (2, c2), (3, c3))))
    if plane:
        ff0 = tie(ff_fetched, lse)
        slots_two = sds((2, many, D // 2), BF16)
        (out0,) = call(
            arrived_kernel, (tie(scalars, lse), *out_fetched), (sds((6 * few, D // 2), BF16),)
        )
        (out_here,) = call(
            pair_kernel, (scalars, out0, along_wide(out0, 2)), (sds((2, 6 * few, D // 2), BF16),)
        )
        out_there = along_wide(out_here, 1)
        (ff_pair,) = call(pair_kernel, (scalars, ff0, along_wide(ff0, 4)), (slots_two,))
        ff_x = along_wide(ff_pair, 2)
        ff_slots = (ff_pair, ff_x, along_wide(ff_pair, 1), along_wide(ff_x, 1))
    else:
        everything = jnp.concatenate(
            [w_in, down_weight, jnp.zeros((padded - 3 * hidden, D), BF16)], axis=0
        )
        even, odd = (x[:, 0] for x in all_slots(everything, (2,)))
        ff_slots = (even[::2], even[1::2], odd[::2], odd[1::2])
        others = jnp.stack([along_narrow(output_weight, k) for k in (1, 2, 3)])
        others = others.reshape(3, 4, few, 2, D // 2).transpose(1, 0, 3, 2, 4)
        others = others.reshape(4, 6 * few, D // 2)
        out_here, out_there = others[::2], others[1::2]

    whole = sds((2 * BLOCK, D), F32)
    own = sds((BLOCK, D), F32)
    own_low = sds((BLOCK, D), BF16)
    part, contexts, cot, act_back = call(
        begin_kernel,
        (scalars, tokens, cotangent, *context, output_weight, down_weight),
        (whole, sds((3, 2 * BLOCK, COLS), BF16), sds((2 * BLOCK, D), BF16),
         sds((2 * BLOCK, hidden), F32)),
    )
    part_act, part_gb = sds((BLOCK, hidden), BF16), sds((BLOCK, 2 * hidden), BF16)
    res, normed_two, act_par, gb_par, branch, back, wo = call(
        middle_kernel,
        (scalars, part, contexts, cot, act_back, output_weight, out_here, out_there, gain_two, w_in,
         down_weight),
        (own, sds((2 * BLOCK, D), BF16), part_act, part_gb, own, own, sds((NARROW, COLS, D), BF16)),
    )
    act_par_two, gb_par_two, out_send, send, other = call(
        partner_kernel,
        (scalars, normed_two, cot, branch, back, *ff_slots),
        (part_act, part_gb, own_low, own_low, sds((padded, D), BF16)),
    )
    recv = along_narrow(send, 1)
    half = -(-3 * hidden // 128) * 128
    out_keep, keep, ff_part = call(
        own_kernel,
        (scalars, normed_two, cot, act_back, res, w_in, down_weight, other, act_par, gb_par,
         act_par_two, gb_par_two),
        (own, own, sds((D, 2 * half), BF16)),
        [pltpu.VMEM((BLOCK, hidden), BF16), pltpu.VMEM((BLOCK, 2 * hidden), BF16)] * 2,
    )
    low_piece = sds((BLOCK // 2, 2 * COLS), BF16)
    back, low, gain_two_part, b0, b1, b2, b3 = call(
        residual_kernel,
        (keep, recv, res, gain_two, cot, wo),
        (own, own_low, sds((1, D), F32), low_piece, low_piece, low_piece, low_piece),
        scalars=0,
    )
    upstream = (b0, *(along_narrow(b, k) for k, b in ((1, b1), (2, b2), (3, b3))))
    grad_cols = 2 * half + NARROW * COLS
    even_part, odd_part = call(
        output_grad_kernel,
        (scalars, low, *context, ff_part),
        (sds((4, D // 8, grad_cols), BF16),) * 2,
        [pltpu.VMEM((D, NARROW * COLS), BF16)],
    )
    block = sds((rows_d, grad_cols), F32)
    if plane:
        block_low = sds((rows_d, grad_cols), BF16)
        grad_sum, *grad_sends = call(
            fold_kernel,
            (even_part, along_wide(odd_part, 1)),
            (block, block_low, block_low, block_low),
            scalars=0,
        )
        grad_recv = [along_wide(x, 2 * (i + 1)) for i, x in enumerate(grad_sends)]
        now = tie(scalars, *grad_sends)
    else:
        blocks = jnp.stack([even_part, odd_part], axis=1)
        grad_sum = sum_wide(blocks.reshape(size, rows_d, grad_cols))
        grad_recv, grad_sends = [jnp.zeros((rows_d, grad_cols), BF16)] * 3, ()
        now = tie(scalars, even_part)

    rows_f32 = sds((LEN, LANES), F32)
    columns_f32 = sds((LANES, LEN), F32)
    pair_qkv = sds((2 * BLOCK, 3 * COLS), BF16)
    n2, n3, qkv_far, back_rows, *grads = call(
        backward_far_kernel,
        (now, segments, segc, q, k, v, lse, trig, *upstream, w_qkv),
        (own, own_low, pair_qkv, wide_rows, rows_f32, columns_f32, columns_f32),
    )
    exchanged = along_narrow(n3, 1)
    branch_recv = along_narrow(tie(out_send, upstream[1], *grad_sends), 1)
    n0, n1, qkv_near = call(
        backward_near_kernel,
        (scalars, segments, segc, q, k, v, lse, trig, back_rows, *grads, w_qkv),
        (own, own_low, pair_qkv),
        [pltpu.VMEM((LEN, LANES), F32)] + [pltpu.VMEM((LANES, LEN), F32)] * 2,
    )
    (qkv_part,) = call(
        qkv_grad_kernel,
        (tie(scalars, n1, branch_recv), normed_one, qkv_near, qkv_far, w_qkv, gain_one, gain_two_part),
        (sds((size, rows_d + GAIN_ROWS, 3 * COLS), BF16),),
        [pltpu.VMEM((D, 3 * COLS), BF16), pltpu.VMEM((LEN, D), BF16)],
    )
    near_recv = along_narrow(n1, 1)
    (pair_sum,) = call(add_kernel, (tie(n2, qkv_part), exchanged), (own_low,), scalars=0)
    far_recv = along_narrow(pair_sum, 2)
    qkv_grad, gains = call(
        qkv_sum_kernel,
        (lax.all_to_all(qkv_part, "wide", 0, 0),),
        (sds((3, rows_d, COLS), F32), sds((2, D), F32)),
        scalars=0,
    )
    few_cols = sds((rows_d, COLS), BF16)
    grad_keep, *there = call(
        collect_kernel,
        (tie(grad_sum, near_recv, pair_sum), *grad_recv),
        (sds((rows_d, half + COLS), F32), few_cols, sds((rows_d, half + COLS), BF16), few_cols),
        scalars=0,
    )
    there = [along_narrow(x, k) for k, x in zip((1, 2, 3), there)]
    tokens_grad, layer_out = call(
        final_kernel,
        (scalars, tokens, gain_one, back, n0, near_recv, far_recv, out_keep, branch_recv),
        (own, own_low),
    )
    gains = gains + along_narrow(gains, 1) + along_narrow(gains, 2) + along_narrow(gains, 3)
    geglu_grad, down_grad, out_grad = call(
        finish_kernel,
        (tie(grad_keep, tokens_grad), *there),
        (sds((2, rows_d, hidden), F32), sds((hidden, rows_d), F32), sds((COLS, rows_d), F32)),
        [pltpu.VMEM((128, -(-hidden // 128) * 128), F32)],
        scalars=0,
    )
    return (
        layer_out, tokens_grad, gains[0], qkv_grad, out_grad, gains[1], geglu_grad, down_grad,
    )


def solution(mesh):
    return jax.shard_map(
        per_device,
        mesh=mesh,
        in_specs=(
            P("wide", None),
            P("wide", None),
            P(),
            P(None, None, "narrow"),
            P("narrow", None),
            P(),
            P(None, None, "narrow"),
            P("narrow", None),
            P("wide", None),
        ),
        out_specs=(
            P(("wide", "narrow"), None),
            P(("wide", "narrow"), None),
            P(),
            P(None, "wide", "narrow"),
            P("narrow", "wide"),
            P(),
            P(None, "wide", "narrow"),
            P("narrow", "wide"),
        ),
        check_vma=False,
    )
```

```python
import functools
import math

import jax
import jax.numpy as jnp
import numpy as np
from jax import lax
from jax.experimental import pallas as pl
from jax.experimental.pallas import tpu as pltpu
from jax.sharding import PartitionSpec as P

HEAD = 64
LEN = 1024
D = 768
HEADS_HERE = 3
COLS = HEADS_HERE * HEAD
LANES = 256
DOC = 256
QB = 128
PART = 32
WINDOW = QB + 2 * DOC
EPSILON = 1e-05
ROPE_BASE = 160000.0
NARROW = 4
BLOCK = LEN // NARROW
ORDER = (0, 2, 4, 6, 1, 3, 5, 7)
F32 = jnp.float32
GAIN_ROWS = 16
BF16 = jnp.bfloat16
NEGATIVE = -1e30
MIB = 1024 * 1024
COST = {
    "finish_kernel": 1,
    "qkv_sum_kernel": 1,
    "pack_kernel": 1,
    "arrived_kernel": 1,
    "pair_kernel": 1,
    "begin_kernel": 100,
    "project_kernel": 6,
    "attend_kernel": 100,
    "middle_kernel": 5,
    "partner_kernel": 3,
    "own_kernel": 10,
    "residual_kernel": 100,
    "output_grad_kernel": 2,
    "fold_kernel": 2,
    "backward_far_kernel": 100,
    "backward_near_kernel": 100,
    "add_kernel": 100,
    "qkv_grad_kernel": 1,
    "collect_kernel": 1,
    "final_kernel": 100,
}

NN = (((1,), (0,)), ((), ()))
NT = (((1,), (1,)), ((), ()))
TN = (((0,), (0,)), ((), ()))


def dot(a, b, dims=NN):
    return lax.dot_general(a, b, dims, preferred_element_type=F32)


def call(body, ins, outs, scratch=(), scalars=1, place=pltpu.VMEM, far=()):
    name = getattr(body, "func", body).__name__
    specs = [pl.BlockSpec(memory_space=pltpu.SMEM)] * scalars
    specs += [pl.BlockSpec(memory_space=place)] * (len(ins) - scalars)
    size = sum(math.prod(x.shape) * x.dtype.itemsize for x in (*ins, *outs))
    held = sum(math.prod(x.shape) * x.dtype.itemsize for x in scratch if hasattr(x.dtype, "itemsize"))
    return pl.pallas_call(
        body,
        name=name,
        out_shape=tuple(pltpu.HBM(o.shape, o.dtype) if i in far else sds(o.shape, o.dtype) for i, o in enumerate(outs)),
        in_specs=specs,
        out_specs=tuple(pl.BlockSpec(memory_space=pltpu.VMEM) for _ in outs),
        scratch_shapes=list(scratch),
        compiler_params=pltpu.CompilerParams(vmem_limit_bytes=size + size // 4 + held + 8 * MIB),
        cost_estimate=pl.CostEstimate(flops=COST[name] * 10**9, bytes_accessed=size, transcendentals=0),
    )(*ins)


def sds(shape, dtype):
    return jax.ShapeDtypeStruct(shape, dtype)


def rotary_table():
    position = np.arange(DOC, dtype=np.float64)
    frequency = ROPE_BASE ** (-2.0 * np.arange(HEAD // 2, dtype=np.float64) / HEAD)
    angle = position[:, None] * frequency[None, :]
    cosine, sine = np.cos(angle), np.sin(angle)
    table = np.zeros((DOC, 2 * 128), np.float32)
    for h in range(2):
        base = h * HEAD
        table[:, base : base + 32] = cosine
        table[:, base + 32 : base + 64] = cosine
        table[:, 128 + base : 128 + base + 32] = -sine
        table[:, 128 + base + 32 : 128 + base + 64] = sine
    high = table.astype(jnp.bfloat16)
    low = (table - high.astype(np.float32)).astype(jnp.bfloat16)
    return np.stack([high, low])


def normalize(values):
    centre = values - jnp.mean(values, axis=-1, keepdims=True)
    spread = jnp.mean(centre * centre, axis=-1, keepdims=True)
    inverse = lax.rsqrt(spread + EPSILON)
    return centre * inverse, inverse


def norm_back(upstream, unit_rows, inverse, gain):
    scaled = upstream * gain
    first_mean = jnp.mean(scaled, axis=-1, keepdims=True)
    second_mean = jnp.mean(scaled * unit_rows, axis=-1, keepdims=True)
    return inverse * (scaled - first_mean - unit_rows * second_mean)


def lane_head(rows):
    return lax.broadcasted_iota(jnp.int32, (rows, LANES), 1) // HEAD


def swap_halves(x):
    lane = lax.broadcasted_iota(jnp.int32, x.shape, 1)
    return jnp.where(
        lane % HEAD < HEAD // 2,
        pltpu.roll(x, LANES - HEAD // 2, 1),
        pltpu.roll(x, HEAD // 2, 1),
    )


def turn(x, trig, sign):
    swapped = swap_halves(x)
    cosine, sine = trig[:, :128], sign * trig[:, 128:]
    parts = [
        x[:, i : i + 128] * cosine + swapped[:, i : i + 128] * sine for i in range(0, LANES, 128)
    ]
    return jnp.concatenate(parts, axis=1)


def by_head(block, head):
    return jnp.concatenate(
        [jnp.where(head == h, block, jnp.zeros_like(block)) for h in range(HEADS_HERE)], axis=0
    )


def merge_heads(stacked, head):
    parts = jnp.split(stacked, HEADS_HERE, axis=0)
    return jnp.where(head == 0, parts[0], jnp.where(head == 1, parts[1], parts[2]))


def static_window(i):
    reach = DOC // QB
    return max(0, i - reach) * QB, min(LEN // QB, i + reach + 1) * QB


def project_kernel(
    tok_ref, seg_ref, gain_ref, w_ref, table_ref,
    q_ref, k_ref, v_ref, normed_ref, trig_ref, segc_ref,
    proj_ref,
):
    seg = jnp.broadcast_to(seg_ref[...].astype(F32), (8, LEN))
    index = lax.broadcasted_iota(jnp.int32, (8, LEN), 1)
    first = jnp.where(seg != pltpu.roll(seg, 1, 1), index, 0)
    first = jnp.where(index == 0, 0, first).astype(F32)
    shift = 1
    while shift < DOC:
        first = jnp.maximum(first, jnp.where(index >= shift, pltpu.roll(first, shift, 1), 0.0))
        shift *= 2
    place = index.astype(F32) - first
    segc_ref[...] = jnp.transpose(jnp.broadcast_to(seg[:1], (128, LEN)))
    placec = jnp.transpose(jnp.broadcast_to(place[:1], (128, LEN)))
    lane = lax.broadcasted_iota(jnp.int32, (LEN, 128), 1).astype(F32)
    hot = jnp.concatenate(
        [jnp.where(placec == lane + 128.0 * j, 1.0, 0.0) for j in range(DOC // 128)], axis=1
    ).astype(BF16)
    trig_ref[...] = dot(hot, table_ref[0]) + dot(hot, table_ref[1])

    step = LEN // 4
    proj_ref[:, COLS:] = jnp.zeros((step, LANES - COLS), F32)
    for i in range(4):
        rows = slice(i * step, (i + 1) * step)
        unit, _ = normalize(tok_ref[rows, :].astype(F32))
        normed = (unit * gain_ref[...]).astype(BF16)
        normed_ref[rows, :] = normed
        for s, out in enumerate((q_ref, k_ref, v_ref)):
            proj_ref[:, :COLS] = dot(normed, w_ref[s], NT)
            x = proj_ref[...]
            out[rows, :] = (turn(x, trig_ref[rows, :], 1.0) if s < 2 else x).astype(BF16)


def attend_kernel(
    s_ref, seg_ref, segc_ref, q_ref, k_ref, v_ref, c0_ref, c1_ref, c2_ref, c3_ref, lse_ref, ctx_ref
):
    z = s_ref[0]
    head = lane_head(QB)
    column = lax.broadcasted_iota(jnp.int32, (QB, 128), 1)

    def products(i):
        low, high = static_window(i)
        block = q_ref[i * QB : (i + 1) * QB, :] * jnp.asarray(1.0 / math.sqrt(HEAD), BF16)
        return dot(by_head(block, head), k_ref[low:high, :], NT)

    ahead = products(0)
    for i in range(LEN // QB):
        low, high = static_window(i)
        rows = slice(i * QB, (i + 1) * QB)
        scores = ahead
        if (i + 1) * QB < LEN:
            ahead = products(i + 1)
        same = segc_ref[rows, 0:1] == seg_ref[0:1, low:high].astype(F32)
        parts, logs = [], []
        for h in range(HEADS_HERE):
            mine = jnp.where(same, scores[h * QB : (h + 1) * QB], NEGATIVE)
            top = jnp.max(mine, axis=-1, keepdims=True)
            weights = jnp.exp(mine - top)
            total = jnp.sum(weights, axis=-1, keepdims=True)
            parts.append((weights * (1.0 / total)).astype(BF16))
            logs.append(top + jnp.log(total))
        lse_ref[rows, :] = jnp.where(column == 0, logs[0], jnp.where(column == 1, logs[1], logs[2]))
        mixed = dot(jnp.concatenate(parts, axis=0), v_ref[low:high, :])
        context = merge_heads(mixed, head)[:, :COLS].astype(BF16)
        block, r = i * QB // BLOCK, i * QB % BLOCK
        ctx_ref[block, r : r + QB, :COLS] = context
        ctx_ref[block ^ 1, r : r + QB, COLS:] = context
    for k, out in enumerate((c0_ref, c1_ref, c2_ref, c3_ref)):
        out[...] = ctx_ref[z ^ k]


def place_slots(s_ref, refs, out_ref):
    rows, cols = refs[0].shape[1:]
    for group, ref in enumerate(refs):
        for i in range(2):
            slot = s_ref[1] ^ ORDER[4 * (group // 2) + 2 * i + group % 2]
            there = pl.ds(pl.multiple_of((slot // 2) * rows, 16), rows)
            out_ref[there, pl.ds(pl.multiple_of((slot % 2) * cols, 128), cols)] = ref[i]


def gated(normed, act_back, w_in, w_down, act_ref, gb_ref, width):
    both = dot(normed, w_in, NT)
    gate, linear = both[:, :width], both[:, width:]
    cdf = 0.5 * (1.0 + lax.erf(gate * math.sqrt(0.5)))
    slope = cdf + gate * (jnp.exp(-0.5 * gate * gate) * (1.0 / math.sqrt(2.0 * math.pi)))
    gelu = gate * cdf
    act_ref[...] = (gelu * linear).astype(BF16)
    gb_ref[:, :width] = (act_back * linear * slope).astype(BF16)
    gb_ref[:, width:] = (act_back * gelu).astype(BF16)
    return dot(act_ref[...], w_down), dot(gb_ref[...], w_in)


def begin_kernel(
    s_ref, tok_ref, cot_ref, c0, c1, c2, c3, w_ref, dw_ref, res_ref, context_ref, cot_out, back_ref
):
    z = s_ref[0]
    for half in range(2):
        base = (z if half == 0 else z ^ 1) * BLOCK
        there = pl.ds(pl.multiple_of(base, BLOCK), BLOCK)
        rows = slice(half * BLOCK, (half + 1) * BLOCK)
        mine = slice(half * COLS, (half + 1) * COLS)
        res_ref[rows, :] = tok_ref[there, :].astype(F32) + dot(c0[:, mine], w_ref[...])
        for k, c in enumerate((c1, c2, c3)):
            context_ref[k, rows, :] = c[:, mine]
        cot_out[rows, :] = cot_ref[there, :]
    back_ref[...] = dot(cot_out[...], dw_ref[...], NT)


def middle_kernel(
    s_ref, part_ref, context_ref, cot_ref, act_back_ref, w_ref, here_ref, there_ref, gain_ref, gw_ref, dw_ref,
    res_ref, normed_ref, act_ref, gb_ref, branch_ref, back_ref, wo_ref,
):
    wo_ref[0] = w_ref[...]
    few = COLS // 4
    pieces = ((0, here_ref, 0), (2, here_ref, 1), (1, there_ref, 0), (3, there_ref, 1))
    for slot, ref, i in pieces:
        there = pl.ds(pl.multiple_of((s_ref[1] % 4 ^ slot) * few, 16), few)
        for k in range(3):
            for side in range(2):
                first = (2 * k + side) * few
                lanes = slice(side * (D // 2), (side + 1) * (D // 2))
                wo_ref[k + 1, there, lanes] = ref[i, first : first + few, :]
    residual = part_ref[...]
    for k in range(3):
        residual += dot(context_ref[k], wo_ref[k + 1])
    res_ref[...] = residual[:BLOCK]
    unit, _ = normalize(residual)
    normed_ref[...] = (unit * gain_ref[...]).astype(BF16)
    branch_ref[...], back_ref[...] = gated(
        normed_ref[BLOCK:, :], act_back_ref[BLOCK:, :], gw_ref[...], dw_ref[...], act_ref, gb_ref, dw_ref.shape[0]
    )


def partner_kernel(
    s_ref, normed_ref, cot_ref, branch_in, back_in, f0, f1, f2, f3,
    act_ref, gb_ref, branch_ref, back_ref, other_ref,
):
    width = act_ref.shape[1]
    place_slots(s_ref, (f0, f1, f2, f3), other_ref)
    branch, back = gated(
        normed_ref[BLOCK:, :], dot(cot_ref[BLOCK:, :], other_ref[2 * width : 3 * width, :], NT), other_ref[: 2 * width, :],
        other_ref[2 * width : 3 * width, :], act_ref, gb_ref, width,
    )
    branch_ref[...] = (branch_in[...] + branch).astype(BF16)
    back_ref[...] = (back_in[...] + back).astype(BF16)


def own_kernel(
    s_ref, normed_ref, cot_ref, act_back_ref, res_ref, gw_ref, dw_ref, other_ref,
    act_par, gb_par, act_par_two, gb_par_two,
    branch_ref, back_ref, whole_ref,
    act_one, gb_one, act_two, gb_two,
):
    width = act_par.shape[1]
    normed, cot = normed_ref[:BLOCK, :], cot_ref[:BLOCK, :]
    w_down = other_ref[2 * width : 3 * width, :]
    branch, back = gated(normed, act_back_ref[:BLOCK, :], gw_ref[...], dw_ref[...], act_one, gb_one, width)
    more, back_more = gated(normed, dot(cot, w_down, NT), other_ref[: 2 * width, :], w_down, act_two, gb_two, width)
    branch_ref[...] = res_ref[...] + branch + more
    back_ref[...] = back + back_more
    half = whole_ref.shape[1] // 2
    shards = ((act_one, gb_one, act_par, gb_par), (act_two, gb_two, act_par_two, gb_par_two))
    for shard, (act, gb, act_there, gb_there) in enumerate(shards):
        at = shard * half
        part = dot(normed, gb[...], TN) + dot(normed_ref[BLOCK:, :], gb_there[...], TN)
        whole_ref[:, at : at + 2 * width] = part.astype(BF16)
        part = dot(cot, act[...], TN) + dot(cot_ref[BLOCK:, :], act_there[...], TN)
        whole_ref[:, at + 2 * width : at + 3 * width] = part.astype(BF16)
        whole_ref[:, at + 3 * width : at + half] = jnp.zeros((D, half - 3 * width), BF16)


def finish_kernel(keep_ref, r1, r2, r3, geglu_ref, down_ref, out_ref, pad_ref):
    half = r2.shape[1] - COLS
    rows, width = geglu_ref.shape[1:]
    ff = keep_ref[:, :half] + r2[:, :half].astype(F32)
    geglu_ref[0] = ff[:, :width]
    geglu_ref[1] = ff[:, width : 2 * width]
    out = keep_ref[:, half:] + r1[...].astype(F32) + r2[:, half:].astype(F32) + r3[...].astype(F32)
    pad_ref[...] = jnp.zeros_like(pad_ref)
    pad_ref[:rows, :width] = ff[:, 2 * width : 3 * width]
    down_ref[...] = jnp.transpose(pad_ref[...])[:width, :rows]
    pad_ref[:rows, :COLS] = out
    out_ref[...] = jnp.transpose(pad_ref[...])[:COLS, :rows]


def qkv_sum_kernel(parts_ref, grad_ref, gains_ref):
    rows = grad_ref.shape[1]
    total = jnp.sum(parts_ref[...].astype(F32), axis=0)
    for s in range(3):
        grad_ref[s] = total[:rows, s * COLS : (s + 1) * COLS]
    for gain in range(2):
        for side in range(2):
            first = rows + 6 * gain + side
            part = total[first : first + 1] + total[first + 2 : first + 3] + total[first + 4 : first + 5]
            gains_ref[gain : gain + 1, side * (D // 2) : (side + 1) * (D // 2)] = part[:, : D // 2]


def residual_kernel(
    keep_ref, recv_ref, res_ref, gain_ref, cot_ref, wo_ref,
    back_ref, low_ref, gain_out, b0, b1, b2, b3,
):
    unit, inverse = normalize(res_ref[...])
    upstream = keep_ref[...] + recv_ref[...].astype(F32)
    back = cot_ref[:BLOCK, :].astype(F32) + norm_back(upstream, unit, inverse, gain_ref[...])
    back_ref[...] = back
    gain_out[...] = jnp.sum(upstream * unit, axis=0, keepdims=True)
    low = back.astype(BF16)
    low_ref[...] = low
    for k, out in enumerate((b0, b1, b2, b3)):
        part = dot(low, wo_ref[k], NT).astype(BF16)
        out[:, :COLS] = part[: BLOCK // 2]
        out[:, COLS:] = part[BLOCK // 2 :]


def output_grad_kernel(s_ref, low_ref, c0, c1, c2, c3, ff_ref, even_ref, odd_ref, whole_ref):
    for k, c in enumerate((c0, c1, c2, c3)):
        whole_ref[:, k * COLS : (k + 1) * COLS] = dot(low_ref[...], c[:, :COLS], TN).astype(BF16)
    rows, ff = even_ref.shape[1], ff_ref.shape[1]
    for i in range(8):
        there = pl.ds(pl.multiple_of((s_ref[1] ^ ORDER[i]) * rows, 16), rows)
        out = even_ref.at[i] if i < 4 else odd_ref.at[i - 4]
        out[:, :ff] = ff_ref[there, :]
        out[:, ff:] = whole_ref[there, :]


def collect_kernel(own_ref, r1, r2, r3, keep_ref, s1, s2, s3):
    total = own_ref[...] + r1[...].astype(F32) + r2[...].astype(F32) + r3[...].astype(F32)
    half = keep_ref.shape[1] - COLS
    keep_ref[:, :half] = total[:, :half]
    keep_ref[:, half:] = total[:, 2 * half : 2 * half + COLS]
    s2[:, :half] = total[:, half : 2 * half].astype(BF16)
    for k, out in ((1, s1), (2, s2), (3, s3)):
        first = 2 * half + k * COLS
        out[:, out.shape[1] - COLS :] = total[:, first : first + COLS].astype(BF16)


def pack_kernel(s_ref, w_in_ref, w_down_ref, w_out_ref, out_ref, ff_ref, sems, out_sems):
    slot = s_ref[1]
    cols = pl.ds(pl.multiple_of((slot % 2) * (D // 2), 128), D // 2)
    few = out_ref.shape[0] // 2
    here = pl.ds(pl.multiple_of(slot % 4 * few, 16), few)
    copies = [
        pltpu.make_async_copy(
            w_out_ref.at[here, side * (D // 2) : (side + 1) * (D // 2)],
            out_ref.at[side * few : (side + 1) * few, :],
            out_sems.at[side],
        )
        for side in range(2)
    ]
    for copy in copies:
        copy.start()
    n_in, n_down = w_in_ref.shape[0] // PART, w_down_ref.shape[0] // PART
    parts = ff_ref.shape[0] // PART
    for i in range(parts):
        at = (slot // 2) * parts + i
        there = ff_ref.at[i * PART : (i + 1) * PART, :]

        def fetch(ref, first):
            rows = pl.ds(pl.multiple_of((at - first) * PART, PART), PART)
            return pltpu.make_async_copy(ref.at[rows, cols], there, sems.at[i])

        @pl.when(at < n_in)
        def _():
            fetch(w_in_ref, 0).start()

        @pl.when((at >= n_in) & (at < n_in + n_down))
        def _():
            fetch(w_down_ref, n_in).start()

        @pl.when(at >= n_in + n_down)
        def _():
            there[...] = jnp.zeros(there.shape, BF16)

    for copy in copies:
        copy.wait()
    for i in range(parts):
        there = ff_ref.at[i * PART : (i + 1) * PART, :]

        @pl.when((slot // 2) * parts + i < n_in + n_down)
        def _():
            pltpu.make_async_copy(w_in_ref.at[:PART, : D // 2], there, sems.at[i]).wait()


def arrived_kernel(s_ref, f1, f2, f3, out_ref):
    few = f1.shape[0]
    for i, piece in enumerate((f1, f2, f3)):
        out_ref[i * few : (i + 1) * few, :] = piece[...]


def pair_kernel(s_ref, a0, a1, out_ref):
    out_ref[0] = a0[...]
    out_ref[1] = a1[...]


def backward_steps(
    mirror, steps, seg_ref, segc_ref, q_ref, k_ref, v_ref, lse_ref, back_ref, dq_ref, dk_ref, dv_ref
):
    last = LEN // QB - 1
    head = lane_head(QB)
    scale = jnp.asarray(1.0 / math.sqrt(HEAD), BF16)

    def products(step):
        low, high = static_window(step)
        i = jnp.where(mirror == 1, last - step, step)
        rows = pl.ds(pl.multiple_of(i * QB, QB), QB)
        keys = jnp.where(mirror == 1, LEN - high, low)
        keys = pl.ds(pl.multiple_of(keys, QB), high - low)
        stacked = by_head(q_ref[rows, :] * scale, head)
        upstream = by_head(back_ref[rows, :], head)
        scores = dot(stacked, k_ref[keys, :], NT)
        prob_back = dot(upstream, v_ref[keys, :], NT)
        return rows, keys, stacked, upstream, scores, prob_back

    ahead = products(steps[0])
    for step in steps:
        rows, keys, stacked, upstream, scores, prob_back = ahead
        if step + 1 in steps:
            ahead = products(step + 1)
        same = segc_ref[rows, 0:1] == seg_ref[0:1, keys].astype(F32)
        probs, grads = [], []
        for h in range(HEADS_HERE):
            at = slice(h * QB, (h + 1) * QB)
            prob = jnp.exp(jnp.where(same, scores[at], NEGATIVE) - lse_ref[rows, h : h + 1])
            inner = jnp.sum(prob * prob_back[at], axis=-1, keepdims=True)
            probs.append(prob.astype(BF16))
            grads.append((prob * (prob_back[at] - inner)).astype(BF16))
        prob = jnp.concatenate(probs, axis=0)
        grad = jnp.concatenate(grads, axis=0)
        dv_ref[:, keys] += dot(upstream, prob, TN)
        dk_ref[:, keys] += dot(stacked, grad, TN)
        dq_ref[rows, :] = merge_heads(dot(grad, k_ref[keys, :]), head) * (1.0 / math.sqrt(HEAD))


def rows_back(base, dq_ref, dk_ref, dv_ref, trig_ref, w_ref, qkv_ref):
    rows = pl.ds(pl.multiple_of(base, BLOCK), BLOCK)
    trig = trig_ref[rows, :]
    total = None
    for part, grad_ref in enumerate((dq_ref, dk_ref, dv_ref)):
        g = jnp.transpose(grad_ref[:, rows]) if part else grad_ref[rows, :]
        if part < 2:
            g = turn(g, trig, -1.0)
        low = g[:, :COLS].astype(BF16)
        qkv_ref[:, part * COLS : (part + 1) * COLS] = low
        product = dot(low, w_ref[part])
        total = product if total is None else total + product
    return total


def backward_far_kernel(
    s_ref, seg_ref, segc_ref, q_ref, k_ref, v_ref, lse_ref, trig_ref, b0, b1, b2, b3, w_ref,
    n2, n3, qkv_ref, back_ref, dq_ref, dk_ref, dv_ref,
):
    z = s_ref[0]
    pair = z // 2
    half = BLOCK // 2
    back_ref[:, COLS:] = jnp.zeros((LEN, LANES - COLS), BF16)
    for k, b in enumerate((b0, b1, b2, b3)):
        base = pl.multiple_of((z ^ k) * BLOCK, BLOCK)
        back_ref[pl.ds(base, half), :COLS] = b[:, :COLS]
        back_ref[pl.ds(pl.multiple_of(base + half, half), half), :COLS] = b[:, COLS:]
    dk_ref[...] = jnp.zeros_like(dk_ref)
    dv_ref[...] = jnp.zeros_like(dv_ref)
    refs = (seg_ref, segc_ref, q_ref, k_ref, v_ref, lse_ref, back_ref, dq_ref, dk_ref, dv_ref)
    steps = LEN // QB
    reach = DOC // QB
    backward_steps(1 - pair, range(steps // 2 + reach), *refs)
    for k, out in ((2, n2), (3, n3)):
        at = qkv_ref.at[(k - 2) * BLOCK : (k - 1) * BLOCK]
        part = rows_back((z ^ k) * BLOCK, dq_ref, dk_ref, dv_ref, trig_ref, w_ref, at)
        out[...] = part.astype(out.dtype)


def add_kernel(mine_ref, recv_ref, out_ref):
    out_ref[...] = (mine_ref[...] + recv_ref[...].astype(F32)).astype(out_ref.dtype)


def backward_near_kernel(
    s_ref, seg_ref, segc_ref, q_ref, k_ref, v_ref, lse_ref, trig_ref, back_ref, dq_in, dk_in, dv_in,
    w_ref, n0, n1, qkv_ref, dq_ref, dk_ref, dv_ref,
):
    z = s_ref[0]
    pair = z // 2
    dq_ref[...] = dq_in[...]
    dk_ref[...] = dk_in[...]
    dv_ref[...] = dv_in[...]
    refs = (seg_ref, segc_ref, q_ref, k_ref, v_ref, lse_ref, back_ref, dq_ref, dk_ref, dv_ref)
    steps = LEN // QB
    reach = DOC // QB
    backward_steps(pair, range(steps // 2 - reach), *refs)
    for k, out in ((0, n0), (1, n1)):
        at = qkv_ref.at[k * BLOCK : (k + 1) * BLOCK]
        part = rows_back((z ^ k) * BLOCK, dq_ref, dk_ref, dv_ref, trig_ref, w_ref, at)
        out[...] = part.astype(out.dtype)


def qkv_grad_kernel(
    s_ref, normed_ref, near_ref, far_ref, w_ref, gain_ref, gain_two_ref, out_ref, whole_ref, rows_ref
):
    for k in range(NARROW):
        base = pl.multiple_of((s_ref[0] ^ k) * BLOCK, BLOCK)
        rows_ref[k * BLOCK : (k + 1) * BLOCK, :] = normed_ref[pl.ds(base, BLOCK), :]
    pair = 2 * BLOCK
    total = None
    for s in range(3):
        cols = slice(s * COLS, (s + 1) * COLS)
        part = dot(rows_ref[:pair, :], near_ref[:, cols], TN)
        part += dot(rows_ref[pair:, :], far_ref[:, cols], TN)
        whole_ref[:, cols] = part.astype(BF16)
        weighted = part * jnp.transpose(w_ref[s].astype(F32))
        total = weighted if total is None else total + weighted
    column = jnp.broadcast_to(jnp.sum(total, axis=1, keepdims=True), (D, 128))
    gains = (jnp.transpose(column)[:1, :] / gain_ref[...], gain_two_ref[...])
    extra = jnp.zeros((GAIN_ROWS, D // 2), F32)
    row = lax.broadcasted_iota(jnp.int32, extra.shape, 0)
    at = 0
    for gain in gains:
        rest = gain
        for _ in range(3):
            term = rest.astype(BF16).astype(F32)
            rest = rest - term
            for side in range(2):
                extra = jnp.where(row == at, term[:, side * (D // 2) : (side + 1) * (D // 2)], extra)
                at += 1
    blocks, rows, cols = out_ref.shape
    rows -= GAIN_ROWS
    for i in range(blocks):
        if rows % 16 == 0:
            out_ref[i, :rows, :] = whole_ref[i * rows : (i + 1) * rows, :]
            out_ref[i, rows:, :] = jnp.zeros((GAIN_ROWS, cols), BF16)
            out_ref[i, rows:, : D // 2] = extra.astype(BF16)
        else:
            lines = [whole_ref[i * rows : (i + 1) * rows, :].astype(F32)]
            pad = jnp.zeros((GAIN_ROWS, cols - D // 2), F32)
            lines.append(jnp.concatenate([extra, pad], axis=1))
            out_ref[i] = jnp.concatenate(lines, axis=0).astype(BF16)


def final_kernel(
    s_ref, tok_ref, gain_ref, back_ref, n0, n1, n2, own_ref, branch_ref, out_ref, layer_ref
):
    upstream = n0[...] + n1[...].astype(F32) + n2[...].astype(F32)
    rows = pl.ds(pl.multiple_of(s_ref[0] * BLOCK, BLOCK), BLOCK)
    unit, inverse = normalize(tok_ref[rows, :].astype(F32))
    out_ref[...] = back_ref[...] + norm_back(upstream, unit, inverse, gain_ref[...])
    layer_ref[...] = (own_ref[...] + branch_ref[...].astype(F32)).astype(BF16)


def fold_kernel(even_ref, recv_ref, own_ref, s1_ref, s2_ref, s3_ref):
    for i, out in enumerate((own_ref, s1_ref, s2_ref, s3_ref)):
        out[...] = (even_ref[i].astype(F32) + recv_ref[i].astype(F32)).astype(out.dtype)


def along_narrow(x, k):
    return lax.ppermute(x, "narrow", [(i, i ^ k) for i in range(NARROW)])


def along_wide(x, k):
    return lax.ppermute(x, "wide", [(i, i ^ k) for i in range(lax.axis_size("wide"))])


def in_hbm(x):
    return pltpu.with_memory_space_constraint(x, pltpu.HBM)


def tie(x, *others):
    return lax.optimization_barrier((x, *others))[0]


def quarter_slice(x, slot):
    rows, cols = x.shape[-2] // 4, x.shape[-1] // 2
    x = lax.dynamic_slice_in_dim(x, (slot // 2) * rows, rows, x.ndim - 2)
    return lax.dynamic_slice_in_dim(x, (slot % 2) * cols, cols, x.ndim - 1)


def all_slots(x, hops):
    whole = jnp.stack([along_narrow(x, k) for k in hops])
    slots = jnp.stack([quarter_slice(whole, i) for i in ORDER])
    return slots[:4], slots[4:]


def sum_wide(x):
    return jnp.sum(lax.all_to_all(x, "wide", 0, 0).astype(F32), axis=0)


def per_device(
    tokens, segments, first_gain, qkv_weight, output_weight, second_gain, geglu_weight, down_weight,
    cotangent,
):
    size = lax.axis_size("wide")
    plane = size == 8
    mine = lax.axis_index("wide").astype(jnp.int32)
    z = lax.axis_index("narrow").astype(jnp.int32)
    scalars = jnp.stack([z, mine if plane else jnp.zeros_like(mine)])
    hidden = geglu_weight.shape[2]
    padded = -(-3 * hidden // 64) * 64
    rows_d = D // size
    gain_one = first_gain.reshape(1, D)
    gain_two = second_gain.reshape(1, D)
    w_qkv = qkv_weight.transpose(0, 2, 1)
    w_in = geglu_weight.transpose(0, 2, 1).reshape(2 * hidden, D)

    few, many = COLS // 4, padded // 4
    now = scalars
    if plane:
        slot_out, slot_ff = call(
            pack_kernel,
            (scalars, in_hbm(w_in), in_hbm(down_weight), in_hbm(output_weight)),
            (sds((2 * few, D // 2), BF16), sds((many, D // 2), BF16)),
            [pltpu.SemaphoreType.DMA((many // PART,)), pltpu.SemaphoreType.DMA((2,))],
            place=pltpu.HBM,
        )
        out_fetched = [along_narrow(slot_out, k) for k in (1, 2, 3)]
        ff_fetched = along_narrow(slot_ff, 2)
    wide_rows = sds((LEN, LANES), BF16)
    q, k, v, normed_one, trig, segc = call(
        project_kernel,
        (tokens, segments, gain_one, w_qkv, jnp.asarray(rotary_table())),
        (wide_rows, wide_rows, wide_rows, sds((LEN, D), BF16), sds((LEN, 2 * 128), F32),
         sds((LEN, 128), F32)),
        [pltpu.VMEM((LEN // 4, LANES), F32)],
        scalars=0,
    )
    piece = sds((BLOCK, 2 * COLS), BF16)
    c0, c1, c2, c3, lse = call(
        attend_kernel,
        (now, segments, segc, q, k, v),
        (piece, piece, piece, piece, sds((LEN, 128), F32)),
        [pltpu.VMEM((NARROW, BLOCK, 2 * COLS), BF16)],
    )
    context = (c0, *(along_narrow(c, k) for k, c in ((1, c1), (2, c2), (3, c3))))
    if plane:
        ff0 = tie(ff_fetched, lse)
        slots_two = sds((2, many, D // 2), BF16)
        (out0,) = call(
            arrived_kernel, (tie(scalars, lse), *out_fetched), (sds((6 * few, D // 2), BF16),)
        )
        (out_here,) = call(
            pair_kernel, (scalars, out0, along_wide(out0, 2)), (sds((2, 6 * few, D // 2), BF16),)
        )
        out_there = along_wide(out_here, 1)
        (ff_pair,) = call(pair_kernel, (scalars, ff0, along_wide(ff0, 4)), (slots_two,))
        ff_x = along_wide(ff_pair, 2)
        ff_slots = (ff_pair, ff_x, along_wide(ff_pair, 1), along_wide(ff_x, 1))
    else:
        everything = jnp.concatenate(
            [w_in, down_weight, jnp.zeros((padded - 3 * hidden, D), BF16)], axis=0
        )
        even, odd = (x[:, 0] for x in all_slots(everything, (2,)))
        ff_slots = (even[::2], even[1::2], odd[::2], odd[1::2])
        others = jnp.stack([along_narrow(output_weight, k) for k in (1, 2, 3)])
        others = others.reshape(3, 4, few, 2, D // 2).transpose(1, 0, 3, 2, 4)
        others = others.reshape(4, 6 * few, D // 2)
        out_here, out_there = others[::2], others[1::2]

    whole = sds((2 * BLOCK, D), F32)
    own = sds((BLOCK, D), F32)
    own_low = sds((BLOCK, D), BF16)
    part, contexts, cot, act_back = call(
        begin_kernel,
        (scalars, tokens, cotangent, *context, output_weight, down_weight),
        (whole, sds((3, 2 * BLOCK, COLS), BF16), sds((2 * BLOCK, D), BF16),
         sds((2 * BLOCK, hidden), F32)),
    )
    part_act, part_gb = sds((BLOCK, hidden), BF16), sds((BLOCK, 2 * hidden), BF16)
    res, normed_two, act_par, gb_par, branch, back, wo = call(
        middle_kernel,
        (scalars, part, contexts, cot, act_back, output_weight, out_here, out_there, gain_two, w_in,
         down_weight),
        (own, sds((2 * BLOCK, D), BF16), part_act, part_gb, own, own, sds((NARROW, COLS, D), BF16)),
    )
    act_par_two, gb_par_two, out_send, send, other = call(
        partner_kernel,
        (scalars, normed_two, cot, branch, back, *ff_slots),
        (part_act, part_gb, own_low, own_low, sds((padded, D), BF16)),
    )
    recv = along_narrow(send, 1)
    half = -(-3 * hidden // 128) * 128
    out_keep, keep, ff_part = call(
        own_kernel,
        (scalars, normed_two, cot, act_back, res, w_in, down_weight, other, act_par, gb_par,
         act_par_two, gb_par_two),
        (own, own, sds((D, 2 * half), BF16)),
        [pltpu.VMEM((BLOCK, hidden), BF16), pltpu.VMEM((BLOCK, 2 * hidden), BF16)] * 2,
    )
    low_piece = sds((BLOCK // 2, 2 * COLS), BF16)
    back, low, gain_two_part, b0, b1, b2, b3 = call(
        residual_kernel,
        (keep, recv, res, gain_two, cot, wo),
        (own, own_low, sds((1, D), F32), low_piece, low_piece, low_piece, low_piece),
        scalars=0,
    )
    upstream = (b0, *(along_narrow(b, k) for k, b in ((1, b1), (2, b2), (3, b3))))
    grad_cols = 2 * half + NARROW * COLS
    even_part, odd_part = call(
        output_grad_kernel,
        (scalars, low, *context, ff_part),
        (sds((4, D // 8, grad_cols), BF16),) * 2,
        [pltpu.VMEM((D, NARROW * COLS), BF16)],
    )
    block = sds((rows_d, grad_cols), F32)
    if plane:
        block_low = sds((rows_d, grad_cols), BF16)
        grad_sum, *grad_sends = call(
            fold_kernel,
            (even_part, along_wide(odd_part, 1)),
            (block, block_low, block_low, block_low),
            scalars=0,
            far=(0,),
        )
        grad_recv = [along_wide(x, 2 * (i + 1)) for i, x in enumerate(grad_sends)]
        now = tie(scalars, *grad_sends)
    else:
        blocks = jnp.stack([even_part, odd_part], axis=1)
        grad_sum = sum_wide(blocks.reshape(size, rows_d, grad_cols))
        grad_recv, grad_sends = [jnp.zeros((rows_d, grad_cols), BF16)] * 3, ()
        now = tie(scalars, even_part)

    rows_f32 = sds((LEN, LANES), F32)
    columns_f32 = sds((LANES, LEN), F32)
    pair_qkv = sds((2 * BLOCK, 3 * COLS), BF16)
    n2, n3, qkv_far, back_rows, *grads = call(
        backward_far_kernel,
        (now, segments, segc, q, k, v, lse, trig, *upstream, w_qkv),
        (own, own_low, pair_qkv, wide_rows, rows_f32, columns_f32, columns_f32),
    )
    exchanged = along_narrow(n3, 1)
    branch_recv = along_narrow(tie(out_send, upstream[1], *grad_sends), 1)
    n0, n1, qkv_near = call(
        backward_near_kernel,
        (scalars, segments, segc, q, k, v, lse, trig, back_rows, *grads, w_qkv),
        (own, own_low, pair_qkv),
        [pltpu.VMEM((LEN, LANES), F32)] + [pltpu.VMEM((LANES, LEN), F32)] * 2,
    )
    (qkv_part,) = call(
        qkv_grad_kernel,
        (tie(scalars, n1, branch_recv), normed_one, qkv_near, qkv_far, w_qkv, gain_one, gain_two_part),
        (sds((size, rows_d + GAIN_ROWS, 3 * COLS), BF16),),
        [pltpu.VMEM((D, 3 * COLS), BF16), pltpu.VMEM((LEN, D), BF16)],
    )
    near_recv = along_narrow(n1, 1)
    (pair_sum,) = call(add_kernel, (tie(n2, qkv_part), exchanged), (own_low,), scalars=0)
    far_recv = along_narrow(pair_sum, 2)
    qkv_grad, gains = call(
        qkv_sum_kernel,
        (lax.all_to_all(qkv_part, "wide", 0, 0),),
        (sds((3, rows_d, COLS), F32), sds((2, D), F32)),
        scalars=0,
    )
    few_cols = sds((rows_d, COLS), BF16)
    grad_keep, *there = call(
        collect_kernel,
        (in_hbm(tie(grad_sum, near_recv, pair_sum)), *grad_recv),
        (sds((rows_d, half + COLS), F32), few_cols, sds((rows_d, half + COLS), BF16), few_cols),
        scalars=0,
    )
    there = [along_narrow(x, k) for k, x in zip((1, 2, 3), there)]
    tokens_grad, layer_out = call(
        final_kernel,
        (scalars, tokens, gain_one, back, n0, near_recv, far_recv, out_keep, branch_recv),
        (own, own_low),
    )
    gains = gains + along_narrow(gains, 1) + along_narrow(gains, 2) + along_narrow(gains, 3)
    geglu_grad, down_grad, out_grad = call(
        finish_kernel,
        (tie(grad_keep, tokens_grad), *there),
        (sds((2, rows_d, hidden), F32), sds((hidden, rows_d), F32), sds((COLS, rows_d), F32)),
        [pltpu.VMEM((128, -(-hidden // 128) * 128), F32)],
        scalars=0,
    )
    return (
        layer_out, tokens_grad, gains[0], qkv_grad, out_grad, gains[1], geglu_grad, down_grad,
    )


def solution(mesh):
    return jax.shard_map(
        per_device,
        mesh=mesh,
        in_specs=(
            P("wide", None),
            P("wide", None),
            P(),
            P(None, None, "narrow"),
            P("narrow", None),
            P(),
            P(None, None, "narrow"),
            P("narrow", None),
            P("wide", None),
        ),
        out_specs=(
            P(("wide", "narrow"), None),
            P(("wide", "narrow"), None),
            P(),
            P(None, "wide", "narrow"),
            P("narrow", "wide"),
            P(),
            P(None, "wide", "narrow"),
            P("narrow", "wide"),
        ),
        check_vma=False,
    )
```

```python
import functools
import math

import jax
import jax.numpy as jnp
import numpy as np
from jax import lax
from jax.experimental import pallas as pl
from jax.experimental.pallas import tpu as pltpu
from jax.sharding import PartitionSpec as P

HEAD = 64
LEN = 1024
D = 768
HEADS_HERE = 3
COLS = HEADS_HERE * HEAD
LANES = 256
DOC = 256
QB = 128
WINDOW = QB + 2 * DOC
EPSILON = 1e-05
ROPE_BASE = 160000.0
NARROW = 4
BLOCK = LEN // NARROW
ORDER = (0, 2, 4, 6, 1, 3, 5, 7)
F32 = jnp.float32
GAIN_ROWS = 16
BF16 = jnp.bfloat16
NEGATIVE = -1e30
MIB = 1024 * 1024
COST = {
    "finish_kernel": 1,
    "qkv_sum_kernel": 1,
    "pack_kernel": 1,
    "arrived_kernel": 1,
    "pair_kernel": 1,
    "begin_kernel": 100,
    "project_kernel": 6,
    "attend_kernel": 100,
    "middle_kernel": 5,
    "partner_kernel": 3,
    "own_kernel": 10,
    "residual_kernel": 100,
    "output_grad_kernel": 2,
    "fold_kernel": 2,
    "backward_far_kernel": 100,
    "backward_near_kernel": 100,
    "add_kernel": 100,
    "qkv_grad_kernel": 1,
    "collect_kernel": 1,
    "final_kernel": 100,
}

NN = (((1,), (0,)), ((), ()))
NT = (((1,), (1,)), ((), ()))
TN = (((0,), (0,)), ((), ()))


def dot(a, b, dims=NN):
    return lax.dot_general(a, b, dims, preferred_element_type=F32)


def call(body, ins, outs, scratch=(), scalars=1, place=pltpu.VMEM, far=()):
    name = getattr(body, "func", body).__name__
    specs = [pl.BlockSpec(memory_space=pltpu.SMEM)] * scalars
    specs += [pl.BlockSpec(memory_space=place)] * (len(ins) - scalars)
    size = sum(math.prod(x.shape) * x.dtype.itemsize for x in (*ins, *outs))
    held = sum(math.prod(x.shape) * x.dtype.itemsize for x in scratch if hasattr(x.dtype, "itemsize"))
    return pl.pallas_call(
        body,
        name=name,
        out_shape=tuple(pltpu.HBM(o.shape, o.dtype) if i in far else sds(o.shape, o.dtype) for i, o in enumerate(outs)),
        in_specs=specs,
        out_specs=tuple(pl.BlockSpec(memory_space=pltpu.VMEM) for _ in outs),
        scratch_shapes=list(scratch),
        compiler_params=pltpu.CompilerParams(vmem_limit_bytes=size + size // 4 + held + 8 * MIB),
        cost_estimate=pl.CostEstimate(flops=COST[name] * 10**9, bytes_accessed=size, transcendentals=0),
    )(*ins)


def sds(shape, dtype):
    return jax.ShapeDtypeStruct(shape, dtype)


def rotary_table():
    position = np.arange(DOC, dtype=np.float64)
    frequency = ROPE_BASE ** (-2.0 * np.arange(HEAD // 2, dtype=np.float64) / HEAD)
    angle = position[:, None] * frequency[None, :]
    cosine, sine = np.cos(angle), np.sin(angle)
    table = np.zeros((DOC, 2 * 128), np.float32)
    for h in range(2):
        base = h * HEAD
        table[:, base : base + 32] = cosine
        table[:, base + 32 : base + 64] = cosine
        table[:, 128 + base : 128 + base + 32] = -sine
        table[:, 128 + base + 32 : 128 + base + 64] = sine
    high = table.astype(jnp.bfloat16)
    low = (table - high.astype(np.float32)).astype(jnp.bfloat16)
    return np.stack([high, low])


def normalize(values):
    centre = values - jnp.mean(values, axis=-1, keepdims=True)
    spread = jnp.mean(centre * centre, axis=-1, keepdims=True)
    inverse = lax.rsqrt(spread + EPSILON)
    return centre * inverse, inverse


def norm_back(upstream, unit_rows, inverse, gain):
    scaled = upstream * gain
    first_mean = jnp.mean(scaled, axis=-1, keepdims=True)
    second_mean = jnp.mean(scaled * unit_rows, axis=-1, keepdims=True)
    return inverse * (scaled - first_mean - unit_rows * second_mean)


def lane_head(rows):
    return lax.broadcasted_iota(jnp.int32, (rows, LANES), 1) // HEAD


def swap_halves(x):
    lane = lax.broadcasted_iota(jnp.int32, x.shape, 1)
    return jnp.where(
        lane % HEAD < HEAD // 2,
        pltpu.roll(x, LANES - HEAD // 2, 1),
        pltpu.roll(x, HEAD // 2, 1),
    )


def turn(x, trig, sign):
    swapped = swap_halves(x)
    cosine, sine = trig[:, :128], sign * trig[:, 128:]
    parts = [
        x[:, i : i + 128] * cosine + swapped[:, i : i + 128] * sine for i in range(0, LANES, 128)
    ]
    return jnp.concatenate(parts, axis=1)


def by_head(block, head):
    return jnp.concatenate(
        [jnp.where(head == h, block, jnp.zeros_like(block)) for h in range(HEADS_HERE)], axis=0
    )


def merge_heads(stacked, head):
    parts = jnp.split(stacked, HEADS_HERE, axis=0)
    return jnp.where(head == 0, parts[0], jnp.where(head == 1, parts[1], parts[2]))


def static_window(i):
    reach = DOC // QB
    return max(0, i - reach) * QB, min(LEN // QB, i + reach + 1) * QB


def project_kernel(
    tok_ref, seg_ref, gain_ref, w_ref, table_ref,
    q_ref, k_ref, v_ref, normed_ref, trig_ref, segc_ref,
    proj_ref,
):
    seg = jnp.broadcast_to(seg_ref[...].astype(F32), (8, LEN))
    index = lax.broadcasted_iota(jnp.int32, (8, LEN), 1)
    first = jnp.where(seg != pltpu.roll(seg, 1, 1), index, 0)
    first = jnp.where(index == 0, 0, first).astype(F32)
    shift = 1
    while shift < DOC:
        first = jnp.maximum(first, jnp.where(index >= shift, pltpu.roll(first, shift, 1), 0.0))
        shift *= 2
    place = index.astype(F32) - first
    segc_ref[...] = jnp.transpose(jnp.broadcast_to(seg[:1], (128, LEN)))
    placec = jnp.transpose(jnp.broadcast_to(place[:1], (128, LEN)))
    lane = lax.broadcasted_iota(jnp.int32, (LEN, 128), 1).astype(F32)
    hot = jnp.concatenate(
        [jnp.where(placec == lane + 128.0 * j, 1.0, 0.0) for j in range(DOC // 128)], axis=1
    ).astype(BF16)
    trig_ref[...] = dot(hot, table_ref[0]) + dot(hot, table_ref[1])

    step = LEN // 4
    proj_ref[:, COLS:] = jnp.zeros((step, LANES - COLS), F32)
    for i in range(4):
        rows = slice(i * step, (i + 1) * step)
        unit, _ = normalize(tok_ref[rows, :].astype(F32))
        normed = (unit * gain_ref[...]).astype(BF16)
        normed_ref[rows, :] = normed
        for s, out in enumerate((q_ref, k_ref, v_ref)):
            proj_ref[:, :COLS] = dot(normed, w_ref[s], NT)
            x = proj_ref[...]
            out[rows, :] = (turn(x, trig_ref[rows, :], 1.0) if s < 2 else x).astype(BF16)


def attend_kernel(
    s_ref, seg_ref, segc_ref, q_ref, k_ref, v_ref, c0_ref, c1_ref, c2_ref, c3_ref, lse_ref, ctx_ref
):
    z = s_ref[0]
    head = lane_head(QB)
    column = lax.broadcasted_iota(jnp.int32, (QB, 128), 1)

    def products(i):
        low, high = static_window(i)
        block = q_ref[i * QB : (i + 1) * QB, :] * jnp.asarray(1.0 / math.sqrt(HEAD), BF16)
        return dot(by_head(block, head), k_ref[low:high, :], NT)

    ahead = products(0)
    for i in range(LEN // QB):
        low, high = static_window(i)
        rows = slice(i * QB, (i + 1) * QB)
        scores = ahead
        if (i + 1) * QB < LEN:
            ahead = products(i + 1)
        same = segc_ref[rows, 0:1] == seg_ref[0:1, low:high].astype(F32)
        parts, logs = [], []
        for h in range(HEADS_HERE):
            mine = jnp.where(same, scores[h * QB : (h + 1) * QB], NEGATIVE)
            top = jnp.max(mine, axis=-1, keepdims=True)
            weights = jnp.exp(mine - top)
            total = jnp.sum(weights, axis=-1, keepdims=True)
            parts.append((weights * (1.0 / total)).astype(BF16))
            logs.append(top + jnp.log(total))
        lse_ref[rows, :] = jnp.where(column == 0, logs[0], jnp.where(column == 1, logs[1], logs[2]))
        mixed = dot(jnp.concatenate(parts, axis=0), v_ref[low:high, :])
        context = merge_heads(mixed, head)[:, :COLS].astype(BF16)
        block, r = i * QB // BLOCK, i * QB % BLOCK
        ctx_ref[block, r : r + QB, :COLS] = context
        ctx_ref[block ^ 1, r : r + QB, COLS:] = context
    for k, out in enumerate((c0_ref, c1_ref, c2_ref, c3_ref)):
        out[...] = ctx_ref[z ^ k]


def place_slots(s_ref, refs, out_ref):
    rows, cols = refs[0].shape[1:]
    for group, ref in enumerate(refs):
        for i in range(2):
            slot = s_ref[1] ^ ORDER[4 * (group // 2) + 2 * i + group % 2]
            there = pl.ds(pl.multiple_of((slot // 2) * rows, 16), rows)
            out_ref[there, pl.ds(pl.multiple_of((slot % 2) * cols, 128), cols)] = ref[i]


def gated(normed, act_back, w_in, w_down, act_ref, gb_ref, width):
    both = dot(normed, w_in, NT)
    gate, linear = both[:, :width], both[:, width:]
    cdf = 0.5 * (1.0 + lax.erf(gate * math.sqrt(0.5)))
    slope = cdf + gate * (jnp.exp(-0.5 * gate * gate) * (1.0 / math.sqrt(2.0 * math.pi)))
    gelu = gate * cdf
    act_ref[...] = (gelu * linear).astype(BF16)
    gb_ref[:, :width] = (act_back * linear * slope).astype(BF16)
    gb_ref[:, width:] = (act_back * gelu).astype(BF16)
    return dot(act_ref[...], w_down), dot(gb_ref[...], w_in)


def begin_kernel(
    s_ref, tok_ref, cot_ref, c0, c1, c2, c3, w_ref, dw_ref, res_ref, context_ref, cot_out, back_ref
):
    z = s_ref[0]
    for half in range(2):
        base = (z if half == 0 else z ^ 1) * BLOCK
        there = pl.ds(pl.multiple_of(base, BLOCK), BLOCK)
        rows = slice(half * BLOCK, (half + 1) * BLOCK)
        mine = slice(half * COLS, (half + 1) * COLS)
        res_ref[rows, :] = tok_ref[there, :].astype(F32) + dot(c0[:, mine], w_ref[...])
        for k, c in enumerate((c1, c2, c3)):
            context_ref[k, rows, :] = c[:, mine]
        cot_out[rows, :] = cot_ref[there, :]
    back_ref[...] = dot(cot_out[...], dw_ref[...], NT)


def middle_kernel(
    s_ref, part_ref, context_ref, cot_ref, act_back_ref, w_ref, here_ref, there_ref, gain_ref, gw_ref, dw_ref,
    res_ref, normed_ref, act_ref, gb_ref, branch_ref, back_ref, wo_ref,
):
    wo_ref[0] = w_ref[...]
    few = COLS // 4
    pieces = ((0, here_ref, 0), (2, here_ref, 1), (1, there_ref, 0), (3, there_ref, 1))
    for slot, ref, i in pieces:
        there = pl.ds(pl.multiple_of((s_ref[1] % 4 ^ slot) * few, 16), few)
        for k in range(3):
            for side in range(2):
                first = (2 * k + side) * few
                lanes = slice(side * (D // 2), (side + 1) * (D // 2))
                wo_ref[k + 1, there, lanes] = ref[i, first : first + few, :]
    residual = part_ref[...]
    for k in range(3):
        residual += dot(context_ref[k], wo_ref[k + 1])
    res_ref[...] = residual[:BLOCK]
    unit, _ = normalize(residual)
    normed_ref[...] = (unit * gain_ref[...]).astype(BF16)
    branch_ref[...], back_ref[...] = gated(
        normed_ref[BLOCK:, :], act_back_ref[BLOCK:, :], gw_ref[...], dw_ref[...], act_ref, gb_ref, dw_ref.shape[0]
    )


def partner_kernel(
    s_ref, normed_ref, cot_ref, branch_in, back_in, f0, f1, f2, f3,
    act_ref, gb_ref, branch_ref, back_ref, other_ref,
):
    width = act_ref.shape[1]
    place_slots(s_ref, (f0, f1, f2, f3), other_ref)
    branch, back = gated(
        normed_ref[BLOCK:, :], dot(cot_ref[BLOCK:, :], other_ref[2 * width : 3 * width, :], NT), other_ref[: 2 * width, :],
        other_ref[2 * width : 3 * width, :], act_ref, gb_ref, width,
    )
    branch_ref[...] = (branch_in[...] + branch).astype(BF16)
    back_ref[...] = (back_in[...] + back).astype(BF16)


def own_kernel(
    s_ref, normed_ref, cot_ref, act_back_ref, res_ref, gw_ref, dw_ref, other_ref,
    act_par, gb_par, act_par_two, gb_par_two,
    branch_ref, back_ref, whole_ref,
    act_one, gb_one, act_two, gb_two,
):
    width = act_par.shape[1]
    normed, cot = normed_ref[:BLOCK, :], cot_ref[:BLOCK, :]
    w_down = other_ref[2 * width : 3 * width, :]
    branch, back = gated(normed, act_back_ref[:BLOCK, :], gw_ref[...], dw_ref[...], act_one, gb_one, width)
    more, back_more = gated(normed, dot(cot, w_down, NT), other_ref[: 2 * width, :], w_down, act_two, gb_two, width)
    branch_ref[...] = res_ref[...] + branch + more
    back_ref[...] = back + back_more
    half = whole_ref.shape[1] // 2
    shards = ((act_one, gb_one, act_par, gb_par), (act_two, gb_two, act_par_two, gb_par_two))
    for shard, (act, gb, act_there, gb_there) in enumerate(shards):
        at = shard * half
        part = dot(normed, gb[...], TN) + dot(normed_ref[BLOCK:, :], gb_there[...], TN)
        whole_ref[:, at : at + 2 * width] = part.astype(BF16)
        part = dot(cot, act[...], TN) + dot(cot_ref[BLOCK:, :], act_there[...], TN)
        whole_ref[:, at + 2 * width : at + 3 * width] = part.astype(BF16)
        whole_ref[:, at + 3 * width : at + half] = jnp.zeros((D, half - 3 * width), BF16)


def finish_kernel(keep_ref, r1, r2, r3, geglu_ref, down_ref, out_ref, pad_ref):
    half = r2.shape[1] - COLS
    rows, width = geglu_ref.shape[1:]
    ff = keep_ref[:, :half] + r2[:, :half].astype(F32)
    geglu_ref[0] = ff[:, :width]
    geglu_ref[1] = ff[:, width : 2 * width]
    out = keep_ref[:, half:] + r1[...].astype(F32) + r2[:, half:].astype(F32) + r3[...].astype(F32)
    pad_ref[...] = jnp.zeros_like(pad_ref)
    pad_ref[:rows, :width] = ff[:, 2 * width : 3 * width]
    down_ref[...] = jnp.transpose(pad_ref[...])[:width, :rows]
    pad_ref[:rows, :COLS] = out
    out_ref[...] = jnp.transpose(pad_ref[...])[:COLS, :rows]


def qkv_sum_kernel(parts_ref, grad_ref, gains_ref):
    rows = grad_ref.shape[1]
    total = jnp.sum(parts_ref[...].astype(F32), axis=0)
    for s in range(3):
        grad_ref[s] = total[:rows, s * COLS : (s + 1) * COLS]
    for gain in range(2):
        for side in range(2):
            first = rows + 6 * gain + side
            part = total[first : first + 1] + total[first + 2 : first + 3] + total[first + 4 : first + 5]
            gains_ref[gain : gain + 1, side * (D // 2) : (side + 1) * (D // 2)] = part[:, : D // 2]


def residual_kernel(
    keep_ref, recv_ref, res_ref, gain_ref, cot_ref, wo_ref,
    back_ref, low_ref, gain_out, b0, b1, b2, b3,
):
    unit, inverse = normalize(res_ref[...])
    upstream = keep_ref[...] + recv_ref[...].astype(F32)
    back = cot_ref[:BLOCK, :].astype(F32) + norm_back(upstream, unit, inverse, gain_ref[...])
    back_ref[...] = back
    gain_out[...] = jnp.sum(upstream * unit, axis=0, keepdims=True)
    low = back.astype(BF16)
    low_ref[...] = low
    for k, out in enumerate((b0, b1, b2, b3)):
        part = dot(low, wo_ref[k], NT).astype(BF16)
        out[:, :COLS] = part[: BLOCK // 2]
        out[:, COLS:] = part[BLOCK // 2 :]


def output_grad_kernel(s_ref, low_ref, c0, c1, c2, c3, ff_ref, even_ref, odd_ref, whole_ref):
    for k, c in enumerate((c0, c1, c2, c3)):
        whole_ref[:, k * COLS : (k + 1) * COLS] = dot(low_ref[...], c[:, :COLS], TN).astype(BF16)
    rows, ff = even_ref.shape[1], ff_ref.shape[1]
    for i in range(8):
        there = pl.ds(pl.multiple_of((s_ref[1] ^ ORDER[i]) * rows, 16), rows)
        out = even_ref.at[i] if i < 4 else odd_ref.at[i - 4]
        out[:, :ff] = ff_ref[there, :]
        out[:, ff:] = whole_ref[there, :]


def collect_kernel(own_ref, r1, r2, r3, keep_ref, s1, s2, s3):
    total = own_ref[...] + r1[...].astype(F32) + r2[...].astype(F32) + r3[...].astype(F32)
    half = keep_ref.shape[1] - COLS
    keep_ref[:, :half] = total[:, :half]
    keep_ref[:, half:] = total[:, 2 * half : 2 * half + COLS]
    s2[:, :half] = total[:, half : 2 * half].astype(BF16)
    for k, out in ((1, s1), (2, s2), (3, s3)):
        first = 2 * half + k * COLS
        out[:, out.shape[1] - COLS :] = total[:, first : first + COLS].astype(BF16)


def pack_kernel(s_ref, w_in_ref, w_down_ref, w_out_ref, out_ref, ff_ref, sems, out_sems):
    slot = s_ref[1]
    cols = pl.ds(pl.multiple_of((slot % 2) * (D // 2), 128), D // 2)
    few = out_ref.shape[0] // 2
    here = pl.ds(pl.multiple_of(slot % 4 * few, 16), few)
    copies = [
        pltpu.make_async_copy(
            w_out_ref.at[here, side * (D // 2) : (side + 1) * (D // 2)],
            out_ref.at[side * few : (side + 1) * few, :],
            out_sems.at[side],
        )
        for side in range(2)
    ]
    for copy in copies:
        copy.start()
    n_in, n_down, rows = w_in_ref.shape[0], w_down_ref.shape[0], ff_ref.shape[0]
    for quarter in range(4):
        first = quarter * rows
        last = min(first + rows, n_in + n_down)

        @pl.when(slot // 2 == quarter)
        def _():
            mine = []
            for ref, base, count in ((w_in_ref, 0, n_in), (w_down_ref, n_in, n_down)):
                low, high = max(first, base), min(last, base + count)
                if low < high:
                    there = ff_ref.at[low - first : high - first, :]
                    here = ref.at[low - base : high - base, cols]
                    mine.append(pltpu.make_async_copy(here, there, sems.at[len(mine)]))
            for copy in mine:
                copy.start()
            if last < first + rows:
                ff_ref[last - first :, :] = jnp.zeros((first + rows - last, D // 2), BF16)
            for copy in mine:
                copy.wait()

    for copy in copies:
        copy.wait()


def arrived_kernel(s_ref, f1, f2, f3, out_ref):
    few = f1.shape[0]
    for i, piece in enumerate((f1, f2, f3)):
        out_ref[i * few : (i + 1) * few, :] = piece[...]


def pair_kernel(s_ref, a0, a1, out_ref):
    out_ref[0] = a0[...]
    out_ref[1] = a1[...]


def backward_steps(
    mirror, steps, seg_ref, segc_ref, q_ref, k_ref, v_ref, lse_ref, back_ref, dq_ref, dk_ref, dv_ref
):
    last = LEN // QB - 1
    head = lane_head(QB)
    scale = jnp.asarray(1.0 / math.sqrt(HEAD), BF16)

    def products(step):
        low, high = static_window(step)
        i = jnp.where(mirror == 1, last - step, step)
        rows = pl.ds(pl.multiple_of(i * QB, QB), QB)
        keys = jnp.where(mirror == 1, LEN - high, low)
        keys = pl.ds(pl.multiple_of(keys, QB), high - low)
        stacked = by_head(q_ref[rows, :] * scale, head)
        upstream = by_head(back_ref[rows, :], head)
        scores = dot(stacked, k_ref[keys, :], NT)
        prob_back = dot(upstream, v_ref[keys, :], NT)
        return rows, keys, stacked, upstream, scores, prob_back

    ahead = products(steps[0])
    for step in steps:
        rows, keys, stacked, upstream, scores, prob_back = ahead
        if step + 1 in steps:
            ahead = products(step + 1)
        same = segc_ref[rows, 0:1] == seg_ref[0:1, keys].astype(F32)
        probs, grads = [], []
        for h in range(HEADS_HERE):
            at = slice(h * QB, (h + 1) * QB)
            prob = jnp.exp(jnp.where(same, scores[at], NEGATIVE) - lse_ref[rows, h : h + 1])
            inner = jnp.sum(prob * prob_back[at], axis=-1, keepdims=True)
            probs.append(prob.astype(BF16))
            grads.append((prob * (prob_back[at] - inner)).astype(BF16))
        prob = jnp.concatenate(probs, axis=0)
        grad = jnp.concatenate(grads, axis=0)
        dv_ref[:, keys] += dot(upstream, prob, TN)
        dk_ref[:, keys] += dot(stacked, grad, TN)
        dq_ref[rows, :] = merge_heads(dot(grad, k_ref[keys, :]), head) * (1.0 / math.sqrt(HEAD))


def rows_back(base, dq_ref, dk_ref, dv_ref, trig_ref, w_ref, qkv_ref):
    rows = pl.ds(pl.multiple_of(base, BLOCK), BLOCK)
    trig = trig_ref[rows, :]
    total = None
    for part, grad_ref in enumerate((dq_ref, dk_ref, dv_ref)):
        g = jnp.transpose(grad_ref[:, rows]) if part else grad_ref[rows, :]
        if part < 2:
            g = turn(g, trig, -1.0)
        low = g[:, :COLS].astype(BF16)
        qkv_ref[:, part * COLS : (part + 1) * COLS] = low
        product = dot(low, w_ref[part])
        total = product if total is None else total + product
    return total


def backward_far_kernel(
    s_ref, seg_ref, segc_ref, q_ref, k_ref, v_ref, lse_ref, trig_ref, b0, b1, b2, b3, w_ref,
    n2, n3, qkv_ref, back_ref, dq_ref, dk_ref, dv_ref,
):
    z = s_ref[0]
    pair = z // 2
    half = BLOCK // 2
    back_ref[:, COLS:] = jnp.zeros((LEN, LANES - COLS), BF16)
    for k, b in enumerate((b0, b1, b2, b3)):
        base = pl.multiple_of((z ^ k) * BLOCK, BLOCK)
        back_ref[pl.ds(base, half), :COLS] = b[:, :COLS]
        back_ref[pl.ds(pl.multiple_of(base + half, half), half), :COLS] = b[:, COLS:]
    dk_ref[...] = jnp.zeros_like(dk_ref)
    dv_ref[...] = jnp.zeros_like(dv_ref)
    refs = (seg_ref, segc_ref, q_ref, k_ref, v_ref, lse_ref, back_ref, dq_ref, dk_ref, dv_ref)
    steps = LEN // QB
    reach = DOC // QB
    backward_steps(1 - pair, range(steps // 2 + reach), *refs)
    for k, out in ((2, n2), (3, n3)):
        at = qkv_ref.at[(k - 2) * BLOCK : (k - 1) * BLOCK]
        part = rows_back((z ^ k) * BLOCK, dq_ref, dk_ref, dv_ref, trig_ref, w_ref, at)
        out[...] = part.astype(out.dtype)


def add_kernel(mine_ref, recv_ref, out_ref):
    out_ref[...] = (mine_ref[...] + recv_ref[...].astype(F32)).astype(out_ref.dtype)


def backward_near_kernel(
    s_ref, seg_ref, segc_ref, q_ref, k_ref, v_ref, lse_ref, trig_ref, back_ref, dq_in, dk_in, dv_in,
    w_ref, n0, n1, qkv_ref, dq_ref, dk_ref, dv_ref,
):
    z = s_ref[0]
    pair = z // 2
    dq_ref[...] = dq_in[...]
    dk_ref[...] = dk_in[...]
    dv_ref[...] = dv_in[...]
    refs = (seg_ref, segc_ref, q_ref, k_ref, v_ref, lse_ref, back_ref, dq_ref, dk_ref, dv_ref)
    steps = LEN // QB
    reach = DOC // QB
    backward_steps(pair, range(steps // 2 - reach), *refs)
    for k, out in ((0, n0), (1, n1)):
        at = qkv_ref.at[k * BLOCK : (k + 1) * BLOCK]
        part = rows_back((z ^ k) * BLOCK, dq_ref, dk_ref, dv_ref, trig_ref, w_ref, at)
        out[...] = part.astype(out.dtype)


def qkv_grad_kernel(
    s_ref, normed_ref, near_ref, far_ref, w_ref, gain_ref, gain_two_ref, out_ref, whole_ref, rows_ref
):
    for k in range(NARROW):
        base = pl.multiple_of((s_ref[0] ^ k) * BLOCK, BLOCK)
        rows_ref[k * BLOCK : (k + 1) * BLOCK, :] = normed_ref[pl.ds(base, BLOCK), :]
    pair = 2 * BLOCK
    total = None
    for s in range(3):
        cols = slice(s * COLS, (s + 1) * COLS)
        part = dot(rows_ref[:pair, :], near_ref[:, cols], TN)
        part += dot(rows_ref[pair:, :], far_ref[:, cols], TN)
        whole_ref[:, cols] = part.astype(BF16)
        weighted = part * jnp.transpose(w_ref[s].astype(F32))
        total = weighted if total is None else total + weighted
    column = jnp.broadcast_to(jnp.sum(total, axis=1, keepdims=True), (D, 128))
    gains = (jnp.transpose(column)[:1, :] / gain_ref[...], gain_two_ref[...])
    extra = jnp.zeros((GAIN_ROWS, D // 2), F32)
    row = lax.broadcasted_iota(jnp.int32, extra.shape, 0)
    at = 0
    for gain in gains:
        rest = gain
        for _ in range(3):
            term = rest.astype(BF16).astype(F32)
            rest = rest - term
            for side in range(2):
                extra = jnp.where(row == at, term[:, side * (D // 2) : (side + 1) * (D // 2)], extra)
                at += 1
    blocks, rows, cols = out_ref.shape
    rows -= GAIN_ROWS
    for i in range(blocks):
        if rows % 16 == 0:
            out_ref[i, :rows, :] = whole_ref[i * rows : (i + 1) * rows, :]
            out_ref[i, rows:, :] = jnp.zeros((GAIN_ROWS, cols), BF16)
            out_ref[i, rows:, : D // 2] = extra.astype(BF16)
        else:
            lines = [whole_ref[i * rows : (i + 1) * rows, :].astype(F32)]
            pad = jnp.zeros((GAIN_ROWS, cols - D // 2), F32)
            lines.append(jnp.concatenate([extra, pad], axis=1))
            out_ref[i] = jnp.concatenate(lines, axis=0).astype(BF16)


def final_kernel(
    s_ref, tok_ref, gain_ref, back_ref, n0, n1, n2, own_ref, branch_ref, out_ref, layer_ref
):
    upstream = n0[...] + n1[...].astype(F32) + n2[...].astype(F32)
    rows = pl.ds(pl.multiple_of(s_ref[0] * BLOCK, BLOCK), BLOCK)
    unit, inverse = normalize(tok_ref[rows, :].astype(F32))
    out_ref[...] = back_ref[...] + norm_back(upstream, unit, inverse, gain_ref[...])
    layer_ref[...] = (own_ref[...] + branch_ref[...].astype(F32)).astype(BF16)


def fold_kernel(even_ref, recv_ref, own_ref, s1_ref, s2_ref, s3_ref):
    for i, out in enumerate((own_ref, s1_ref, s2_ref, s3_ref)):
        out[...] = (even_ref[i].astype(F32) + recv_ref[i].astype(F32)).astype(out.dtype)


def along_narrow(x, k):
    return lax.ppermute(x, "narrow", [(i, i ^ k) for i in range(NARROW)])


def along_wide(x, k):
    return lax.ppermute(x, "wide", [(i, i ^ k) for i in range(lax.axis_size("wide"))])


def in_hbm(x):
    return pltpu.with_memory_space_constraint(x, pltpu.HBM)


def tie(x, *others):
    return lax.optimization_barrier((x, *others))[0]


def quarter_slice(x, slot):
    rows, cols = x.shape[-2] // 4, x.shape[-1] // 2
    x = lax.dynamic_slice_in_dim(x, (slot // 2) * rows, rows, x.ndim - 2)
    return lax.dynamic_slice_in_dim(x, (slot % 2) * cols, cols, x.ndim - 1)


def all_slots(x, hops):
    whole = jnp.stack([along_narrow(x, k) for k in hops])
    slots = jnp.stack([quarter_slice(whole, i) for i in ORDER])
    return slots[:4], slots[4:]


def sum_wide(x):
    return jnp.sum(lax.all_to_all(x, "wide", 0, 0).astype(F32), axis=0)


def per_device(
    tokens, segments, first_gain, qkv_weight, output_weight, second_gain, geglu_weight, down_weight,
    cotangent,
):
    size = lax.axis_size("wide")
    plane = size == 8
    mine = lax.axis_index("wide").astype(jnp.int32)
    z = lax.axis_index("narrow").astype(jnp.int32)
    scalars = jnp.stack([z, mine if plane else jnp.zeros_like(mine)])
    hidden = geglu_weight.shape[2]
    padded = -(-3 * hidden // 64) * 64
    rows_d = D // size
    gain_one = first_gain.reshape(1, D)
    gain_two = second_gain.reshape(1, D)
    w_qkv = qkv_weight.transpose(0, 2, 1)
    w_in = geglu_weight.transpose(0, 2, 1).reshape(2 * hidden, D)

    few, many = COLS // 4, padded // 4
    now = scalars
    if plane:
        slot_out, slot_ff = call(
            pack_kernel,
            (scalars, in_hbm(w_in), in_hbm(down_weight), in_hbm(output_weight)),
            (sds((2 * few, D // 2), BF16), sds((many, D // 2), BF16)),
            [pltpu.SemaphoreType.DMA((2,)), pltpu.SemaphoreType.DMA((2,))],
            place=pltpu.HBM,
        )
        out_fetched = [along_narrow(slot_out, k) for k in (1, 2, 3)]
        ff_fetched = along_narrow(slot_ff, 2)
    wide_rows = sds((LEN, LANES), BF16)
    q, k, v, normed_one, trig, segc = call(
        project_kernel,
        (tokens, segments, gain_one, w_qkv, jnp.asarray(rotary_table())),
        (wide_rows, wide_rows, wide_rows, sds((LEN, D), BF16), sds((LEN, 2 * 128), F32),
         sds((LEN, 128), F32)),
        [pltpu.VMEM((LEN // 4, LANES), F32)],
        scalars=0,
    )
    piece = sds((BLOCK, 2 * COLS), BF16)
    c0, c1, c2, c3, lse = call(
        attend_kernel,
        (now, segments, segc, q, k, v),
        (piece, piece, piece, piece, sds((LEN, 128), F32)),
        [pltpu.VMEM((NARROW, BLOCK, 2 * COLS), BF16)],
    )
    context = (c0, *(along_narrow(c, k) for k, c in ((1, c1), (2, c2), (3, c3))))
    if plane:
        ff0 = tie(ff_fetched, lse)
        slots_two = sds((2, many, D // 2), BF16)
        (out0,) = call(
            arrived_kernel, (tie(scalars, lse), *out_fetched), (sds((6 * few, D // 2), BF16),)
        )
        (out_here,) = call(
            pair_kernel, (scalars, out0, along_wide(out0, 2)), (sds((2, 6 * few, D // 2), BF16),)
        )
        out_there = along_wide(out_here, 1)
        (ff_pair,) = call(pair_kernel, (scalars, ff0, along_wide(ff0, 4)), (slots_two,))
        ff_x = along_wide(ff_pair, 2)
        ff_slots = (ff_pair, ff_x, along_wide(ff_pair, 1), along_wide(ff_x, 1))
    else:
        everything = jnp.concatenate(
            [w_in, down_weight, jnp.zeros((padded - 3 * hidden, D), BF16)], axis=0
        )
        even, odd = (x[:, 0] for x in all_slots(everything, (2,)))
        ff_slots = (even[::2], even[1::2], odd[::2], odd[1::2])
        others = jnp.stack([along_narrow(output_weight, k) for k in (1, 2, 3)])
        others = others.reshape(3, 4, few, 2, D // 2).transpose(1, 0, 3, 2, 4)
        others = others.reshape(4, 6 * few, D // 2)
        out_here, out_there = others[::2], others[1::2]

    whole = sds((2 * BLOCK, D), F32)
    own = sds((BLOCK, D), F32)
    own_low = sds((BLOCK, D), BF16)
    part, contexts, cot, act_back = call(
        begin_kernel,
        (scalars, tokens, cotangent, *context, output_weight, down_weight),
        (whole, sds((3, 2 * BLOCK, COLS), BF16), sds((2 * BLOCK, D), BF16),
         sds((2 * BLOCK, hidden), F32)),
    )
    part_act, part_gb = sds((BLOCK, hidden), BF16), sds((BLOCK, 2 * hidden), BF16)
    res, normed_two, act_par, gb_par, branch, back, wo = call(
        middle_kernel,
        (scalars, part, contexts, cot, act_back, output_weight, out_here, out_there, gain_two, w_in,
         down_weight),
        (own, sds((2 * BLOCK, D), BF16), part_act, part_gb, own, own, sds((NARROW, COLS, D), BF16)),
    )
    act_par_two, gb_par_two, out_send, send, other = call(
        partner_kernel,
        (scalars, normed_two, cot, branch, back, *ff_slots),
        (part_act, part_gb, own_low, own_low, sds((padded, D), BF16)),
    )
    recv = along_narrow(send, 1)
    half = -(-3 * hidden // 128) * 128
    out_keep, keep, ff_part = call(
        own_kernel,
        (scalars, normed_two, cot, act_back, res, w_in, down_weight, other, act_par, gb_par,
         act_par_two, gb_par_two),
        (own, own, sds((D, 2 * half), BF16)),
        [pltpu.VMEM((BLOCK, hidden), BF16), pltpu.VMEM((BLOCK, 2 * hidden), BF16)] * 2,
    )
    low_piece = sds((BLOCK // 2, 2 * COLS), BF16)
    back, low, gain_two_part, b0, b1, b2, b3 = call(
        residual_kernel,
        (keep, recv, res, gain_two, cot, wo),
        (own, own_low, sds((1, D), F32), low_piece, low_piece, low_piece, low_piece),
        scalars=0,
    )
    upstream = (b0, *(along_narrow(b, k) for k, b in ((1, b1), (2, b2), (3, b3))))
    grad_cols = 2 * half + NARROW * COLS
    even_part, odd_part = call(
        output_grad_kernel,
        (scalars, low, *context, ff_part),
        (sds((4, D // 8, grad_cols), BF16),) * 2,
        [pltpu.VMEM((D, NARROW * COLS), BF16)],
    )
    block = sds((rows_d, grad_cols), F32)
    if plane:
        block_low = sds((rows_d, grad_cols), BF16)
        grad_sum, *grad_sends = call(
            fold_kernel,
            (even_part, along_wide(odd_part, 1)),
            (block, block_low, block_low, block_low),
            scalars=0,
            far=(0,),
        )
        grad_recv = [along_wide(x, 2 * (i + 1)) for i, x in enumerate(grad_sends)]
        now = tie(scalars, *grad_sends)
    else:
        blocks = jnp.stack([even_part, odd_part], axis=1)
        grad_sum = sum_wide(blocks.reshape(size, rows_d, grad_cols))
        grad_recv, grad_sends = [jnp.zeros((rows_d, grad_cols), BF16)] * 3, ()
        now = tie(scalars, even_part)

    rows_f32 = sds((LEN, LANES), F32)
    columns_f32 = sds((LANES, LEN), F32)
    pair_qkv = sds((2 * BLOCK, 3 * COLS), BF16)
    n2, n3, qkv_far, back_rows, *grads = call(
        backward_far_kernel,
        (now, segments, segc, q, k, v, lse, trig, *upstream, w_qkv),
        (own, own_low, pair_qkv, wide_rows, rows_f32, columns_f32, columns_f32),
    )
    exchanged = along_narrow(n3, 1)
    branch_recv = along_narrow(tie(out_send, upstream[1], *grad_sends), 1)
    n0, n1, qkv_near = call(
        backward_near_kernel,
        (scalars, segments, segc, q, k, v, lse, trig, back_rows, *grads, w_qkv),
        (own, own_low, pair_qkv),
        [pltpu.VMEM((LEN, LANES), F32)] + [pltpu.VMEM((LANES, LEN), F32)] * 2,
    )
    (qkv_part,) = call(
        qkv_grad_kernel,
        (tie(scalars, n1, branch_recv), normed_one, qkv_near, qkv_far, w_qkv, gain_one, gain_two_part),
        (sds((size, rows_d + GAIN_ROWS, 3 * COLS), BF16),),
        [pltpu.VMEM((D, 3 * COLS), BF16), pltpu.VMEM((LEN, D), BF16)],
    )
    near_recv = along_narrow(n1, 1)
    (pair_sum,) = call(add_kernel, (tie(n2, qkv_part), exchanged), (own_low,), scalars=0)
    far_recv = along_narrow(pair_sum, 2)
    qkv_grad, gains = call(
        qkv_sum_kernel,
        (lax.all_to_all(qkv_part, "wide", 0, 0),),
        (sds((3, rows_d, COLS), F32), sds((2, D), F32)),
        scalars=0,
    )
    few_cols = sds((rows_d, COLS), BF16)
    grad_keep, *there = call(
        collect_kernel,
        (in_hbm(tie(grad_sum, near_recv, pair_sum)), *grad_recv),
        (sds((rows_d, half + COLS), F32), few_cols, sds((rows_d, half + COLS), BF16), few_cols),
        scalars=0,
    )
    there = [along_narrow(x, k) for k, x in zip((1, 2, 3), there)]
    tokens_grad, layer_out = call(
        final_kernel,
        (scalars, tokens, gain_one, back, n0, near_recv, far_recv, out_keep, branch_recv),
        (own, own_low),
    )
    gains = gains + along_narrow(gains, 1) + along_narrow(gains, 2) + along_narrow(gains, 3)
    geglu_grad, down_grad, out_grad = call(
        finish_kernel,
        (tie(grad_keep, tokens_grad), *there),
        (sds((2, rows_d, hidden), F32), sds((hidden, rows_d), F32), sds((COLS, rows_d), F32)),
        [pltpu.VMEM((128, -(-hidden // 128) * 128), F32)],
        scalars=0,
    )
    return (
        layer_out, tokens_grad, gains[0], qkv_grad, out_grad, gains[1], geglu_grad, down_grad,
    )


def solution(mesh):
    return jax.shard_map(
        per_device,
        mesh=mesh,
        in_specs=(
            P("wide", None),
            P("wide", None),
            P(),
            P(None, None, "narrow"),
            P("narrow", None),
            P(),
            P(None, None, "narrow"),
            P("narrow", None),
            P("wide", None),
        ),
        out_specs=(
            P(("wide", "narrow"), None),
            P(("wide", "narrow"), None),
            P(),
            P(None, "wide", "narrow"),
            P("narrow", "wide"),
            P(),
            P(None, "wide", "narrow"),
            P("narrow", "wide"),
        ),
        check_vma=False,
    )
```
